32 devices in a mesh: dp: 8 (over z, core), tensor: 4 (over y, x).
Axes of the slice: x: 2, y: 2, z: 4, core: 2. Of those that a mesh axis runs over, the one named last changes fastest.
Arguments:
- hidden_in: bfloat16 [1920, 4, 5120], P('dp', None, 'tensor'), may hold values from -6 to 6
- kv_weight: bfloat16 [2, 5120, 1024], P(None, 'tensor'), may hold values from -0.078125 to 0.078125
- factor_a: float32 [2, 64, 5120], P(None, None, 'tensor'), may hold values from -0.078125 to 0.078125
- factor_b: float32 [2, 64, 1024], P(None, None, 'tensor'), may hold values from -0.75 to 0.75
- grad_a: float32 [8, 2, 64, 5120], P('dp', None, None, 'tensor'), may hold values from -6 to 6
- grad_b: float32 [8, 2, 64, 1024], P('dp', None, None, 'tensor'), may hold values from -6 to 6
- key_gain: float32 [128], replicated, may hold values from 0.1 to 1.9
- queries: bfloat16 [1920, 4, 4096], P(('dp', 'tensor')), may hold values from -27 to 27
- cache_keys: bfloat16 [1920, 16, 1024], P(('dp', 'tensor')), may hold values from -6 to 6
- cache_values: bfloat16 [1920, 16, 1024], P(('dp', 'tensor')), may hold values from -6 to 6
- cache_lengths: int32 [1920], P(('dp', 'tensor')), may hold values from 2 to 12, as said below
- positions: int32 [1920], P(('dp', 'tensor')), may hold values from 0 to 32767
Outputs:
- attended: bfloat16 [1920, 4, 4096], P(('dp', 'tensor'))
- new_a: float32 [2, 64, 5120], P(None, None, 'tensor')
- new_b: float32 [2, 64, 1024], P(None, None, 'tensor')
The draws below stay inside these ranges and needn't reach their ends.
Inputs may be any that keep to these rules, and one draw needn't show every extreme that they name: `cache_lengths`: some row holds 12 filled slots.
All inputs are finite; a program needn't handle non-finite values.
Results may differ from the reference program's by a relative error of at most 0.035.
Values may be sent and summed in bfloat16 or wider, within the bound.
No kernel may reach another device: no remote copies, remote signals or barrier semaphores. Data moves between devices by JAX's collectives and lax.ppermute only.
A program may use at most 64 MiB of HBM per device.

```python
import math
import jax
import jax.numpy as jnp
from jax import lax

D = 5120
KVH = 8
HD = 128
QH = 32
R = 64
STEPS = 4
CACHE = 16
KVW = 1024
ROWS = 1920
N_DP = 8
N_TENSOR = 4


def draw_cache_keys(key, part):
    key = jax.random.fold_in(key, 21)
    keys = jnp.clip(jax.random.normal(key, (ROWS, CACHE, KVH, HD), jnp.float32), -6.0, 6.0)
    return keys.reshape(ROWS, CACHE, KVH * HD).astype(jnp.bfloat16)


def draw_queries(key, part):
    key = jax.random.fold_in(key, 22)
    values = jnp.clip(jax.random.normal(key, (ROWS, STEPS, QH * HD), jnp.float32), -6.0, 6.0)
    return values.astype(jnp.bfloat16)


def draw_cache_lengths(key, part):
    key = jax.random.fold_in(key, 23)
    first, second = jax.random.split(key)
    lengths = jax.random.randint(first, (ROWS,), 2, CACHE - STEPS + 1)
    full_row = jax.random.randint(second, (), 0, ROWS)
    return jnp.where(jnp.arange(ROWS) == full_row, CACHE - STEPS, lengths).astype(jnp.int32)


def with_ends(entries, own_key, least, largest):
    spot = [jax.random.randint(jax.random.fold_in(own_key, axis), (), 0, length) for axis, length in enumerate(entries.shape)]
    widest = entries.shape.index(max(entries.shape))
    next_to = spot[:widest] + [(spot[widest] + 1) % entries.shape[widest]] + spot[widest + 1:]
    return entries.at[tuple(spot)].set(least).at[tuple(next_to)].set(largest)


def steps_of(stream_key, extent, shards, least, top_value):
    factor_of = 1.0
    for dim, parts in shards:
        steps = jax.random.uniform(jax.random.fold_in(jax.random.fold_in(stream_key, 6), dim), (parts,), jnp.float32, least / len(shards), top_value / len(shards))
        factor_of = factor_of * jnp.repeat(jnp.exp(steps), extent[dim] // parts).reshape((-1,) + (1,) * (len(extent) - 1 - dim))
    return factor_of


def bell_draw(key, extent, scale, most, cuts=(), kind=jnp.bfloat16):
    factor_of = steps_of(key, extent, cuts, -0.22, 0.18) if cuts else 1.0
    drawn = jax.random.normal(key, extent, jnp.float32) * scale * factor_of
    return jnp.minimum(jnp.maximum(drawn, -most), most).astype(kind)


def setup_inputs(seed: int = 0) -> dict:
    key_list = jax.random.split(jax.random.key(seed), 13)
    hidden_in = bell_draw(key_list[0], (ROWS, STEPS, D), 1.0, 6.0, ((0, 8), (2, 4)))
    kv_weight = bell_draw(key_list[1], (2, D, KVW), D ** -0.5, 0.078125, ((1, 4),))
    factor_a = bell_draw(key_list[2], (2, R, D), D ** -0.5, 0.078125, ((2, 4),), jnp.float32)
    factor_b = bell_draw(key_list[3], (2, R, KVW), R ** -0.5, 0.75, ((2, 4),), jnp.float32)
    grad_a = bell_draw(key_list[4], (N_DP, 2, R, D), 1.0, 6.0, ((0, 8), (3, 4)), jnp.float32)
    grad_b = bell_draw(key_list[5], (N_DP, 2, R, KVW), 1.0, 6.0, ((0, 8), (3, 4)), jnp.float32)
    key_gain = jnp.clip(1.0 + 0.18 * jax.random.normal(key_list[6], (HD,), jnp.float32), 0.1, 1.9)
    queries = draw_queries(jax.random.fold_in(key_list[12], 71), 0)
    cache_keys = draw_cache_keys(jax.random.fold_in(key_list[12], 71), 0)
    cache_values = bell_draw(key_list[9], (ROWS, CACHE, KVW), 1.0, 6.0, ((0, 32),))
    cache_lengths = draw_cache_lengths(jax.random.fold_in(key_list[12], 71), 0)
    positions = with_ends(jax.random.randint(key_list[11], (ROWS,), 0, 32768), jax.random.fold_in(key_list[11], 1), 0, 32767).astype(jnp.int32)
    return {"hidden_in": hidden_in, "kv_weight": kv_weight, "factor_a": factor_a, "factor_b": factor_b, "grad_a": grad_a, "grad_b": grad_b, "key_gain": key_gain, "queries": queries, "cache_keys": cache_keys, "cache_values": cache_values, "cache_lengths": cache_lengths, "positions": positions}


def normed_rotated(keys, gain, position):
    scale = lax.rsqrt(lax.optimization_barrier(jnp.mean(keys * keys, axis=-1, keepdims=True)) + 1e-06)
    keys = keys * scale * gain
    half = keys.shape[-1] // 2
    freq = jnp.exp(-math.log(1000000.0) * (jnp.arange(half, dtype=jnp.float32) * 2.0 / keys.shape[-1]))
    angle = position.astype(jnp.float32)[..., None] * freq
    cosine = jnp.concatenate([jnp.cos(angle), jnp.cos(angle)], axis=-1)[..., None, :]
    sine = jnp.concatenate([jnp.sin(angle), jnp.sin(angle)], axis=-1)[..., None, :]
    turned = jnp.concatenate([-keys[..., half:], keys[..., :half]], axis=-1)
    return keys * cosine + turned * sine

def attend(queries, cache_keys, cache_values, new_keys, new_values, lengths):
    rows, steps, width = queries.shape
    slots = cache_keys.shape[1]
    slot = jnp.arange(slots, dtype=jnp.int32)
    for step in range(steps):
        hit = (slot[None, :] == lengths[:, None] + step)[:, :, None]
        cache_keys = jnp.where(hit, new_keys[:, step][:, None, :], cache_keys)
        cache_values = jnp.where(hit, new_values[:, step][:, None, :], cache_values)
    groups = QH // KVH
    query_five = queries.reshape(rows, steps, KVH, groups, HD).astype(jnp.float32)
    key_four = cache_keys.reshape(rows, slots, KVH, HD).astype(jnp.float32)
    value_four = cache_values.reshape(rows, slots, KVH, HD).astype(jnp.float32)
    scores = jnp.einsum('rtkgd,rckd->rtkgc', query_five, key_four) * HD ** (-0.5)
    limit = lengths[:, None] + jnp.arange(steps, dtype=jnp.int32)[None, :]
    valid = (slot[None, None, :] <= limit[:, :, None])[:, :, None, None, :]
    scores = jnp.where(valid, scores, jnp.float32(-1e+30))
    top = lax.optimization_barrier(jnp.max(scores, axis=-1, keepdims=True))
    expo = jnp.exp(scores - top)
    weights = (expo / lax.optimization_barrier(jnp.sum(expo, axis=-1, keepdims=True))).astype(jnp.bfloat16)
    result = jnp.einsum('rtkgc,rckd->rtkgd', weights.astype(jnp.float32), value_four)
    return result.reshape(rows, steps, width).astype(jnp.bfloat16)

def reference(hidden_in, kv_weight, factor_a, factor_b, grad_a, grad_b, key_gain, queries, cache_keys, cache_values, cache_lengths, positions):
    new_a = factor_a - 2.0 / math.sqrt(N_DP * D) * lax.optimization_barrier(jnp.sum(grad_a, axis=0))
    new_b = factor_b - 2.0 / math.sqrt(N_DP * R) * lax.optimization_barrier(jnp.sum(grad_b, axis=0))
    delta = jnp.einsum('prd,prk->pdk', new_a, new_b, precision=lax.Precision.HIGHEST)
    merged = (kv_weight.astype(jnp.float32) + 0.25 * delta).astype(jnp.bfloat16)
    joined = jnp.concatenate([merged[0], merged[1]], axis=1)
    block = D // N_TENSOR
    flat = hidden_in.reshape(ROWS * STEPS, D)

    def shard_sum(total, index):
        part_x = lax.dynamic_slice_in_dim(flat, index * block, block, 1)
        part_w = lax.dynamic_slice_in_dim(joined, index * block, block, 0)
        term = jnp.dot(part_x, part_w, preferred_element_type=jnp.float32).astype(jnp.bfloat16)
        return (total + term.astype(jnp.float32), None)
    start_total = jnp.zeros((ROWS * STEPS, 2 * KVW), jnp.float32)
    projected, _ = lax.scan(shard_sum, start_total, jnp.arange(N_TENSOR, dtype=jnp.int32))
    projected = projected.reshape(ROWS, STEPS, 2 * KVW)
    place = positions[:, None] + jnp.arange(STEPS, dtype=jnp.int32)[None, :]
    keys = normed_rotated(projected[..., :KVW].reshape(ROWS, STEPS, KVH, HD), key_gain, place)
    new_keys = keys.reshape(ROWS, STEPS, KVW).astype(jnp.bfloat16)
    new_values = projected[..., KVW:].astype(jnp.bfloat16)
    attended = attend(queries, cache_keys, cache_values, new_keys, new_values, cache_lengths)
    return (attended, new_a, new_b)
```

```python
import functools
import math

import jax
import jax.numpy as jnp
from jax import lax
from jax.experimental import pallas as pl
from jax.experimental.pallas import tpu as pltpu
from jax.sharding import PartitionSpec as P

D = 5120
KVH = 8
HD = 128
QH = 32
R = 64
STEPS = 4
BF = jnp.bfloat16
F32 = jnp.float32
VMEM_LIMIT = 24 * 1024 * 1024


def normed_rotated(keys, gain, position):
    scale = lax.rsqrt(jnp.mean(keys * keys, axis=-1, keepdims=True) + 1e-06)
    keys = keys * scale * gain
    half = keys.shape[-1] // 2
    freq = jnp.exp(
        -math.log(1000000.0) * (jnp.arange(half, dtype=jnp.float32) * 2.0 / keys.shape[-1])
    )
    angle = position.astype(jnp.float32)[..., None] * freq
    cosine = jnp.concatenate([jnp.cos(angle), jnp.cos(angle)], axis=-1)[..., None, :]
    sine = jnp.concatenate([jnp.sin(angle), jnp.sin(angle)], axis=-1)[..., None, :]
    turned = jnp.concatenate([-keys[..., half:], keys[..., :half]], axis=-1)
    return keys * cosine + turned * sine


def attend(queries, cache_keys, cache_values, new_keys, new_values, lengths):
    rows, steps, width = queries.shape
    slots = cache_keys.shape[1]
    slot = jnp.arange(slots, dtype=jnp.int32)
    for step in range(steps):
        hit = (slot[None, :] == lengths[:, None] + step)[:, :, None]
        cache_keys = jnp.where(hit, new_keys[:, step][:, None, :], cache_keys)
        cache_values = jnp.where(hit, new_values[:, step][:, None, :], cache_values)
    groups = QH // KVH
    query_five = queries.reshape(rows, steps, KVH, groups, HD)
    key_four = cache_keys.reshape(rows, slots, KVH, HD)
    value_four = cache_values.reshape(rows, slots, KVH, HD)
    scores = jnp.einsum(
        "rtkgd,rckd->rtkgc", query_five, key_four, preferred_element_type=jnp.float32
    ) * HD ** (-0.5)
    limit = lengths[:, None] + jnp.arange(steps, dtype=jnp.int32)[None, :]
    valid = (slot[None, None, :] <= limit[:, :, None])[:, :, None, None, :]
    scores = jnp.where(valid, scores, jnp.float32(-1e30))
    top = jnp.max(scores, axis=-1, keepdims=True)
    expo = jnp.exp(scores - top)
    weights = (expo / jnp.sum(expo, axis=-1, keepdims=True)).astype(jnp.bfloat16)
    result = jnp.einsum(
        "rtkgc,rckd->rtkgd", weights, value_four, preferred_element_type=jnp.float32
    )
    return result.reshape(rows, steps, width).astype(jnp.bfloat16)


def general(
    hidden_in,
    kv_weight,
    factor_a,
    factor_b,
    grad_a,
    grad_b,
    key_gain,
    queries,
    cache_keys,
    cache_values,
    cache_lengths,
    positions,
):
    groups_dp = lax.axis_size("dp")
    rate_a = 2.0 / math.sqrt(groups_dp * D)
    rate_b = 2.0 / math.sqrt(groups_dp * R)
    sum_a, sum_b = (
        lax.psum(grad_a[0].astype(jnp.bfloat16), "dp").astype(jnp.float32),
        lax.psum(grad_b[0].astype(jnp.bfloat16), "dp").astype(jnp.float32),
    )
    new_a = factor_a - rate_a * sum_a
    new_b = factor_b - rate_b * sum_b
    full_b = lax.all_gather(new_b.astype(jnp.bfloat16), "tensor", axis=2, tiled=True).astype(
        new_b.dtype
    )
    delta = jnp.einsum("prd,prk->pdk", new_a, full_b, precision=lax.Precision.HIGHEST)
    merged = (kv_weight.astype(jnp.float32) + 0.25 * delta).astype(jnp.bfloat16)
    joined = jnp.concatenate([merged[0], merged[1]], axis=1)
    rows_here = hidden_in.shape[0] // lax.axis_size("tensor")
    pieces = []
    for step in range(STEPS):
        term = jnp.dot(hidden_in[:, step, :], joined, preferred_element_type=jnp.float32)
        pieces.append(
            lax.psum_scatter(
                term.astype(jnp.bfloat16), "tensor", scatter_dimension=0, tiled=True
            ).astype(jnp.float32)
        )
    projected = jnp.stack(pieces, axis=1)
    kv_width = KVH * HD
    place = positions[:, None] + jnp.arange(STEPS, dtype=jnp.int32)[None, :]
    keys = normed_rotated(
        projected[..., :kv_width].reshape(rows_here, STEPS, KVH, HD), key_gain, place
    )
    new_keys = keys.reshape(rows_here, STEPS, kv_width).astype(jnp.bfloat16)
    new_values = projected[..., kv_width:].astype(jnp.bfloat16)
    attended = attend(queries, cache_keys, cache_values, new_keys, new_values, cache_lengths)
    return (attended, new_a, new_b)


CHUNKS = (4, 4)
GROUP = 12
HEADS_STEP = 2


def params(limit=VMEM_LIMIT):
    return pltpu.CompilerParams(vmem_limit_bytes=limit)


def cost(flops, args, outs):
    size = sum(math.prod(x.shape) * x.dtype.itemsize for x in [*args, *outs])
    return pl.CostEstimate(flops=flops, bytes_accessed=size, transcendentals=0)


def dot(a, b):
    return jnp.dot(a, b, preferred_element_type=F32)


def dot_t(a, b):
    return lax.dot_general(a, b, (((1,), (1,)), ((), ())), preferred_element_type=F32)


def whole(shape):
    return pl.BlockSpec(shape, lambda i, *_: (0,) * len(shape))


def hbm(x):
    return pltpu.with_memory_space_constraint(x, pltpu.HBM)


TILE = 256


def terms_kernel(first, ids, hidden, wk, wv, after, *outs):
    del after
    if first:
        x, *outs = outs
        tokens = x.shape[0] // 4

        @pl.when(pl.program_id(0) == 0)
        def _():
            for r in range(4):
                at = pl.ds((ids[0] ^ r) * (tokens // STEPS), tokens // STEPS)
                x[r * tokens : (r + 1) * tokens] = hidden[at].reshape(tokens, x.shape[1])

    else:
        x = hidden
        tokens = x.shape[0] // 4
    ksend, kkeep, vsend, vkeep0, vkeep1 = outs
    steps = x.shape[1] // TILE

    def push(k):
        at = slice(k * TILE, (k + 1) * TILE)
        pltpu.matmul_push_rhs(wk[0, at, :], k % 2, 0)
        pltpu.matmul_push_rhs(wv[0, at, :], k % 2, 1)

    def multiply(*accs):
        accs_k, accs_v = accs[:4], accs[4:]
        push(0)
        for k in range(steps):
            if k + 1 < steps:
                push(k + 1)
            for r in range(4):
                rows = x[r * tokens : (r + 1) * tokens, k * TILE : (k + 1) * TILE]
                staged = k % 2 if r == 0 else None
                pltpu.matmul_acc_lhs(accs_k[r], rows, load_staged_rhs=staged)
                pltpu.matmul_acc_lhs(accs_v[r], rows, load_staged_rhs=staged)
        key = [pltpu.matmul_pop(acc).astype(BF) for acc in accs_k]
        value = [pltpu.matmul_pop(acc).astype(BF) for acc in accs_v]
        kkeep[:tokens], kkeep[tokens:] = key[0], key[2]
        ksend[:tokens], ksend[tokens:] = key[3], key[1]
        vkeep0[...], vkeep1[...] = value[0], value[1]
        vsend[:tokens], vsend[tokens:] = value[2], value[3]

    pl.run_scoped(
        multiply, *[pltpu.ACC(unit)((tokens, TILE), F32) for unit in range(2) for _ in range(4)]
    )


def projection_terms(ids, hidden, kv_weight, start, count, tokens, after):
    first = len(hidden.shape) == 3
    width = hidden.shape[-1]
    wide = count * HD
    base = start * HD // TILE
    assert wide % TILE == 0 and start * HD % TILE == 0 and width % TILE == 0
    rows = (2, 2, 2, 1, 1)
    outs = [jax.ShapeDtypeStruct((n * tokens, wide), BF) for n in rows]
    specs = [pl.BlockSpec((n * tokens, TILE), lambda i, _: (0, i)) for n in rows]
    if first:
        outs.insert(0, jax.ShapeDtypeStruct((4 * tokens, width), BF))
        specs.insert(0, whole(outs[0].shape))
    return pl.pallas_call(
        functools.partial(terms_kernel, first),
        out_shape=outs,
        grid_spec=pltpu.PrefetchScalarGridSpec(
            num_scalar_prefetch=1,
            grid=(wide // TILE,),
            in_specs=[
                whole(hidden.shape),
                pl.BlockSpec((1, width, TILE), lambda i, _: (0, 0, base + i)),
                pl.BlockSpec((1, width, TILE), lambda i, _: (1, 0, base + i)),
                pl.BlockSpec(memory_space=pl.ANY),
            ],
            out_specs=specs,
        ),
        compiler_params=params(),
        cost_estimate=cost(2 * 4 * tokens * width * 2 * wide, [hidden], outs),
        name="projection_terms",
    )(ids, hbm(hidden) if first else hidden, hbm(kv_weight), hbm(kv_weight), after)


def mid_kernel(kkeep, kcame, vkeep, vcame, after, kout, vout):
    del after
    kout[...] = (kkeep[...].astype(F32) + kcame[...].astype(F32)).astype(BF)
    vout[...] = (vkeep[...].astype(F32) + vcame[...].astype(F32)).astype(BF)


def mid_sums(kkeep, kcame, vkeep, vcame, after):
    shape = vkeep.shape
    low = pl.BlockSpec(shape, lambda i: (0, 0))
    high = pl.BlockSpec(shape, lambda i: (1, 0))
    return pl.pallas_call(
        mid_kernel,
        out_shape=[jax.ShapeDtypeStruct(shape, BF)] * 2,
        grid=(1,),
        in_specs=[high, low, low, high, pl.BlockSpec(memory_space=pl.ANY)],
        out_specs=[low, low],
        compiler_params=params(),
        cost_estimate=cost(0, [vkeep] * 6, []),
        name="mid_sums",
    )(kkeep, kcame, vkeep, vcame, after)


def pack_kernel(ids, grad_a, grad_b, out):
    del ids
    wide = grad_a.shape[-1]
    out[:, :wide] = grad_a[0, 0].astype(BF)
    out[:, wide:] = grad_b[0, 0].astype(BF)


def chip_kernel(ids, grad_a, grad_b, other, out):
    del ids
    wide = grad_a.shape[-1]
    out[:, :wide] = (grad_a[0, 0] + other[:, :wide].astype(F32)).astype(BF)
    out[:, wide:] = (grad_b[0, 0] + other[:, wide:].astype(F32)).astype(BF)


def grad_half(kernel, name, ids, grad_a, grad_b, flip, *rest):
    rank, wide = grad_a.shape[2], grad_a.shape[3] + grad_b.shape[3]

    def spec(x):
        return pl.BlockSpec((1, 1) + x.shape[2:], lambda i, ids: (0, ids[2] ^ flip, 0, 0))

    out = jax.ShapeDtypeStruct((rank, wide), BF)
    return pl.pallas_call(
        kernel,
        out_shape=out,
        grid_spec=pltpu.PrefetchScalarGridSpec(
            num_scalar_prefetch=1,
            grid=(1,),
            in_specs=[spec(grad_a), spec(grad_b)] + [whole(x.shape) for x in rest],
            out_specs=whole(out.shape),
        ),
        compiler_params=params(),
        cost_estimate=cost(0, [out] * 4, []),
        name=name,
    )(ids, hbm(grad_a), hbm(grad_b), *rest)


def small_call(kernel, name, ids, args, outs, after=()):
    count = len(args)

    def body(ids, *refs):
        kernel(ids, *refs[:count], *refs[count + len(after) :])

    return pl.pallas_call(
        body,
        out_shape=outs,
        grid_spec=pltpu.PrefetchScalarGridSpec(
            num_scalar_prefetch=1,
            grid=(1,),
            in_specs=[whole(x.shape) for x in args]
            + [pl.BlockSpec(memory_space=pl.ANY)] * len(after),
            out_specs=[whole(x.shape) for x in outs],
        ),
        compiler_params=params(),
        cost_estimate=cost(0, args, outs),
        name=name,
    )(ids, *args, *after)


def core_flip(x, count):
    return lax.ppermute(x, "dp", [(i, i ^ 1) for i in range(count)])


def plus_kernel(a, b, after, out):
    del after
    out[...] = (a[...].astype(F32) + b[...].astype(F32)).astype(BF)


def plus(a, b, after):
    out = jax.ShapeDtypeStruct(a.shape, BF)
    return pl.pallas_call(
        plus_kernel,
        out_shape=out,
        grid=(1,),
        in_specs=[whole(a.shape)] * 2 + [pl.BlockSpec(memory_space=pl.ANY)],
        out_specs=whole(a.shape),
        compiler_params=params(),
        cost_estimate=cost(0, [a, b], [out]),
        name="plus",
    )(a, b, after)


def along_line(x, d, count):
    return lax.ppermute(x, "dp", [(i, i ^ (2 * d)) for i in range(count)])


TOP = 2 * R


def update_kernel(rates, ids, half, other, factor_a, factor_b, new_a, new_b, a):
    wide = factor_a.shape[-1]
    for index, part in ((ids[2], half), (ids[2] ^ 1, other)):
        new_a[index] = factor_a[index] - rates[0] * part[:, :wide].astype(F32)
        new_b[index] = factor_b[index] - rates[1] * part[:, wide:].astype(F32)
    for p in range(2):
        a[p * R : (p + 1) * R] = new_a[p].astype(BF)


def updated(ids, half, other, factor_a, factor_b, dp, after):
    rates = (2.0 / math.sqrt(dp * D), 2.0 / math.sqrt(dp * R))
    outs = [
        jax.ShapeDtypeStruct(factor_a.shape, F32),
        jax.ShapeDtypeStruct(factor_b.shape, F32),
        jax.ShapeDtypeStruct((2 * R, factor_a.shape[2]), BF),
    ]
    return small_call(
        functools.partial(update_kernel, rates),
        "update_factors",
        ids,
        (half, other, factor_a, factor_b),
        outs,
        (after,),
    )


def payload_kernel(ids, u, new_b, *sends):
    del ids
    tokens = u.shape[0] // 4
    for r, out in enumerate(sends):
        first = r * tokens
        for p in range(2):
            out[p * R : (p + 1) * R, :] = new_b[p].astype(BF)
        out[TOP:, :TOP] = u[first : first + TOP]
        out[TOP:tokens, TOP:] = u[first + TOP : first + tokens]
        out[tokens:, TOP:] = jnp.zeros((2 * TOP - tokens, TOP), BF)


def payloads(ids, u, new_b):
    outs = [jax.ShapeDtypeStruct((2 * TOP, 2 * TOP), BF)] * 4
    return small_call(payload_kernel, "pack_terms", ids, (u, new_b), outs)


def attend_kernel(start, ids, lengths, *refs):
    q, cache_k, cache_v, k0, k1, k2, v0, v1, v2, *ub, cosine, sine = refs[:15]
    out = refs[-1]
    rows, slots, _ = cache_k.shape
    tokens = rows * STEPS
    u_top = sum(x[TOP:, :TOP].astype(F32) for x in ub)
    u_low = sum(x[TOP:tokens, TOP:].astype(F32) for x in ub)
    u = jnp.concatenate([u_top, u_low], axis=0).astype(BF)
    rel = ids[0] ^ (start // HEADS_STEP + pl.program_id(0))
    low = jnp.where(rel == 0, ub[0][:TOP].astype(F32), ub[1][:TOP].astype(F32))
    high = jnp.where(rel == 2, ub[2][:TOP].astype(F32), ub[3][:TOP].astype(F32))
    b = jnp.where(rel < 2, low, high).astype(BF)
    k = k0[...].astype(F32) + k1[...].astype(F32) + k2[...].astype(F32) + dot(u[:, :R], b[:R])
    v = v0[...].astype(F32) + v1[...].astype(F32) + v2[...].astype(F32) + dot(u[:, R:], b[R:])
    v = v.astype(BF)
    keys = []
    for n in range(HEADS_STEP):
        key = k[:, n * HD : (n + 1) * HD]
        scale = lax.rsqrt(jnp.sum(key * key, axis=-1, keepdims=True) * (1.0 / HD) + 1e-06)
        key = scale * (key * cosine[...] + pltpu.roll(key, HD // 2, 1) * sine[...])
        keys.append(key.astype(BF))
    n_q, n_c = GROUP * STEPS, GROUP * slots
    shape = (n_q, n_c + n_q)
    here = lax.broadcasted_iota(jnp.int32, shape, 0)
    col = lax.broadcasted_iota(jnp.int32, shape, 1)
    fresh = col - n_c
    cached = (col < n_c) & (here // STEPS == col // slots)
    new = (col >= n_c) & (here // STEPS == fresh // STEPS) & (fresh % STEPS <= here % STEPS)
    bias_here = jnp.where(cached | new, 0.0, -1e30)
    col = lax.broadcasted_iota(jnp.int32, (1, n_c + n_q), 1)
    ones = jnp.ones((n_c + n_q, HD), BF)
    factor = math.log2(math.e) * HD**-0.5
    heads = QH // KVH
    blocks = rows // GROUP
    query = q[...].reshape(tokens, HEADS_STEP * heads * HD)

    def block(n, g, cache, fresh):
        old = cache[g * GROUP : (g + 1) * GROUP, :, n * HD : (n + 1) * HD].reshape(n_c, HD)
        return jnp.concatenate([old, fresh[g * n_q : (g + 1) * n_q]], axis=0)

    every = [(n, g) for n in range(HEADS_STEP) for g in range(blocks)]
    scores = []
    for n, g in every:
        part = [query[g * n_q : (g + 1) * n_q, h * HD : (h + 1) * HD] for h in range(n * heads, (n + 1) * heads)]
        scores.append(dot_t(jnp.concatenate(part, axis=0), block(n, g, cache_k, keys[n])))
    biases = []
    for g in range(blocks):
        filled = jnp.full(col.shape, lengths[g * GROUP], jnp.int32)
        for i in range(1, GROUP):
            filled = jnp.where(col // slots == i, lengths[g * GROUP + i], filled)
        bias = jnp.where((col >= n_c) | (col % slots < filled), 0.0, -1e30) + bias_here
        biases.append(jnp.concatenate([bias] * heads, axis=0))
    weights = []
    for (n, g), s in zip(every, scores):
        s = s * factor + biases[g]
        top = jnp.max(s, axis=-1, keepdims=True)
        weights.append(jnp.exp2(s - top).astype(BF))
    results = []
    for (n, g), w in zip(every, weights):
        here_v = block(n, g, cache_v, v[:, n * HD : (n + 1) * HD])
        r = dot(w, jnp.concatenate([here_v, ones], axis=1))
        total = r[:, HD:]
        inverse = pl.reciprocal(total, approx=True)
        inverse = inverse * (2.0 - total * inverse)
        results.append((r[:, :HD] * inverse).astype(BF))
    for n in range(HEADS_STEP):
        for h in range(heads):
            part = [r[h * n_q : (h + 1) * n_q] for r in results[n * blocks : (n + 1) * blocks]]
            at = (n * heads + h) * HD
            out[:, :, at : at + HD] = jnp.concatenate(part, axis=0).reshape(rows, STEPS, HD)


def attend_chunk(
    ids, lengths, start, count, queries, cache_keys, cache_values, terms, ub, tables, before
):
    rows, slots, _ = cache_keys.shape
    tokens = rows * STEPS
    heads = QH // KVH
    args = [queries, cache_keys, cache_values, *terms, *ub, *tables]
    assert start % HEADS_STEP == 0 and count % HEADS_STEP == 0
    first = start // HEADS_STEP
    size = HEADS_STEP * HD
    part = pl.BlockSpec((tokens, size), lambda i, *_: (0, i))
    low = pl.BlockSpec((tokens, size), lambda i, *_: (1, i))
    cache = pl.BlockSpec((rows, slots, size), lambda i, *_: (0, 0, first + i))
    wide = pl.BlockSpec((rows, STEPS, heads * size), lambda i, *_: (0, 0, first + i))
    specs = [wide, cache, cache, part, low, part, part, part, part]
    specs += [whole(x.shape) for x in (*ub, *tables)]
    aliases = {}
    if before is not None:
        args.append(before)
        specs.append(pl.BlockSpec(memory_space=pl.ANY))
        aliases = {len(args) + 1: 0}
    return pl.pallas_call(
        functools.partial(attend_kernel, start),
        out_shape=jax.ShapeDtypeStruct(queries.shape, BF),
        grid_spec=pltpu.PrefetchScalarGridSpec(
            num_scalar_prefetch=2, grid=(count // HEADS_STEP,), in_specs=specs, out_specs=wide
        ),
        input_output_aliases=aliases,
        compiler_params=params(),
        cost_estimate=cost(count * 4 * 10**9, args, []),
        name="attend_chunk",
    )(ids, lengths, *args)


def rotary_tables(key_gain, positions):
    half = HD // 2
    place = positions[:, None] + jnp.arange(STEPS, dtype=jnp.int32)[None, :]
    freq = jnp.exp(-math.log(1000000.0) * (jnp.arange(half, dtype=F32) * 2.0 / HD))
    angle = place.reshape(-1).astype(F32)[:, None] * jnp.concatenate([freq, freq])
    turned = jnp.concatenate([-key_gain[half:], key_gain[:half]])
    return jnp.cos(angle) * key_gain, jnp.sin(angle) * turned


def across(x, r):
    return lax.ppermute(x, "tensor", [(i, i ^ r) for i in range(4)])


def square(
    hidden_in,
    kv_weight,
    factor_a,
    factor_b,
    grad_a,
    grad_b,
    key_gain,
    queries,
    cache_keys,
    cache_values,
    cache_lengths,
    positions,
):
    tokens = cache_keys.shape[0] * STEPS
    count_dp = lax.axis_size("dp")
    dp = lax.axis_index("dp")
    ids = jnp.stack([lax.axis_index("tensor"), dp // 2, dp % 2]).astype(jnp.int32)
    tables = rotary_tables(key_gain, positions)

    packed = grad_half(pack_kernel, "pack_grads", ids, grad_a, grad_b, 1)
    other = core_flip(packed, count_dp)
    half = grad_half(chip_kernel, "chip_grads", ids, grad_a, grad_b, 0, other)
    x, *first = projection_terms(ids, hidden_in, kv_weight, 0, CHUNKS[0], tokens, half)
    step, before = 1, first[0]
    while 4 * step < count_dp:
        half = plus(half, along_line(half, step, count_dp), before)
        step, before = 2 * step, half
    second = projection_terms(ids, x, kv_weight, CHUNKS[0], CHUNKS[1], tokens, half)
    if step * 2 < count_dp:
        half = plus(half, along_line(half, step, count_dp), second[0])
    other = core_flip(half, count_dp)

    def first_exchange(term, after):
        ksend, kkeep, vsend, vkeep0, vkeep1 = term
        kcame, vcame = across(ksend, 1), across(vsend, 2)
        mids = mid_sums(kkeep, kcame, vkeep1, vcame, after)
        return mids, (kkeep, kcame, vkeep0, vcame)

    def second_exchange(mids, parts):
        kkeep, kcame, vkeep0, vcame = parts
        return kkeep, kcame, across(mids[0], 2), vkeep0, vcame, across(mids[1], 1)

    mids, parts = first_exchange(first, half)
    first = second_exchange(mids, parts)
    new_a, new_b, a = updated(ids, half, other, factor_a, factor_b, count_dp, mids[0])
    sends = payloads(ids, (0.25 * dot_t(x, a)).astype(BF), new_b)
    ub = [sends[0]] + [across(sends[r], r) for r in (1, 2, 3)]
    second = second_exchange(*first_exchange(second, sends[0]))
    attended = None
    for start, count, came in ((0, CHUNKS[0], first), (CHUNKS[0], CHUNKS[1], second)):
        attended = attend_chunk(
            ids,
            cache_lengths,
            start,
            count,
            queries,
            cache_keys,
            cache_values,
            came,
            ub,
            tables,
            attended,
        )
    return attended, new_a, new_b


def solution(mesh):
    fits = mesh.shape["tensor"] == 4 and mesh.shape["dp"] in (2, 4, 8)
    return jax.shard_map(
        square if fits else general,
        mesh=mesh,
        in_specs=(
            P("dp", None, "tensor"),
            P(None, "tensor", None),
            P(None, None, "tensor"),
            P(None, None, "tensor"),
            P("dp", None, None, "tensor"),
            P("dp", None, None, "tensor"),
            P(),
            P(("dp", "tensor"), None, None),
            P(("dp", "tensor"), None, None),
            P(("dp", "tensor"), None, None),
            P(("dp", "tensor")),
            P(("dp", "tensor")),
        ),
        out_specs=(
            P(("dp", "tensor"), None, None),
            P(None, None, "tensor"),
            P(None, None, "tensor"),
        ),
        check_vma=False,
    )
```

```python
import functools
import math

import jax
import jax.numpy as jnp
from jax import lax
from jax.experimental import pallas as pl
from jax.experimental.pallas import tpu as pltpu
from jax.sharding import PartitionSpec as P

D = 5120
KVH = 8
HD = 128
QH = 32
R = 64
STEPS = 4
BF = jnp.bfloat16
F32 = jnp.float32
VMEM_LIMIT = 24 * 1024 * 1024


def normed_rotated(keys, gain, position):
    scale = lax.rsqrt(jnp.mean(keys * keys, axis=-1, keepdims=True) + 1e-06)
    keys = keys * scale * gain
    half = keys.shape[-1] // 2
    freq = jnp.exp(
        -math.log(1000000.0) * (jnp.arange(half, dtype=jnp.float32) * 2.0 / keys.shape[-1])
    )
    angle = position.astype(jnp.float32)[..., None] * freq
    cosine = jnp.concatenate([jnp.cos(angle), jnp.cos(angle)], axis=-1)[..., None, :]
    sine = jnp.concatenate([jnp.sin(angle), jnp.sin(angle)], axis=-1)[..., None, :]
    turned = jnp.concatenate([-keys[..., half:], keys[..., :half]], axis=-1)
    return keys * cosine + turned * sine


def attend(queries, cache_keys, cache_values, new_keys, new_values, lengths):
    rows, steps, width = queries.shape
    slots = cache_keys.shape[1]
    slot = jnp.arange(slots, dtype=jnp.int32)
    for step in range(steps):
        hit = (slot[None, :] == lengths[:, None] + step)[:, :, None]
        cache_keys = jnp.where(hit, new_keys[:, step][:, None, :], cache_keys)
        cache_values = jnp.where(hit, new_values[:, step][:, None, :], cache_values)
    groups = QH // KVH
    query_five = queries.reshape(rows, steps, KVH, groups, HD)
    key_four = cache_keys.reshape(rows, slots, KVH, HD)
    value_four = cache_values.reshape(rows, slots, KVH, HD)
    scores = jnp.einsum(
        "rtkgd,rckd->rtkgc", query_five, key_four, preferred_element_type=jnp.float32
    ) * HD ** (-0.5)
    limit = lengths[:, None] + jnp.arange(steps, dtype=jnp.int32)[None, :]
    valid = (slot[None, None, :] <= limit[:, :, None])[:, :, None, None, :]
    scores = jnp.where(valid, scores, jnp.float32(-1e30))
    top = jnp.max(scores, axis=-1, keepdims=True)
    expo = jnp.exp(scores - top)
    weights = (expo / jnp.sum(expo, axis=-1, keepdims=True)).astype(jnp.bfloat16)
    result = jnp.einsum(
        "rtkgc,rckd->rtkgd", weights, value_four, preferred_element_type=jnp.float32
    )
    return result.reshape(rows, steps, width).astype(jnp.bfloat16)


def general(
    hidden_in,
    kv_weight,
    factor_a,
    factor_b,
    grad_a,
    grad_b,
    key_gain,
    queries,
    cache_keys,
    cache_values,
    cache_lengths,
    positions,
):
    groups_dp = lax.axis_size("dp")
    rate_a = 2.0 / math.sqrt(groups_dp * D)
    rate_b = 2.0 / math.sqrt(groups_dp * R)
    sum_a, sum_b = (
        lax.psum(grad_a[0].astype(jnp.bfloat16), "dp").astype(jnp.float32),
        lax.psum(grad_b[0].astype(jnp.bfloat16), "dp").astype(jnp.float32),
    )
    new_a = factor_a - rate_a * sum_a
    new_b = factor_b - rate_b * sum_b
    full_b = lax.all_gather(new_b.astype(jnp.bfloat16), "tensor", axis=2, tiled=True).astype(
        new_b.dtype
    )
    delta = jnp.einsum("prd,prk->pdk", new_a, full_b, precision=lax.Precision.HIGHEST)
    merged = (kv_weight.astype(jnp.float32) + 0.25 * delta).astype(jnp.bfloat16)
    joined = jnp.concatenate([merged[0], merged[1]], axis=1)
    rows_here = hidden_in.shape[0] // lax.axis_size("tensor")
    pieces = []
    for step in range(STEPS):
        term = jnp.dot(hidden_in[:, step, :], joined, preferred_element_type=jnp.float32)
        pieces.append(
            lax.psum_scatter(
                term.astype(jnp.bfloat16), "tensor", scatter_dimension=0, tiled=True
            ).astype(jnp.float32)
        )
    projected = jnp.stack(pieces, axis=1)
    kv_width = KVH * HD
    place = positions[:, None] + jnp.arange(STEPS, dtype=jnp.int32)[None, :]
    keys = normed_rotated(
        projected[..., :kv_width].reshape(rows_here, STEPS, KVH, HD), key_gain, place
    )
    new_keys = keys.reshape(rows_here, STEPS, kv_width).astype(jnp.bfloat16)
    new_values = projected[..., kv_width:].astype(jnp.bfloat16)
    attended = attend(queries, cache_keys, cache_values, new_keys, new_values, cache_lengths)
    return (attended, new_a, new_b)


CHUNKS = (4, 4)
GROUP = 12
HEADS_STEP = 2


def params(limit=VMEM_LIMIT):
    return pltpu.CompilerParams(vmem_limit_bytes=limit)


def cost(flops, args, outs):
    size = sum(math.prod(x.shape) * x.dtype.itemsize for x in [*args, *outs])
    return pl.CostEstimate(flops=flops, bytes_accessed=size, transcendentals=0)


def dot(a, b):
    return jnp.dot(a, b, preferred_element_type=F32)


def dot_t(a, b):
    return lax.dot_general(a, b, (((1,), (1,)), ((), ())), preferred_element_type=F32)


def whole(shape):
    return pl.BlockSpec(shape, lambda i, *_: (0,) * len(shape))


def hbm(x):
    return pltpu.with_memory_space_constraint(x, pltpu.HBM)


TILE = 256


def terms_kernel(first, ids, hidden, weight, *rest):
    *outs, w, sems = rest[1:]
    wide = w.shape[1] * TILE
    start = 0 if first else weight.shape[2] - wide
    tiles = w.shape[1]

    def weight_copy(p, i):
        at = pl.ds(start + i * TILE, TILE)
        return pltpu.make_async_copy(weight.at[p, :, at], w.at[p, i], sems.at[p, i])

    if first:
        x, *outs, held, hidden_sems = outs
        tokens = x.shape[0] // 4
        rows = tokens // STEPS

        def hidden_copy(r):
            at = pl.ds((ids[0] ^ r) * rows, rows)
            return pltpu.make_async_copy(hidden.at[at], held.at[r], hidden_sems.at[r])

        for r in range(4):
            hidden_copy(r).start()
    else:
        x = hidden
        tokens = x.shape[0] // 4
    for i in range(tiles):
        for p in range(2):
            weight_copy(p, i).start()
    if first:
        for r in range(4):
            hidden_copy(r).wait()
            x[r * tokens : (r + 1) * tokens] = held[r].reshape(tokens, x.shape[1])
    ksend, kkeep, vsend, vkeep0, vkeep1 = outs
    steps = x.shape[1] // TILE

    def multiply(*accs):
        accs_k, accs_v = accs[:4], accs[4:]

        @pl.loop(0, tiles)
        def _(i):
            for p in range(2):
                weight_copy(p, i).wait()

            def push(k):
                for p in range(2):
                    pltpu.matmul_push_rhs(w[p, i, k * TILE : (k + 1) * TILE, :], k % 2, p)

            push(0)
            for k in range(steps):
                if k + 1 < steps:
                    push(k + 1)
                for r in range(4):
                    rows = x[r * tokens : (r + 1) * tokens, k * TILE : (k + 1) * TILE]
                    staged = k % 2 if r == 0 else None
                    pltpu.matmul_acc_lhs(accs_k[r], rows, load_staged_rhs=staged)
                    pltpu.matmul_acc_lhs(accs_v[r], rows, load_staged_rhs=staged)
            at = pl.ds(pl.multiple_of(i * TILE, TILE), TILE)
            low, high = slice(0, tokens), slice(tokens, 2 * tokens)
            kkeep[low, at] = pltpu.matmul_pop(accs_k[0]).astype(BF)
            vkeep0[:, at] = pltpu.matmul_pop(accs_v[0]).astype(BF)
            ksend[high, at] = pltpu.matmul_pop(accs_k[1]).astype(BF)
            vkeep1[:, at] = pltpu.matmul_pop(accs_v[1]).astype(BF)
            kkeep[high, at] = pltpu.matmul_pop(accs_k[2]).astype(BF)
            vsend[low, at] = pltpu.matmul_pop(accs_v[2]).astype(BF)
            ksend[low, at] = pltpu.matmul_pop(accs_k[3]).astype(BF)
            vsend[high, at] = pltpu.matmul_pop(accs_v[3]).astype(BF)

    pl.run_scoped(
        multiply, *[pltpu.ACC(unit)((tokens, TILE), F32) for unit in range(2) for _ in range(4)]
    )


def projection_terms(ids, hidden, kv_weight, count, tokens, after):
    first = len(hidden.shape) == 3
    width = hidden.shape[-1]
    wide = count * HD
    assert wide % TILE == 0 and width % TILE == 0
    rows = (2, 2, 2, 1, 1)
    outs = [jax.ShapeDtypeStruct((n * tokens, wide), BF) for n in rows]
    scratch = []
    if first:
        outs.insert(0, jax.ShapeDtypeStruct((4 * tokens, width), BF))
        scratch += [
            pltpu.VMEM((4, tokens // STEPS, STEPS, width), BF),
            pltpu.SemaphoreType.DMA((4,)),
        ]
    scratch += [
        pltpu.VMEM((2, wide // TILE, width, TILE), BF),
        pltpu.SemaphoreType.DMA((2, wide // TILE)),
    ]
    here = pl.BlockSpec(memory_space=pl.ANY)
    return pl.pallas_call(
        functools.partial(terms_kernel, first),
        out_shape=outs,
        grid_spec=pltpu.PrefetchScalarGridSpec(
            num_scalar_prefetch=1,
            grid=(1,),
            in_specs=[here if first else whole(hidden.shape), here, here],
            out_specs=[whole(x.shape) for x in outs],
            scratch_shapes=scratch,
        ),
        compiler_params=params(),
        cost_estimate=cost(2 * 4 * tokens * width * 2 * wide, [hidden], outs),
        name="projection_terms",
    )(ids, hbm(hidden) if first else hidden, hbm(kv_weight), after)


def mid_kernel(kkeep, kcame, vkeep, vcame, after, kout, vout):
    del after
    kout[...] = (kkeep[...].astype(F32) + kcame[...].astype(F32)).astype(BF)
    vout[...] = (vkeep[...].astype(F32) + vcame[...].astype(F32)).astype(BF)


def mid_sums(kkeep, kcame, vkeep, vcame, after):
    shape = vkeep.shape
    low = pl.BlockSpec(shape, lambda i: (0, 0))
    high = pl.BlockSpec(shape, lambda i: (1, 0))
    return pl.pallas_call(
        mid_kernel,
        out_shape=[jax.ShapeDtypeStruct(shape, BF)] * 2,
        grid=(1,),
        in_specs=[high, low, low, high, pl.BlockSpec(memory_space=pl.ANY)],
        out_specs=[low, low],
        compiler_params=params(),
        cost_estimate=cost(0, [vkeep] * 6, []),
        name="mid_sums",
    )(kkeep, kcame, vkeep, vcame, after)


def pack_kernel(ids, grad_a, grad_b, after, out, unwritten):
    del ids, after, unwritten
    wide = grad_a.shape[-1]
    out[:, :wide] = grad_a[0, 0].astype(BF)
    out[:, wide:] = grad_b[0, 0].astype(BF)


def chip_kernel(ids, grad_a, grad_b, other, out):
    del ids
    wide = grad_a.shape[-1]
    out[:, :wide] = (grad_a[0, 0] + other[:, :wide].astype(F32)).astype(BF)
    out[:, wide:] = (grad_b[0, 0] + other[:, wide:].astype(F32)).astype(BF)


def grad_half(kernel, name, ids, grad_a, grad_b, flip, rest, rest_specs, more_outs=()):
    rank, wide = grad_a.shape[2], grad_a.shape[3] + grad_b.shape[3]

    def spec(x):
        return pl.BlockSpec((1, 1) + x.shape[2:], lambda i, ids: (0, ids[2] ^ flip, 0, 0))

    out = jax.ShapeDtypeStruct((rank, wide), BF)
    return pl.pallas_call(
        kernel,
        out_shape=[out, *more_outs],
        grid_spec=pltpu.PrefetchScalarGridSpec(
            num_scalar_prefetch=1,
            grid=(1,),
            in_specs=[spec(grad_a), spec(grad_b), *rest_specs],
            out_specs=[whole(out.shape)] + [pl.BlockSpec(memory_space=pl.ANY)] * len(more_outs),
        ),
        compiler_params=params(),
        cost_estimate=cost(0, [out] * 4, []),
        name=name,
    )(ids, hbm(grad_a), hbm(grad_b), *rest)


def small_call(kernel, name, ids, args, outs, after=(), scratch=()):
    count = len(args)

    def body(ids, *refs):
        kernel(ids, *refs[:count], *refs[count + len(after) :])

    return pl.pallas_call(
        body,
        out_shape=outs,
        grid_spec=pltpu.PrefetchScalarGridSpec(
            num_scalar_prefetch=1,
            grid=(1,),
            in_specs=[whole(x.shape) for x in args]
            + [pl.BlockSpec(memory_space=pl.ANY)] * len(after),
            out_specs=[whole(x.shape) for x in outs],
            scratch_shapes=list(scratch),
        ),
        compiler_params=params(),
        cost_estimate=cost(0, args, []),
        name=name,
    )(ids, *args, *after)


def core_flip(x, count):
    return lax.ppermute(x, "dp", [(i, i ^ 1) for i in range(count)])


def plus_kernel(a, b, after, out):
    del after
    out[...] = (a[...].astype(F32) + b[...].astype(F32)).astype(BF)


def plus(a, b, after):
    out = jax.ShapeDtypeStruct(a.shape, BF)
    return pl.pallas_call(
        plus_kernel,
        out_shape=out,
        grid=(1,),
        in_specs=[whole(a.shape)] * 2 + [pl.BlockSpec(memory_space=pl.ANY)],
        out_specs=whole(a.shape),
        compiler_params=params(),
        cost_estimate=cost(0, [a, b], [out]),
        name="plus",
    )(a, b, after)


def along_line(x, d, count):
    return lax.ppermute(x, "dp", [(i, i ^ (2 * d)) for i in range(count)])


TOP = 2 * R


def update_kernel(rates, ids, half, other, factor_a, factor_b, x, new_a, new_b, *rest):
    *sends, a = rest
    wide = factor_a.shape[-1]
    for index, part in ((ids[2], half), (ids[2] ^ 1, other)):
        new_a[index] = factor_a[index] - rates[0] * part[:, :wide].astype(F32)
        new_b[index] = factor_b[index] - rates[1] * part[:, wide:].astype(F32)
    for p in range(2):
        a[p * R : (p + 1) * R] = new_a[p].astype(BF)
    a[TOP:] = jnp.zeros((TILE - TOP, wide), BF)
    tokens = x.shape[0] // 4

    def multiply(*accs):
        steps = wide // TILE

        def push(k):
            for unit in range(2):
                tile = a[:, k * TILE : (k + 1) * TILE]
                pltpu.matmul_push_rhs(tile, k % 2, unit, transpose=True)

        push(0)
        for k in range(steps):
            if k + 1 < steps:
                push(k + 1)
            for r in range(4):
                rows = x[r * tokens : (r + 1) * tokens, k * TILE : (k + 1) * TILE]
                staged = k % 2 if r < 2 else None
                pltpu.matmul_acc_lhs(accs[r], rows, load_staged_rhs=staged)
        for r, send in enumerate(sends):
            u = (0.25 * pltpu.matmul_pop(accs[r])[:, :TOP]).astype(BF)
            for p in range(2):
                send[p * R : (p + 1) * R, :] = new_b[p].astype(BF)
            send[TOP:, :TOP] = u[:TOP]
            send[TOP:tokens, TOP:] = u[TOP:]
            send[tokens:, TOP:] = jnp.zeros((2 * TOP - tokens, TOP), BF)

    pl.run_scoped(multiply, *[pltpu.ACC(r % 2)((tokens, TILE), F32) for r in range(4)])


def updated(ids, half, other, factor_a, factor_b, x, dp, after):
    rates = (2.0 / math.sqrt(dp * D), 2.0 / math.sqrt(dp * R))
    outs = [pltpu.VMEM(f.shape, F32) for f in (factor_a, factor_b)]
    outs += [jax.ShapeDtypeStruct((2 * TOP, 2 * TOP), BF)] * 4
    return small_call(
        functools.partial(update_kernel, rates),
        "update_factors",
        ids,
        (half, other, factor_a, factor_b, x),
        outs,
        (after,),
        [pltpu.VMEM((TILE, factor_a.shape[-1]), BF)],
    )


def attend_kernel(ids, first, lengths, *refs):
    q, cache_k, cache_v, k0, k1, k2, v0, v1, v2, *ub, cosine, sine = refs[:15]
    out = refs[-1]
    rows, slots, _ = cache_k.shape
    tokens = rows * STEPS
    u_top = sum(x[TOP:, :TOP].astype(F32) for x in ub)
    u_low = sum(x[TOP:tokens, TOP:].astype(F32) for x in ub)
    u = jnp.concatenate([u_top, u_low], axis=0).astype(BF)
    rel = ids[0] ^ (first[0] + pl.program_id(0))
    low = jnp.where(rel == 0, ub[0][:TOP].astype(F32), ub[1][:TOP].astype(F32))
    high = jnp.where(rel == 2, ub[2][:TOP].astype(F32), ub[3][:TOP].astype(F32))
    b = jnp.where(rel < 2, low, high).astype(BF)
    k = k0[...].astype(F32) + k1[...].astype(F32) + k2[...].astype(F32) + dot(u[:, :R], b[:R])
    v = v0[...].astype(F32) + v1[...].astype(F32) + v2[...].astype(F32) + dot(u[:, R:], b[R:])
    v = v.astype(BF)
    keys = []
    for n in range(HEADS_STEP):
        key = k[:, n * HD : (n + 1) * HD]
        scale = lax.rsqrt(jnp.sum(key * key, axis=-1, keepdims=True) * (1.0 / HD) + 1e-06)
        key = scale * (key * cosine[...] + pltpu.roll(key, HD // 2, 1) * sine[...])
        keys.append(key.astype(BF))
    n_q, n_c = GROUP * STEPS, GROUP * slots
    shape = (n_q, n_c + n_q)
    here = lax.broadcasted_iota(jnp.int32, shape, 0)
    col = lax.broadcasted_iota(jnp.int32, shape, 1)
    fresh = col - n_c
    cached = (col < n_c) & (here // STEPS == col // slots)
    new = (col >= n_c) & (here // STEPS == fresh // STEPS) & (fresh % STEPS <= here % STEPS)
    bias_here = jnp.where(cached | new, 0.0, -1e30)
    col = lax.broadcasted_iota(jnp.int32, (1, n_c + n_q), 1)
    ones = jnp.ones((n_c + n_q, HD), BF)
    factor = math.log2(math.e) * HD**-0.5
    heads = QH // KVH
    blocks = rows // GROUP
    query = q[...].reshape(tokens, HEADS_STEP * heads * HD)

    def block(n, g, cache, fresh):
        old = cache[g * GROUP : (g + 1) * GROUP, :, n * HD : (n + 1) * HD].reshape(n_c, HD)
        return jnp.concatenate([old, fresh[g * n_q : (g + 1) * n_q]], axis=0)

    every = [(n, g) for n in range(HEADS_STEP) for g in range(blocks)]
    scores = []
    for n, g in every:
        part = [query[g * n_q : (g + 1) * n_q, h * HD : (h + 1) * HD] for h in range(n * heads, (n + 1) * heads)]
        scores.append(dot_t(jnp.concatenate(part, axis=0), block(n, g, cache_k, keys[n])))
    biases = []
    for g in range(blocks):
        filled = jnp.full(col.shape, lengths[g * GROUP], jnp.int32)
        for i in range(1, GROUP):
            filled = jnp.where(col // slots == i, lengths[g * GROUP + i], filled)
        bias = jnp.where((col >= n_c) | (col % slots < filled), 0.0, -1e30) + bias_here
        biases.append(jnp.concatenate([bias] * heads, axis=0))
    weights = []
    for (n, g), s in zip(every, scores):
        s = s * factor + biases[g]
        top = jnp.max(s, axis=-1, keepdims=True)
        weights.append(jnp.exp2(s - top).astype(BF))
    results = []
    for (n, g), w in zip(every, weights):
        here_v = block(n, g, cache_v, v[:, n * HD : (n + 1) * HD])
        r = dot(w, jnp.concatenate([here_v, ones], axis=1))
        total = r[:, HD:]
        inverse = pl.reciprocal(total, approx=True)
        inverse = inverse * (2.0 - total * inverse)
        results.append((r[:, :HD] * inverse).astype(BF))
    for n in range(HEADS_STEP):
        for h in range(heads):
            part = [r[h * n_q : (h + 1) * n_q] for r in results[n * blocks : (n + 1) * blocks]]
            at = (n * heads + h) * HD
            out[:, :, at : at + HD] = jnp.concatenate(part, axis=0).reshape(rows, STEPS, HD)


def attend_chunk(
    ids, lengths, start, count, queries, cache_keys, cache_values, terms, ub, tables, before
):
    rows, slots, _ = cache_keys.shape
    tokens = rows * STEPS
    heads = QH // KVH
    args = [queries, cache_keys, cache_values, *terms, *ub, *tables]
    assert start % HEADS_STEP == 0 and count % HEADS_STEP == 0
    first = jnp.full((1,), start // HEADS_STEP, jnp.int32)
    size = HEADS_STEP * HD
    part = pl.BlockSpec((tokens, size), lambda i, *_: (0, i))
    low = pl.BlockSpec((tokens, size), lambda i, *_: (1, i))
    cache = pl.BlockSpec((rows, slots, size), lambda i, _, first, *__: (0, 0, first[0] + i))
    wide = pl.BlockSpec((rows, STEPS, heads * size), lambda i, _, first, *__: (0, 0, first[0] + i))
    specs = [wide, cache, cache, part, low, part, part, part, part]
    specs += [whole(x.shape) for x in (*ub, *tables)]
    args.append(before)
    specs.append(pl.BlockSpec(memory_space=pl.ANY))
    return pl.pallas_call(
        attend_kernel,
        out_shape=jax.ShapeDtypeStruct(queries.shape, BF),
        grid_spec=pltpu.PrefetchScalarGridSpec(
            num_scalar_prefetch=3, grid=(count // HEADS_STEP,), in_specs=specs, out_specs=wide
        ),
        input_output_aliases={len(args) + 2: 0},
        compiler_params=params(),
        cost_estimate=cost(count * 4 * 10**9, args, []),
        name="attend_chunk",
    )(ids, first, lengths, *args)


def rotary_tables(key_gain, positions):
    half = HD // 2
    place = positions[:, None] + jnp.arange(STEPS, dtype=jnp.int32)[None, :]
    freq = jnp.exp(-math.log(1000000.0) * (jnp.arange(half, dtype=F32) * 2.0 / HD))
    angle = place.reshape(-1).astype(F32)[:, None] * jnp.concatenate([freq, freq])
    turned = jnp.concatenate([-key_gain[half:], key_gain[:half]])
    return jnp.cos(angle) * key_gain, jnp.sin(angle) * turned


def across(x, r):
    return lax.ppermute(x, "tensor", [(i, i ^ r) for i in range(4)])


def square(
    hidden_in,
    kv_weight,
    factor_a,
    factor_b,
    grad_a,
    grad_b,
    key_gain,
    queries,
    cache_keys,
    cache_values,
    cache_lengths,
    positions,
):
    tokens = cache_keys.shape[0] * STEPS
    count_dp = lax.axis_size("dp")
    dp = lax.axis_index("dp")
    ids = jnp.stack([lax.axis_index("tensor"), dp // 2, dp % 2]).astype(jnp.int32)
    tables = rotary_tables(key_gain, positions)

    x, *first = projection_terms(ids, hidden_in, kv_weight, CHUNKS[0], tokens, ids)
    here = pl.BlockSpec(memory_space=pl.ANY)
    packed, attended = grad_half(
        pack_kernel,
        "pack_grads",
        ids,
        grad_a,
        grad_b,
        1,
        [first[0]],
        [here],
        [jax.ShapeDtypeStruct(queries.shape, BF)],
    )
    other = core_flip(packed, count_dp)
    (half,) = grad_half(
        chip_kernel, "chip_grads", ids, grad_a, grad_b, 0, [other], [whole(other.shape)]
    )
    step = 1
    while 4 * step < count_dp:
        came = along_line(half, step, count_dp)
        if step == 1:
            second = projection_terms(ids, x, kv_weight, CHUNKS[1], tokens, half)
        half = plus(half, came, second[0])
        step *= 2
    if step == 1:
        second = projection_terms(ids, x, kv_weight, CHUNKS[1], tokens, half)
    if 2 * step < count_dp:
        half = plus(half, along_line(half, step, count_dp), second[0])
    other = core_flip(half, count_dp)

    def first_exchange(term, after):
        ksend, kkeep, vsend, vkeep0, vkeep1 = term
        kcame, vcame = across(ksend, 1), across(vsend, 2)
        mids = mid_sums(kkeep, kcame, vkeep1, vcame, after)
        return mids, (kkeep, kcame, vkeep0, vcame)

    def second_exchange(mids, parts):
        kkeep, kcame, vkeep0, vcame = parts
        return kkeep, kcame, across(mids[0], 2), vkeep0, vcame, across(mids[1], 1)

    mids, parts = first_exchange(first, half)
    first = second_exchange(mids, parts)
    new_a, new_b, *sends = updated(
        ids, half, other, factor_a, factor_b, x, count_dp, mids[0]
    )
    ub = [sends[0]] + [across(sends[r], r) for r in (1, 2, 3)]
    second = second_exchange(*first_exchange(second, sends[0]))
    for start, count, came in ((0, CHUNKS[0], first), (CHUNKS[0], CHUNKS[1], second)):
        attended = attend_chunk(
            ids,
            cache_lengths,
            start,
            count,
            queries,
            cache_keys,
            cache_values,
            came,
            ub,
            tables,
            attended,
        )
    return attended, new_a, new_b


def solution(mesh):
    fits = mesh.shape["tensor"] == 4 and mesh.shape["dp"] in (2, 4, 8)
    return jax.shard_map(
        square if fits else general,
        mesh=mesh,
        in_specs=(
            P("dp", None, "tensor"),
            P(None, "tensor", None),
            P(None, None, "tensor"),
            P(None, None, "tensor"),
            P("dp", None, None, "tensor"),
            P("dp", None, None, "tensor"),
            P(),
            P(("dp", "tensor"), None, None),
            P(("dp", "tensor"), None, None),
            P(("dp", "tensor"), None, None),
            P(("dp", "tensor")),
            P(("dp", "tensor")),
        ),
        out_specs=(
            P(("dp", "tensor"), None, None),
            P(None, None, "tensor"),
            P(None, None, "tensor"),
        ),
        check_vma=False,
    )
```

```python
import functools
import math

import jax
import jax.numpy as jnp
from jax import lax
from jax.experimental import pallas as pl
from jax.experimental.pallas import tpu as pltpu
from jax.sharding import PartitionSpec as P

D = 5120
KVH = 8
HD = 128
QH = 32
R = 64
STEPS = 4
BF = jnp.bfloat16
F32 = jnp.float32
VMEM_LIMIT = 16 * 1024 * 1024


def normed_rotated(keys, gain, position):
    scale = lax.rsqrt(jnp.mean(keys * keys, axis=-1, keepdims=True) + 1e-06)
    keys = keys * scale * gain
    half = keys.shape[-1] // 2
    freq = jnp.exp(
        -math.log(1000000.0) * (jnp.arange(half, dtype=jnp.float32) * 2.0 / keys.shape[-1])
    )
    angle = position.astype(jnp.float32)[..., None] * freq
    cosine = jnp.concatenate([jnp.cos(angle), jnp.cos(angle)], axis=-1)[..., None, :]
    sine = jnp.concatenate([jnp.sin(angle), jnp.sin(angle)], axis=-1)[..., None, :]
    turned = jnp.concatenate([-keys[..., half:], keys[..., :half]], axis=-1)
    return keys * cosine + turned * sine


def attend(queries, cache_keys, cache_values, new_keys, new_values, lengths):
    rows, steps, width = queries.shape
    slots = cache_keys.shape[1]
    slot = jnp.arange(slots, dtype=jnp.int32)
    for step in range(steps):
        hit = (slot[None, :] == lengths[:, None] + step)[:, :, None]
        cache_keys = jnp.where(hit, new_keys[:, step][:, None, :], cache_keys)
        cache_values = jnp.where(hit, new_values[:, step][:, None, :], cache_values)
    groups = QH // KVH
    query_five = queries.reshape(rows, steps, KVH, groups, HD)
    key_four = cache_keys.reshape(rows, slots, KVH, HD)
    value_four = cache_values.reshape(rows, slots, KVH, HD)
    scores = jnp.einsum(
        "rtkgd,rckd->rtkgc", query_five, key_four, preferred_element_type=jnp.float32
    ) * HD ** (-0.5)
    limit = lengths[:, None] + jnp.arange(steps, dtype=jnp.int32)[None, :]
    valid = (slot[None, None, :] <= limit[:, :, None])[:, :, None, None, :]
    scores = jnp.where(valid, scores, jnp.float32(-1e30))
    top = jnp.max(scores, axis=-1, keepdims=True)
    expo = jnp.exp(scores - top)
    weights = (expo / jnp.sum(expo, axis=-1, keepdims=True)).astype(jnp.bfloat16)
    result = jnp.einsum(
        "rtkgc,rckd->rtkgd", weights, value_four, preferred_element_type=jnp.float32
    )
    return result.reshape(rows, steps, width).astype(jnp.bfloat16)


def general(
    hidden_in,
    kv_weight,
    factor_a,
    factor_b,
    grad_a,
    grad_b,
    key_gain,
    queries,
    cache_keys,
    cache_values,
    cache_lengths,
    positions,
):
    groups_dp = lax.axis_size("dp")
    rate_a = 2.0 / math.sqrt(groups_dp * D)
    rate_b = 2.0 / math.sqrt(groups_dp * R)
    sum_a, sum_b = (
        lax.psum(grad_a[0].astype(jnp.bfloat16), "dp").astype(jnp.float32),
        lax.psum(grad_b[0].astype(jnp.bfloat16), "dp").astype(jnp.float32),
    )
    new_a = factor_a - rate_a * sum_a
    new_b = factor_b - rate_b * sum_b
    full_b = lax.all_gather(new_b.astype(jnp.bfloat16), "tensor", axis=2, tiled=True).astype(
        new_b.dtype
    )
    delta = jnp.einsum("prd,prk->pdk", new_a, full_b, precision=lax.Precision.HIGHEST)
    merged = (kv_weight.astype(jnp.float32) + 0.25 * delta).astype(jnp.bfloat16)
    joined = jnp.concatenate([merged[0], merged[1]], axis=1)
    rows_here = hidden_in.shape[0] // lax.axis_size("tensor")
    pieces = []
    for step in range(STEPS):
        term = jnp.dot(hidden_in[:, step, :], joined, preferred_element_type=jnp.float32)
        pieces.append(
            lax.psum_scatter(
                term.astype(jnp.bfloat16), "tensor", scatter_dimension=0, tiled=True
            ).astype(jnp.float32)
        )
    projected = jnp.stack(pieces, axis=1)
    kv_width = KVH * HD
    place = positions[:, None] + jnp.arange(STEPS, dtype=jnp.int32)[None, :]
    keys = normed_rotated(
        projected[..., :kv_width].reshape(rows_here, STEPS, KVH, HD), key_gain, place
    )
    new_keys = keys.reshape(rows_here, STEPS, kv_width).astype(jnp.bfloat16)
    new_values = projected[..., kv_width:].astype(jnp.bfloat16)
    attended = attend(queries, cache_keys, cache_values, new_keys, new_values, cache_lengths)
    return (attended, new_a, new_b)


CHUNKS = (4, 4)
GROUP = 12
HEADS_STEP = 2


def params(limit=VMEM_LIMIT):
    return pltpu.CompilerParams(vmem_limit_bytes=limit)


def cost(flops, args, outs):
    size = sum(math.prod(x.shape) * x.dtype.itemsize for x in [*args, *outs])
    return pl.CostEstimate(flops=flops, bytes_accessed=size, transcendentals=0)


def dot(a, b):
    return jnp.dot(a, b, preferred_element_type=F32)


def dot_t(a, b):
    return lax.dot_general(a, b, (((1,), (1,)), ((), ())), preferred_element_type=F32)


def whole(shape):
    return pl.BlockSpec(shape, lambda i, *_: (0,) * len(shape))


def hbm(x):
    return pltpu.with_memory_space_constraint(x, pltpu.HBM)


TILE = 256


def terms_kernel(first, ids, hidden, weight, *rest):
    if first:
        x, *outs, held, hidden_sems, w, sems = rest[1:]
        tiles = w.shape[1]
        tokens = x.shape[0] // 4
        rows = tokens // STEPS

        def hidden_copy(r):
            at = pl.ds((ids[0] ^ r) * rows, rows)
            return pltpu.make_async_copy(hidden.at[at], held.at[r], hidden_sems.at[r])

        def weight_copy(p, i):
            at = pl.ds(i * TILE, TILE)
            return pltpu.make_async_copy(weight.at[p, :, at], w.at[p, i], sems.at[p, i])

        for r in range(4):
            hidden_copy(r).start()
        for i in range(tiles):
            for p in range(2):
                weight_copy(p, i).start()
        for r in range(4):
            hidden_copy(r).wait()
            x[r * tokens : (r + 1) * tokens] = held[r].reshape(tokens, x.shape[1])
    else:
        x, outs = hidden, rest[1:]
        tokens = x.shape[0] // 4
        tiles = outs[0].shape[1] // TILE
        base = weight.shape[2] - tiles * TILE
    ksend, kkeep, vsend, vkeep0, vkeep1 = outs
    steps = x.shape[1] // TILE

    def multiply(*accs):
        accs_k, accs_v = accs[:4], accs[4:]

        @pl.loop(0, tiles)
        def _(i):
            if first:
                for p in range(2):
                    weight_copy(p, i).wait()

            def push(k):
                rows = slice(k * TILE, (k + 1) * TILE)
                for p in range(2):
                    if first:
                        tile = w[p, i, rows, :]
                    else:
                        tile = weight[p, rows, pl.ds(pl.multiple_of(base + i * TILE, TILE), TILE)]
                    pltpu.matmul_push_rhs(tile, k % 2, p)

            push(0)
            for k in range(steps):
                if k + 1 < steps:
                    push(k + 1)
                for r in range(4):
                    rows = x[r * tokens : (r + 1) * tokens, k * TILE : (k + 1) * TILE]
                    staged = k % 2 if r == 0 else None
                    pltpu.matmul_acc_lhs(accs_k[r], rows, load_staged_rhs=staged)
                    pltpu.matmul_acc_lhs(accs_v[r], rows, load_staged_rhs=staged)
            at = pl.ds(pl.multiple_of(i * TILE, TILE), TILE)
            low, high = slice(0, tokens), slice(tokens, 2 * tokens)
            kkeep[low, at] = pltpu.matmul_pop(accs_k[0]).astype(BF)
            vkeep0[:, at] = pltpu.matmul_pop(accs_v[0]).astype(BF)
            ksend[high, at] = pltpu.matmul_pop(accs_k[1]).astype(BF)
            vkeep1[:, at] = pltpu.matmul_pop(accs_v[1]).astype(BF)
            kkeep[high, at] = pltpu.matmul_pop(accs_k[2]).astype(BF)
            vsend[low, at] = pltpu.matmul_pop(accs_v[2]).astype(BF)
            ksend[low, at] = pltpu.matmul_pop(accs_k[3]).astype(BF)
            vsend[high, at] = pltpu.matmul_pop(accs_v[3]).astype(BF)

    pl.run_scoped(
        multiply, *[pltpu.ACC(unit)((tokens, TILE), F32) for unit in range(2) for _ in range(4)]
    )


def projection_terms(ids, hidden, kv_weight, count, tokens, after):
    first = len(hidden.shape) == 3
    width = hidden.shape[-1]
    wide = count * HD
    assert wide % TILE == 0 and width % TILE == 0
    rows = (2, 2, 2, 1, 1)
    outs = [jax.ShapeDtypeStruct((n * tokens, wide), BF) for n in rows]
    scratch = []
    if first:
        outs.insert(0, jax.ShapeDtypeStruct((4 * tokens, width), BF))
        scratch += [
            pltpu.VMEM((4, tokens // STEPS, STEPS, width), BF),
            pltpu.SemaphoreType.DMA((4,)),
            pltpu.VMEM((2, wide // TILE, width, TILE), BF),
            pltpu.SemaphoreType.DMA((2, wide // TILE)),
        ]
    here = pl.BlockSpec(memory_space=pl.ANY)
    return pl.pallas_call(
        functools.partial(terms_kernel, first),
        out_shape=outs,
        grid_spec=pltpu.PrefetchScalarGridSpec(
            num_scalar_prefetch=1,
            grid=(1,),
            in_specs=[here, here, here]
            if first
            else [whole(hidden.shape), whole(kv_weight.shape), here],
            out_specs=[whole(x.shape) for x in outs],
            scratch_shapes=scratch,
        ),
        compiler_params=params(),
        cost_estimate=cost(2 * 4 * tokens * width * 2 * wide, [hidden], outs),
        name="projection_terms",
    )(ids, *(map(hbm, (hidden, kv_weight)) if first else (hidden, kv_weight)), after)


def mid_kernel(kkeep, kcame, vkeep, vcame, after, kout, vout):
    del after
    kout[...] = (kkeep[...].astype(F32) + kcame[...].astype(F32)).astype(BF)
    vout[...] = (vkeep[...].astype(F32) + vcame[...].astype(F32)).astype(BF)


def mid_sums(kkeep, kcame, vkeep, vcame, after):
    shape = vkeep.shape
    low = pl.BlockSpec(shape, lambda i: (0, 0))
    high = pl.BlockSpec(shape, lambda i: (1, 0))
    return pl.pallas_call(
        mid_kernel,
        out_shape=[jax.ShapeDtypeStruct(shape, BF)] * 2,
        grid=(1,),
        in_specs=[high, low, low, high, pl.BlockSpec(memory_space=pl.ANY)],
        out_specs=[low, low],
        compiler_params=params(),
        cost_estimate=cost(0, [vkeep] * 6, []),
        name="mid_sums",
    )(kkeep, kcame, vkeep, vcame, after)


def pack_kernel(ids, grad_a, grad_b, after, out, unwritten):
    del ids, after, unwritten
    wide = grad_a.shape[-1]
    out[:, :wide] = grad_a[0, 0].astype(BF)
    out[:, wide:] = grad_b[0, 0].astype(BF)


def chip_kernel(ids, grad_a, grad_b, other, out):
    del ids
    wide = grad_a.shape[-1]
    out[:, :wide] = (grad_a[0, 0] + other[:, :wide].astype(F32)).astype(BF)
    out[:, wide:] = (grad_b[0, 0] + other[:, wide:].astype(F32)).astype(BF)


def grad_half(kernel, name, ids, grad_a, grad_b, flip, rest, rest_specs, more_outs=()):
    rank, wide = grad_a.shape[2], grad_a.shape[3] + grad_b.shape[3]

    def spec(x):
        return pl.BlockSpec((1, 1) + x.shape[2:], lambda i, ids: (0, ids[2] ^ flip, 0, 0))

    out = jax.ShapeDtypeStruct((rank, wide), BF)
    return pl.pallas_call(
        kernel,
        out_shape=[out, *more_outs],
        grid_spec=pltpu.PrefetchScalarGridSpec(
            num_scalar_prefetch=1,
            grid=(1,),
            in_specs=[spec(grad_a), spec(grad_b), *rest_specs],
            out_specs=[whole(out.shape)] + [pl.BlockSpec(memory_space=pl.ANY)] * len(more_outs),
        ),
        compiler_params=params(),
        cost_estimate=cost(0, [out] * 4, []),
        name=name,
    )(ids, hbm(grad_a), hbm(grad_b), *rest)


def small_call(kernel, name, ids, args, outs, after=(), scratch=(), copied=0):
    count = len(args)

    def body(ids, *refs):
        kernel(ids, *refs[:count], *refs[count + len(after) :])

    return pl.pallas_call(
        body,
        out_shape=outs,
        grid_spec=pltpu.PrefetchScalarGridSpec(
            num_scalar_prefetch=1,
            grid=(1,),
            in_specs=[whole(x.shape) for x in args]
            + [pl.BlockSpec(memory_space=pl.ANY)] * len(after),
            out_specs=[pl.BlockSpec(memory_space=pltpu.HBM)] * copied
            + [whole(x.shape) for x in outs[copied:]],
            scratch_shapes=list(scratch),
        ),
        compiler_params=params(),
        cost_estimate=cost(0, args, []),
        name=name,
    )(ids, *args, *after)


def core_flip(x, count):
    return lax.ppermute(x, "dp", [(i, i ^ 1) for i in range(count)])


def plus_kernel(a, b, *rest):
    rest[-1][...] = (a[...].astype(F32) + b[...].astype(F32)).astype(BF)


def plus(a, b, *after):
    out = jax.ShapeDtypeStruct(a.shape, BF)
    return pl.pallas_call(
        plus_kernel,
        out_shape=out,
        grid=(1,),
        in_specs=[whole(a.shape)] * 2 + [pl.BlockSpec(memory_space=pl.ANY)] * len(after),
        out_specs=whole(a.shape),
        compiler_params=params(),
        cost_estimate=cost(0, [a, b], [out]),
        name="plus",
    )(a, b, *after)


def along_line(x, d, count):
    return lax.ppermute(x, "dp", [(i, i ^ (2 * d)) for i in range(count)])


TOP = 2 * R


def update_kernel(rates, ids, half, other, factor_a, factor_b, x, out_a, out_b, *rest):
    *sends, a, new_a, new_b, sems = rest
    copies = [
        pltpu.make_async_copy(new_a, out_a, sems.at[0]),
        pltpu.make_async_copy(new_b, out_b, sems.at[1]),
    ]
    wide = factor_a.shape[-1]
    for index, part in ((ids[2], half), (ids[2] ^ 1, other)):
        new_a[index] = factor_a[index] - rates[0] * part[:, :wide].astype(F32)
        new_b[index] = factor_b[index] - rates[1] * part[:, wide:].astype(F32)
    for copy in copies:
        copy.start()
    for p in range(2):
        a[p * R : (p + 1) * R] = new_a[p].astype(BF)
    a[TOP:] = jnp.zeros((TILE - TOP, wide), BF)
    tokens = x.shape[0] // 4

    def multiply(*accs):
        steps = wide // TILE

        def push(k):
            for unit in range(2):
                tile = a[:, k * TILE : (k + 1) * TILE]
                pltpu.matmul_push_rhs(tile, k % 2, unit, transpose=True)

        push(0)
        for k in range(steps):
            if k + 1 < steps:
                push(k + 1)
            for r in range(4):
                rows = x[r * tokens : (r + 1) * tokens, k * TILE : (k + 1) * TILE]
                staged = k % 2 if r < 2 else None
                pltpu.matmul_acc_lhs(accs[r], rows, load_staged_rhs=staged)
        for r, send in enumerate(sends):
            u = (0.25 * pltpu.matmul_pop(accs[r])[:, :TOP]).astype(BF)
            for p in range(2):
                send[p * R : (p + 1) * R, :] = new_b[p].astype(BF)
            send[TOP:, :TOP] = u[:TOP]
            send[TOP:tokens, TOP:] = u[TOP:]
            send[tokens:, TOP:] = jnp.zeros((2 * TOP - tokens, TOP), BF)

    pl.run_scoped(multiply, *[pltpu.ACC(r % 2)((tokens, TILE), F32) for r in range(4)])
    for copy in copies:
        copy.wait()


def updated(ids, half, other, factor_a, factor_b, x, dp, after):
    rates = (2.0 / math.sqrt(dp * D), 2.0 / math.sqrt(dp * R))
    outs = [pltpu.HBM(f.shape, F32) for f in (factor_a, factor_b)]
    outs += [jax.ShapeDtypeStruct((2 * TOP, 2 * TOP), BF)] * 4
    return small_call(
        functools.partial(update_kernel, rates),
        "update_factors",
        ids,
        (half, other, factor_a, factor_b, x),
        outs,
        (after,),
        [
            pltpu.VMEM((TILE, factor_a.shape[-1]), BF),
            pltpu.VMEM(factor_a.shape, F32),
            pltpu.VMEM(factor_b.shape, F32),
            pltpu.SemaphoreType.DMA((2,)),
        ],
        2,
    )


def attend_kernel(ids, first, lengths, *refs):
    q, cache_k, cache_v, k0, k1, k2, v0, v1, v2, *ub, cosine, sine = refs[:15]
    out = refs[-1]
    rows, slots, _ = cache_k.shape
    tokens = rows * STEPS
    u_top = sum(x[TOP:, :TOP].astype(F32) for x in ub)
    u_low = sum(x[TOP:tokens, TOP:].astype(F32) for x in ub)
    u = jnp.concatenate([u_top, u_low], axis=0).astype(BF)
    rel = ids[0] ^ (first[0] + pl.program_id(0))
    low = jnp.where(rel == 0, ub[0][:TOP].astype(F32), ub[1][:TOP].astype(F32))
    high = jnp.where(rel == 2, ub[2][:TOP].astype(F32), ub[3][:TOP].astype(F32))
    b = jnp.where(rel < 2, low, high).astype(BF)
    k = k0[...].astype(F32) + k1[...].astype(F32) + k2[...].astype(F32) + dot(u[:, :R], b[:R])
    v = v0[...].astype(F32) + v1[...].astype(F32) + v2[...].astype(F32) + dot(u[:, R:], b[R:])
    v = v.astype(BF)
    keys = []
    for n in range(HEADS_STEP):
        key = k[:, n * HD : (n + 1) * HD]
        scale = lax.rsqrt(jnp.sum(key * key, axis=-1, keepdims=True) * (1.0 / HD) + 1e-06)
        key = scale * (key * cosine[...] + pltpu.roll(key, HD // 2, 1) * sine[...])
        keys.append(key.astype(BF))
    n_q, n_c = GROUP * STEPS, GROUP * slots
    shape = (n_q, n_c + n_q)
    here = lax.broadcasted_iota(jnp.int32, shape, 0)
    col = lax.broadcasted_iota(jnp.int32, shape, 1)
    fresh = col - n_c
    cached = (col < n_c) & (here // STEPS == col // slots)
    new = (col >= n_c) & (here // STEPS == fresh // STEPS) & (fresh % STEPS <= here % STEPS)
    bias_here = jnp.where(cached | new, 0.0, -1e30)
    col = lax.broadcasted_iota(jnp.int32, (1, n_c + n_q), 1)
    ones = jnp.ones((n_c + n_q, HD), BF)
    factor = math.log2(math.e) * HD**-0.5
    heads = QH // KVH
    blocks = rows // GROUP
    query = q[...].reshape(tokens, HEADS_STEP * heads * HD)

    def block(n, g, cache, fresh):
        old = cache[g * GROUP : (g + 1) * GROUP, :, n * HD : (n + 1) * HD].reshape(n_c, HD)
        return jnp.concatenate([old, fresh[g * n_q : (g + 1) * n_q]], axis=0)

    every = [(n, g) for n in range(HEADS_STEP) for g in range(blocks)]
    scores = []
    for n, g in every:
        part = [query[g * n_q : (g + 1) * n_q, h * HD : (h + 1) * HD] for h in range(n * heads, (n + 1) * heads)]
        scores.append(dot_t(jnp.concatenate(part, axis=0), block(n, g, cache_k, keys[n])))
    biases = []
    for g in range(blocks):
        filled = jnp.full(col.shape, lengths[g * GROUP], jnp.int32)
        for i in range(1, GROUP):
            filled = jnp.where(col // slots == i, lengths[g * GROUP + i], filled)
        bias = jnp.where((col >= n_c) | (col % slots < filled), 0.0, -1e30) + bias_here
        biases.append(jnp.concatenate([bias] * heads, axis=0))
    weights = []
    for (n, g), s in zip(every, scores):
        s = s * factor + biases[g]
        top = jnp.max(s, axis=-1, keepdims=True)
        weights.append(jnp.exp2(s - top).astype(BF))
    results = []
    for (n, g), w in zip(every, weights):
        here_v = block(n, g, cache_v, v[:, n * HD : (n + 1) * HD])
        r = dot(w, jnp.concatenate([here_v, ones], axis=1))
        total = r[:, HD:]
        inverse = pl.reciprocal(total, approx=True)
        inverse = inverse * (2.0 - total * inverse)
        results.append((r[:, :HD] * inverse).astype(BF))
    for n in range(HEADS_STEP):
        for h in range(heads):
            part = [r[h * n_q : (h + 1) * n_q] for r in results[n * blocks : (n + 1) * blocks]]
            at = (n * heads + h) * HD
            out[:, :, at : at + HD] = jnp.concatenate(part, axis=0).reshape(rows, STEPS, HD)


def attend_chunk(
    ids, lengths, start, count, queries, cache_keys, cache_values, terms, ub, tables, before
):
    rows, slots, _ = cache_keys.shape
    tokens = rows * STEPS
    heads = QH // KVH
    args = [queries, cache_keys, cache_values, *terms, *ub, *tables]
    assert start % HEADS_STEP == 0 and count % HEADS_STEP == 0
    first = jnp.full((1,), start // HEADS_STEP, jnp.int32)
    size = HEADS_STEP * HD
    part = pl.BlockSpec((tokens, size), lambda i, *_: (0, i))
    low = pl.BlockSpec((tokens, size), lambda i, *_: (1, i))
    cache = pl.BlockSpec((rows, slots, size), lambda i, _, first, *__: (0, 0, first[0] + i))
    wide = pl.BlockSpec((rows, STEPS, heads * size), lambda i, _, first, *__: (0, 0, first[0] + i))
    specs = [wide, cache, cache, part, low, part, part, part, part]
    specs += [whole(x.shape) for x in (*ub, *tables)]
    args.append(before)
    specs.append(pl.BlockSpec(memory_space=pl.ANY))
    return pl.pallas_call(
        attend_kernel,
        out_shape=jax.ShapeDtypeStruct(queries.shape, BF),
        grid_spec=pltpu.PrefetchScalarGridSpec(
            num_scalar_prefetch=3, grid=(count // HEADS_STEP,), in_specs=specs, out_specs=wide
        ),
        input_output_aliases={len(args) + 2: 0},
        compiler_params=params(),
        cost_estimate=cost(count * 4 * 10**9, args, []),
        name="attend_chunk",
    )(ids, first, lengths, *args)


def rotary_tables(key_gain, positions):
    half = HD // 2
    place = positions[:, None] + jnp.arange(STEPS, dtype=jnp.int32)[None, :]
    freq = jnp.exp(-math.log(1000000.0) * (jnp.arange(half, dtype=F32) * 2.0 / HD))
    angle = place.reshape(-1).astype(F32)[:, None] * jnp.concatenate([freq, freq])
    turned = jnp.concatenate([-key_gain[half:], key_gain[:half]])
    return jnp.cos(angle) * key_gain, jnp.sin(angle) * turned


def across(x, r):
    return lax.ppermute(x, "tensor", [(i, i ^ r) for i in range(4)])


def square(
    hidden_in,
    kv_weight,
    factor_a,
    factor_b,
    grad_a,
    grad_b,
    key_gain,
    queries,
    cache_keys,
    cache_values,
    cache_lengths,
    positions,
):
    tokens = cache_keys.shape[0] * STEPS
    count_dp = lax.axis_size("dp")
    dp = lax.axis_index("dp")
    ids = jnp.stack([lax.axis_index("tensor"), dp // 2, dp % 2]).astype(jnp.int32)
    tables = rotary_tables(key_gain, positions)

    x, *first = projection_terms(ids, hidden_in, kv_weight, CHUNKS[0], tokens, ids)
    here = pl.BlockSpec(memory_space=pl.ANY)
    packed, attended = grad_half(
        pack_kernel,
        "pack_grads",
        ids,
        grad_a,
        grad_b,
        1,
        [first[0]],
        [here],
        [jax.ShapeDtypeStruct(queries.shape, BF)],
    )
    other = core_flip(packed, count_dp)
    (half,) = grad_half(
        chip_kernel, "chip_grads", ids, grad_a, grad_b, 0, [other], [whole(other.shape)]
    )
    def first_exchange(term, after):
        ksend, kkeep, vsend, vkeep0, vkeep1 = term
        kcame, vcame = across(ksend, 1), across(vsend, 2)
        mids = mid_sums(kkeep, kcame, vkeep1, vcame, after)
        return mids, (kkeep, kcame, vkeep0, vcame)

    def second_exchange(mids, parts):
        kkeep, kcame, vkeep0, vcame = parts
        return kkeep, kcame, across(mids[0], 2), vkeep0, vcame, across(mids[1], 1)

    second = projection_terms(ids, x, kv_weight, CHUNKS[1], tokens, half)
    step, after = 1, second[:1]
    while 2 * step < count_dp:
        half = plus(half, along_line(half, step, count_dp), *after)
        step *= 2
        if step == 2:
            mids, parts = first_exchange(first, half)
            after = (mids[0], tables[0])
    if step == 1:
        mids, parts = first_exchange(first, half)
    other = core_flip(half, count_dp)
    first = second_exchange(mids, parts)
    new_a, new_b, *sends = updated(
        ids, half, other, factor_a, factor_b, x, count_dp, mids[0]
    )
    ub = [sends[0]] + [across(sends[r], r) for r in (1, 2, 3)]
    second = second_exchange(*first_exchange(second, sends[0]))
    for start, count, came in ((0, CHUNKS[0], first), (CHUNKS[0], CHUNKS[1], second)):
        attended = attend_chunk(
            ids,
            cache_lengths,
            start,
            count,
            queries,
            cache_keys,
            cache_values,
            came,
            ub,
            tables,
            attended,
        )
    return attended, new_a, new_b


def solution(mesh):
    fits = mesh.shape["tensor"] == 4 and mesh.shape["dp"] in (2, 4, 8)
    return jax.shard_map(
        square if fits else general,
        mesh=mesh,
        in_specs=(
            P("dp", None, "tensor"),
            P(None, "tensor", None),
            P(None, None, "tensor"),
            P(None, None, "tensor"),
            P("dp", None, None, "tensor"),
            P("dp", None, None, "tensor"),
            P(),
            P(("dp", "tensor"), None, None),
            P(("dp", "tensor"), None, None),
            P(("dp", "tensor"), None, None),
            P(("dp", "tensor")),
            P(("dp", "tensor")),
        ),
        out_specs=(
            P(("dp", "tensor"), None, None),
            P(None, None, "tensor"),
            P(None, None, "tensor"),
        ),
        check_vma=False,
    )
```

```python
import functools
import math

import jax
import jax.numpy as jnp
from jax import lax
from jax.experimental import pallas as pl
from jax.experimental.pallas import tpu as pltpu
from jax.sharding import PartitionSpec as P

D = 5120
KVH = 8
HD = 128
QH = 32
R = 64
STEPS = 4
BF = jnp.bfloat16
F32 = jnp.float32
VMEM_LIMIT = 16 * 1024 * 1024


def normed_rotated(keys, gain, position):
    scale = lax.rsqrt(jnp.mean(keys * keys, axis=-1, keepdims=True) + 1e-06)
    keys = keys * scale * gain
    half = keys.shape[-1] // 2
    freq = jnp.exp(
        -math.log(1000000.0) * (jnp.arange(half, dtype=jnp.float32) * 2.0 / keys.shape[-1])
    )
    angle = position.astype(jnp.float32)[..., None] * freq
    cosine = jnp.concatenate([jnp.cos(angle), jnp.cos(angle)], axis=-1)[..., None, :]
    sine = jnp.concatenate([jnp.sin(angle), jnp.sin(angle)], axis=-1)[..., None, :]
    turned = jnp.concatenate([-keys[..., half:], keys[..., :half]], axis=-1)
    return keys * cosine + turned * sine


def attend(queries, cache_keys, cache_values, new_keys, new_values, lengths):
    rows, steps, width = queries.shape
    slots = cache_keys.shape[1]
    slot = jnp.arange(slots, dtype=jnp.int32)
    for step in range(steps):
        hit = (slot[None, :] == lengths[:, None] + step)[:, :, None]
        cache_keys = jnp.where(hit, new_keys[:, step][:, None, :], cache_keys)
        cache_values = jnp.where(hit, new_values[:, step][:, None, :], cache_values)
    groups = QH // KVH
    query_five = queries.reshape(rows, steps, KVH, groups, HD)
    key_four = cache_keys.reshape(rows, slots, KVH, HD)
    value_four = cache_values.reshape(rows, slots, KVH, HD)
    scores = jnp.einsum(
        "rtkgd,rckd->rtkgc", query_five, key_four, preferred_element_type=jnp.float32
    ) * HD ** (-0.5)
    limit = lengths[:, None] + jnp.arange(steps, dtype=jnp.int32)[None, :]
    valid = (slot[None, None, :] <= limit[:, :, None])[:, :, None, None, :]
    scores = jnp.where(valid, scores, jnp.float32(-1e30))
    top = jnp.max(scores, axis=-1, keepdims=True)
    expo = jnp.exp(scores - top)
    weights = (expo / jnp.sum(expo, axis=-1, keepdims=True)).astype(jnp.bfloat16)
    result = jnp.einsum(
        "rtkgc,rckd->rtkgd", weights, value_four, preferred_element_type=jnp.float32
    )
    return result.reshape(rows, steps, width).astype(jnp.bfloat16)


def general(
    hidden_in,
    kv_weight,
    factor_a,
    factor_b,
    grad_a,
    grad_b,
    key_gain,
    queries,
    cache_keys,
    cache_values,
    cache_lengths,
    positions,
):
    groups_dp = lax.axis_size("dp")
    rate_a = 2.0 / math.sqrt(groups_dp * D)
    rate_b = 2.0 / math.sqrt(groups_dp * R)
    sum_a, sum_b = (
        lax.psum(grad_a[0].astype(jnp.bfloat16), "dp").astype(jnp.float32),
        lax.psum(grad_b[0].astype(jnp.bfloat16), "dp").astype(jnp.float32),
    )
    new_a = factor_a - rate_a * sum_a
    new_b = factor_b - rate_b * sum_b
    full_b = lax.all_gather(new_b.astype(jnp.bfloat16), "tensor", axis=2, tiled=True).astype(
        new_b.dtype
    )
    delta = jnp.einsum("prd,prk->pdk", new_a, full_b, precision=lax.Precision.HIGHEST)
    merged = (kv_weight.astype(jnp.float32) + 0.25 * delta).astype(jnp.bfloat16)
    joined = jnp.concatenate([merged[0], merged[1]], axis=1)
    rows_here = hidden_in.shape[0] // lax.axis_size("tensor")
    pieces = []
    for step in range(STEPS):
        term = jnp.dot(hidden_in[:, step, :], joined, preferred_element_type=jnp.float32)
        pieces.append(
            lax.psum_scatter(
                term.astype(jnp.bfloat16), "tensor", scatter_dimension=0, tiled=True
            ).astype(jnp.float32)
        )
    projected = jnp.stack(pieces, axis=1)
    kv_width = KVH * HD
    place = positions[:, None] + jnp.arange(STEPS, dtype=jnp.int32)[None, :]
    keys = normed_rotated(
        projected[..., :kv_width].reshape(rows_here, STEPS, KVH, HD), key_gain, place
    )
    new_keys = keys.reshape(rows_here, STEPS, kv_width).astype(jnp.bfloat16)
    new_values = projected[..., kv_width:].astype(jnp.bfloat16)
    attended = attend(queries, cache_keys, cache_values, new_keys, new_values, cache_lengths)
    return (attended, new_a, new_b)


CHUNKS = (4, 4)
GROUP = 12
HEADS_STEP = 2


def params(limit=VMEM_LIMIT):
    return pltpu.CompilerParams(vmem_limit_bytes=limit)


def dot(a, b):
    return jnp.dot(a, b, preferred_element_type=F32)


def dot_t(a, b):
    return lax.dot_general(a, b, (((1,), (1,)), ((), ())), preferred_element_type=F32)


def whole(shape):
    return pl.BlockSpec(shape, lambda i, *_: (0,) * len(shape))


def hbm(x):
    return pltpu.with_memory_space_constraint(x, pltpu.HBM)


TILE = 256


def multiply_terms(x, w, outs, ready):
    ksend, kkeep, vsend, vkeep0, vkeep1 = outs
    tokens = x.shape[0] // 4
    steps = x.shape[1] // TILE
    low, high = slice(0, tokens), slice(tokens, 2 * tokens)

    def multiply(*accs):
        accs_k, accs_v = accs[:4], accs[4:]

        @pl.loop(0, w.shape[1])
        def _(i):
            ready(i)

            def push(k):
                for p in range(2):
                    pltpu.matmul_push_rhs(w[p, i, k * TILE : (k + 1) * TILE, :], k % 2, p)

            push(0)
            for k in range(steps):
                if k + 1 < steps:
                    push(k + 1)
                for r in range(4):
                    rows = x[r * tokens : (r + 1) * tokens, k * TILE : (k + 1) * TILE]
                    staged = k % 2 if r == 0 else None
                    pltpu.matmul_acc_lhs(accs_k[r], rows, load_staged_rhs=staged)
                    pltpu.matmul_acc_lhs(accs_v[r], rows, load_staged_rhs=staged)
            at = pl.ds(pl.multiple_of(i * TILE, TILE), TILE)
            kkeep[low, at] = pltpu.matmul_pop(accs_k[0]).astype(BF)
            vkeep0[:, at] = pltpu.matmul_pop(accs_v[0]).astype(BF)
            ksend[high, at] = pltpu.matmul_pop(accs_k[1]).astype(BF)
            vkeep1[:, at] = pltpu.matmul_pop(accs_v[1]).astype(BF)
            kkeep[high, at] = pltpu.matmul_pop(accs_k[2]).astype(BF)
            vsend[low, at] = pltpu.matmul_pop(accs_v[2]).astype(BF)
            ksend[low, at] = pltpu.matmul_pop(accs_k[3]).astype(BF)
            vsend[high, at] = pltpu.matmul_pop(accs_v[3]).astype(BF)

    pl.run_scoped(
        multiply, *[pltpu.ACC(unit)((tokens, TILE), F32) for unit in range(2) for _ in range(4)]
    )


def first_kernel(ids, hidden, weight, grad_a, grad_b, *rest):
    x, *outs = rest[:6]
    send, own, later, _ = rest[6:10]
    held, w, held_a, held_b, hidden_sems, sems, later_sems, grad_sems = rest[10:]
    tokens = x.shape[0] // 4
    rows = tokens // STEPS

    def hidden_copy(r):
        at = pl.ds((ids[0] ^ r) * rows, rows)
        return pltpu.make_async_copy(hidden.at[at], held.at[r], hidden_sems.at[r])

    def weight_copy(p, i):
        at = pl.ds(i * TILE, TILE)
        return pltpu.make_async_copy(weight.at[p, :, at], w.at[p, i], sems.at[p, i])

    def later_copy(p, i):
        at = pl.ds((w.shape[1] + i) * TILE, TILE)
        return pltpu.make_async_copy(weight.at[p, :, at], later.at[p, i], later_sems.at[p, i])

    others = [
        pltpu.make_async_copy(grad_a.at[0], held_a, grad_sems.at[0]),
        pltpu.make_async_copy(grad_b.at[0], held_b, grad_sems.at[1]),
    ]
    others += [later_copy(p, i) for i in range(later.shape[1]) for p in range(2)]
    for r in range(4):
        hidden_copy(r).start()
    for i in range(w.shape[1]):
        for p in range(2):
            weight_copy(p, i).start()
    for r in range(4):
        hidden_copy(r).wait()
        x[r * tokens : (r + 1) * tokens] = held[r].reshape(tokens, x.shape[1])
    for copy in others:
        copy.start()

    def ready(i):
        for p in range(2):
            weight_copy(p, i).wait()

    multiply_terms(x, w, outs, ready)
    for copy in others:
        copy.wait()
    wide = grad_a.shape[-1]
    for out, p in ((send, ids[2] ^ 1), (own, ids[2])):
        out[:, :wide] = held_a[p].astype(BF)
        out[:, wide:] = held_b[p].astype(BF)


def later_kernel(x, w, after, *outs):
    del after
    multiply_terms(x, w, outs, lambda i: None)


def term_shapes(tokens, count):
    return [jax.ShapeDtypeStruct((n * tokens, count * HD), BF) for n in (2, 2, 2, 1, 1)]


def first_terms(ids, hidden, kv_weight, grad_a, grad_b, queries, tokens):
    width = hidden.shape[2]
    rank, wide = grad_a.shape[2], grad_a.shape[3] + grad_b.shape[3]
    here = pl.BlockSpec(memory_space=pl.ANY)
    outs = [jax.ShapeDtypeStruct((4 * tokens, width), BF), *term_shapes(tokens, CHUNKS[0])]
    outs += [jax.ShapeDtypeStruct((rank, wide), BF)] * 2
    tiles = [count * HD // TILE for count in CHUNKS]
    outs.append(pltpu.VMEM((2, tiles[1], width, TILE), BF))
    specs = [whole(x.shape) for x in outs] + [here]
    outs.append(jax.ShapeDtypeStruct(queries.shape, BF))
    return pl.pallas_call(
        first_kernel,
        out_shape=outs,
        grid_spec=pltpu.PrefetchScalarGridSpec(
            num_scalar_prefetch=1,
            grid=(1,),
            in_specs=[here] * 4,
            out_specs=specs,
            scratch_shapes=[
                pltpu.VMEM((4, tokens // STEPS, STEPS, width), BF),
                pltpu.VMEM((2, tiles[0], width, TILE), BF),
                pltpu.VMEM(grad_a.shape[1:], F32),
                pltpu.VMEM(grad_b.shape[1:], F32),
                pltpu.SemaphoreType.DMA((4,)),
                pltpu.SemaphoreType.DMA((2, tiles[0])),
                pltpu.SemaphoreType.DMA((2, tiles[1])),
                pltpu.SemaphoreType.DMA((2,)),
            ],
        ),
        compiler_params=params(),
        name="first_terms",
    )(ids, *map(hbm, (hidden, kv_weight, grad_a, grad_b)))


def later_terms(x, w, after):
    outs = term_shapes(x.shape[0] // 4, CHUNKS[1])
    return pl.pallas_call(
        later_kernel,
        out_shape=outs,
        grid=(1,),
        in_specs=[whole(x.shape), whole(w.shape), pl.BlockSpec(memory_space=pl.ANY)],
        out_specs=[whole(out.shape) for out in outs],
        compiler_params=params(),
        name="later_terms",
    )(x, w, after)


def mid_kernel(kkeep, kcame, vkeep, vcame, after, kout, vout):
    del after
    kout[...] = (kkeep[...].astype(F32) + kcame[...].astype(F32)).astype(BF)
    vout[...] = (vkeep[...].astype(F32) + vcame[...].astype(F32)).astype(BF)


def mid_sums(kkeep, kcame, vkeep, vcame, after):
    shape = vkeep.shape
    low = pl.BlockSpec(shape, lambda i: (0, 0))
    high = pl.BlockSpec(shape, lambda i: (1, 0))
    return pl.pallas_call(
        mid_kernel,
        out_shape=[jax.ShapeDtypeStruct(shape, BF)] * 2,
        grid=(1,),
        in_specs=[high, low, low, high, pl.BlockSpec(memory_space=pl.ANY)],
        out_specs=[low, low],
        compiler_params=params(),
        name="mid_sums",
    )(kkeep, kcame, vkeep, vcame, after)


def small_call(kernel, name, ids, args, outs, after=(), scratch=(), copied=0):
    count = len(args)

    def body(ids, *refs):
        kernel(ids, *refs[:count], *refs[count + len(after) :])

    return pl.pallas_call(
        body,
        out_shape=outs,
        grid_spec=pltpu.PrefetchScalarGridSpec(
            num_scalar_prefetch=1,
            grid=(1,),
            in_specs=[whole(x.shape) for x in args]
            + [pl.BlockSpec(memory_space=pl.ANY)] * len(after),
            out_specs=[pl.BlockSpec(memory_space=pltpu.HBM)] * copied
            + [whole(x.shape) for x in outs[copied:]],
            scratch_shapes=list(scratch),
        ),
        compiler_params=params(),
        name=name,
    )(ids, *args, *after)


def core_flip(x, count):
    return lax.ppermute(x, "dp", [(i, i ^ 1) for i in range(count)])


def plus_kernel(a, b, *rest):
    rest[-1][...] = (a[...].astype(F32) + b[...].astype(F32)).astype(BF)


def plus(a, b, *after):
    out = jax.ShapeDtypeStruct(a.shape, BF)
    return pl.pallas_call(
        plus_kernel,
        out_shape=out,
        grid=(1,),
        in_specs=[whole(a.shape)] * 2 + [pl.BlockSpec(memory_space=pl.ANY)] * len(after),
        out_specs=whole(a.shape),
        compiler_params=params(),
        name="plus",
    )(a, b, *after)


def along_line(x, d, count):
    return lax.ppermute(x, "dp", [(i, i ^ (2 * d)) for i in range(count)])


TOP = 2 * R


def update_kernel(rates, ids, half, other, factor_a, factor_b, x, out_a, out_b, *rest):
    *sends, a, new_a, new_b, sems = rest
    copies = [
        pltpu.make_async_copy(new_a, out_a, sems.at[0]),
        pltpu.make_async_copy(new_b, out_b, sems.at[1]),
    ]
    wide = factor_a.shape[-1]
    for index, part in ((ids[2], half), (ids[2] ^ 1, other)):
        new_a[index] = factor_a[index] - rates[0] * part[:, :wide].astype(F32)
        new_b[index] = factor_b[index] - rates[1] * part[:, wide:].astype(F32)
    for copy in copies:
        copy.start()
    for p in range(2):
        a[p * R : (p + 1) * R] = new_a[p].astype(BF)
    a[TOP:] = jnp.zeros((TILE - TOP, wide), BF)
    tokens = x.shape[0] // 4

    def multiply(*accs):
        steps = wide // TILE

        def push(k):
            for unit in range(2):
                tile = a[:, k * TILE : (k + 1) * TILE]
                pltpu.matmul_push_rhs(tile, k % 2, unit, transpose=True)

        push(0)
        for k in range(steps):
            if k + 1 < steps:
                push(k + 1)
            for r in range(4):
                rows = x[r * tokens : (r + 1) * tokens, k * TILE : (k + 1) * TILE]
                staged = k % 2 if r < 2 else None
                pltpu.matmul_acc_lhs(accs[r], rows, load_staged_rhs=staged)
        for r, send in enumerate(sends):
            u = (0.25 * pltpu.matmul_pop(accs[r])[:, :TOP]).astype(BF)
            for p in range(2):
                send[p * R : (p + 1) * R, :] = new_b[p].astype(BF)
            send[TOP:, :TOP] = u[:TOP]
            send[TOP:tokens, TOP:] = u[TOP:]
            send[tokens:, TOP:] = jnp.zeros((2 * TOP - tokens, TOP), BF)

    pl.run_scoped(multiply, *[pltpu.ACC(r % 2)((tokens, TILE), F32) for r in range(4)])
    for copy in copies:
        copy.wait()


def updated(ids, half, other, factor_a, factor_b, x, dp, after):
    rates = (2.0 / math.sqrt(dp * D), 2.0 / math.sqrt(dp * R))
    outs = [pltpu.HBM(f.shape, F32) for f in (factor_a, factor_b)]
    outs += [jax.ShapeDtypeStruct((2 * TOP, 2 * TOP), BF)] * 4
    return small_call(
        functools.partial(update_kernel, rates),
        "update_factors",
        ids,
        (half, other, factor_a, factor_b, x),
        outs,
        (after,),
        [
            pltpu.VMEM((TILE, factor_a.shape[-1]), BF),
            pltpu.VMEM(factor_a.shape, F32),
            pltpu.VMEM(factor_b.shape, F32),
            pltpu.SemaphoreType.DMA((2,)),
        ],
        2,
    )


def attend_kernel(ids, first, lengths, *refs):
    q, cache_k, cache_v, k0, k1, k2, v0, v1, v2, *ub, cosine, sine = refs[:15]
    out = refs[-1]
    rows, slots, _ = cache_k.shape
    tokens = rows * STEPS
    u_top = sum(x[TOP:, :TOP].astype(F32) for x in ub)
    u_low = sum(x[TOP:tokens, TOP:].astype(F32) for x in ub)
    u = jnp.concatenate([u_top, u_low], axis=0).astype(BF)
    rel = ids[0] ^ (first[0] + pl.program_id(0))
    low = jnp.where(rel == 0, ub[0][:TOP].astype(F32), ub[1][:TOP].astype(F32))
    high = jnp.where(rel == 2, ub[2][:TOP].astype(F32), ub[3][:TOP].astype(F32))
    b = jnp.where(rel < 2, low, high).astype(BF)
    k = k0[...].astype(F32) + k1[...].astype(F32) + k2[...].astype(F32) + dot(u[:, :R], b[:R])
    v = v0[...].astype(F32) + v1[...].astype(F32) + v2[...].astype(F32) + dot(u[:, R:], b[R:])
    v = v.astype(BF)
    keys = []
    for n in range(HEADS_STEP):
        key = k[:, n * HD : (n + 1) * HD]
        scale = lax.rsqrt(jnp.sum(key * key, axis=-1, keepdims=True) * (1.0 / HD) + 1e-06)
        key = scale * (key * cosine[...] + pltpu.roll(key, HD // 2, 1) * sine[...])
        keys.append(key.astype(BF))
    n_q, n_c = GROUP * STEPS, GROUP * slots
    shape = (n_q, n_c + n_q)
    here = lax.broadcasted_iota(jnp.int32, shape, 0)
    col = lax.broadcasted_iota(jnp.int32, shape, 1)
    fresh = col - n_c
    cached = (col < n_c) & (here // STEPS == col // slots)
    new = (col >= n_c) & (here // STEPS == fresh // STEPS) & (fresh % STEPS <= here % STEPS)
    bias_here = jnp.where(cached | new, 0.0, -1e30)
    col = lax.broadcasted_iota(jnp.int32, (1, n_c + n_q), 1)
    ones = jnp.ones((n_c + n_q, HD), BF)
    factor = math.log2(math.e) * HD**-0.5
    heads = QH // KVH
    blocks = rows // GROUP
    query = q[...].reshape(tokens, HEADS_STEP * heads * HD)

    def block(n, g, cache, fresh):
        old = cache[g * GROUP : (g + 1) * GROUP, :, n * HD : (n + 1) * HD].reshape(n_c, HD)
        return jnp.concatenate([old, fresh[g * n_q : (g + 1) * n_q]], axis=0)

    every = [(n, g) for n in range(HEADS_STEP) for g in range(blocks)]
    scores = []
    for n, g in every:
        part = [query[g * n_q : (g + 1) * n_q, h * HD : (h + 1) * HD] for h in range(n * heads, (n + 1) * heads)]
        scores.append(dot_t(jnp.concatenate(part, axis=0), block(n, g, cache_k, keys[n])))
    biases = []
    for g in range(blocks):
        filled = jnp.full(col.shape, lengths[g * GROUP], jnp.int32)
        for i in range(1, GROUP):
            filled = jnp.where(col // slots == i, lengths[g * GROUP + i], filled)
        bias = jnp.where((col >= n_c) | (col % slots < filled), 0.0, -1e30) + bias_here
        biases.append(jnp.concatenate([bias] * heads, axis=0))
    weights = []
    for (n, g), s in zip(every, scores):
        s = s * factor + biases[g]
        top = jnp.max(s, axis=-1, keepdims=True)
        weights.append(jnp.exp2(s - top).astype(BF))
    results = []
    for (n, g), w in zip(every, weights):
        here_v = block(n, g, cache_v, v[:, n * HD : (n + 1) * HD])
        r = dot(w, jnp.concatenate([here_v, ones], axis=1))
        total = r[:, HD:]
        inverse = pl.reciprocal(total, approx=True)
        inverse = inverse * (2.0 - total * inverse)
        results.append((r[:, :HD] * inverse).astype(BF))
    for n in range(HEADS_STEP):
        for h in range(heads):
            part = [r[h * n_q : (h + 1) * n_q] for r in results[n * blocks : (n + 1) * blocks]]
            at = (n * heads + h) * HD
            out[:, :, at : at + HD] = jnp.concatenate(part, axis=0).reshape(rows, STEPS, HD)


def attend_chunk(
    ids, lengths, start, count, queries, cache_keys, cache_values, terms, ub, tables, before
):
    rows, slots, _ = cache_keys.shape
    tokens = rows * STEPS
    heads = QH // KVH
    args = [*map(hbm, (queries, cache_keys, cache_values)), *terms, *ub, *tables]
    assert start % HEADS_STEP == 0 and count % HEADS_STEP == 0
    first = jnp.full((1,), start // HEADS_STEP, jnp.int32)
    size = HEADS_STEP * HD
    part = pl.BlockSpec((tokens, size), lambda i, *_: (0, i))
    low = pl.BlockSpec((tokens, size), lambda i, *_: (1, i))
    cache = pl.BlockSpec((rows, slots, size), lambda i, _, first, *__: (0, 0, first[0] + i))
    wide = pl.BlockSpec((rows, STEPS, heads * size), lambda i, _, first, *__: (0, 0, first[0] + i))
    specs = [wide, cache, cache, part, low, part, part, part, part]
    specs += [whole(x.shape) for x in (*ub, *tables)]
    args.append(before)
    specs.append(pl.BlockSpec(memory_space=pl.ANY))
    return pl.pallas_call(
        attend_kernel,
        out_shape=jax.ShapeDtypeStruct(queries.shape, BF),
        grid_spec=pltpu.PrefetchScalarGridSpec(
            num_scalar_prefetch=3, grid=(count // HEADS_STEP,), in_specs=specs, out_specs=wide
        ),
        input_output_aliases={len(args) + 2: 0},
        compiler_params=params(),
        name="attend_chunk",
    )(ids, first, lengths, *args)


def rotary_tables(key_gain, positions):
    half = HD // 2
    place = positions[:, None] + jnp.arange(STEPS, dtype=jnp.int32)[None, :]
    freq = jnp.exp(-math.log(1000000.0) * (jnp.arange(half, dtype=F32) * 2.0 / HD))
    angle = place.reshape(-1).astype(F32)[:, None] * jnp.concatenate([freq, freq])
    turned = jnp.concatenate([-key_gain[half:], key_gain[:half]])
    return jnp.cos(angle) * key_gain, jnp.sin(angle) * turned


def across(x, r):
    return lax.ppermute(x, "tensor", [(i, i ^ r) for i in range(4)])


def square(
    hidden_in,
    kv_weight,
    factor_a,
    factor_b,
    grad_a,
    grad_b,
    key_gain,
    queries,
    cache_keys,
    cache_values,
    cache_lengths,
    positions,
):
    tokens = cache_keys.shape[0] * STEPS
    count_dp = lax.axis_size("dp")
    dp = lax.axis_index("dp")
    ids = jnp.stack([lax.axis_index("tensor"), dp // 2, dp % 2]).astype(jnp.int32)
    tables = rotary_tables(key_gain, positions)

    x, *first, packed, own, weights, attended = first_terms(
        ids, hidden_in, kv_weight, grad_a, grad_b, queries, tokens
    )
    half = plus(own, core_flip(packed, count_dp))

    def first_exchange(term, after):
        ksend, kkeep, vsend, vkeep0, vkeep1 = term
        kcame, vcame = across(ksend, 1), across(vsend, 2)
        mids = mid_sums(kkeep, kcame, vkeep1, vcame, after)
        return mids, (kkeep, kcame, vkeep0, vcame)

    def second_exchange(mids, parts):
        kkeep, kcame, vkeep0, vcame = parts
        return kkeep, kcame, across(mids[0], 2), vkeep0, vcame, across(mids[1], 1)

    second = later_terms(x, weights, half)
    step, after = 1, second[:1]
    while 2 * step < count_dp:
        half = plus(half, along_line(half, step, count_dp), *after)
        step *= 2
        if step == 2:
            mids, parts = first_exchange(first, half)
            after = (mids[0], tables[0])
    if step == 1:
        mids, parts = first_exchange(first, half)
    first = second_exchange(mids, parts)
    other = core_flip(half, count_dp)
    mids, parts = first_exchange(second, half)
    second = second_exchange(mids, parts)
    new_a, new_b, *sends = updated(
        ids, half, other, factor_a, factor_b, x, count_dp, mids[0]
    )
    ub = [sends[0]] + [across(sends[r], r) for r in (1, 2, 3)]
    for start, count, came in ((0, CHUNKS[0], first), (CHUNKS[0], CHUNKS[1], second)):
        attended = attend_chunk(
            ids,
            cache_lengths,
            start,
            count,
            queries,
            cache_keys,
            cache_values,
            came,
            ub,
            tables,
            attended,
        )
    return attended, new_a, new_b


def solution(mesh):
    fits = mesh.shape["tensor"] == 4 and mesh.shape["dp"] in (2, 4, 8)
    return jax.shard_map(
        square if fits else general,
        mesh=mesh,
        in_specs=(
            P("dp", None, "tensor"),
            P(None, "tensor", None),
            P(None, None, "tensor"),
            P(None, None, "tensor"),
            P("dp", None, None, "tensor"),
            P("dp", None, None, "tensor"),
            P(),
            P(("dp", "tensor"), None, None),
            P(("dp", "tensor"), None, None),
            P(("dp", "tensor"), None, None),
            P(("dp", "tensor")),
            P(("dp", "tensor")),
        ),
        out_specs=(
            P(("dp", "tensor"), None, None),
            P(None, None, "tensor"),
            P(None, None, "tensor"),
        ),
        check_vma=False,
    )
```

```python
import functools
import math

import jax
import jax.numpy as jnp
from jax import lax
from jax.experimental import pallas as pl
from jax.experimental.pallas import tpu as pltpu
from jax.sharding import PartitionSpec as P

D = 5120
KVH = 8
HD = 128
QH = 32
R = 64
STEPS = 4
BF = jnp.bfloat16
F32 = jnp.float32
MIB = 1024 * 1024


def normed_rotated(keys, gain, position):
    scale = lax.rsqrt(jnp.mean(keys * keys, axis=-1, keepdims=True) + 1e-06)
    keys = keys * scale * gain
    half = keys.shape[-1] // 2
    freq = jnp.exp(
        -math.log(1000000.0) * (jnp.arange(half, dtype=jnp.float32) * 2.0 / keys.shape[-1])
    )
    angle = position.astype(jnp.float32)[..., None] * freq
    cosine = jnp.concatenate([jnp.cos(angle), jnp.cos(angle)], axis=-1)[..., None, :]
    sine = jnp.concatenate([jnp.sin(angle), jnp.sin(angle)], axis=-1)[..., None, :]
    turned = jnp.concatenate([-keys[..., half:], keys[..., :half]], axis=-1)
    return keys * cosine + turned * sine


def attend(queries, cache_keys, cache_values, new_keys, new_values, lengths):
    rows, steps, width = queries.shape
    slots = cache_keys.shape[1]
    slot = jnp.arange(slots, dtype=jnp.int32)
    for step in range(steps):
        hit = (slot[None, :] == lengths[:, None] + step)[:, :, None]
        cache_keys = jnp.where(hit, new_keys[:, step][:, None, :], cache_keys)
        cache_values = jnp.where(hit, new_values[:, step][:, None, :], cache_values)
    groups = QH // KVH
    query_five = queries.reshape(rows, steps, KVH, groups, HD)
    key_four = cache_keys.reshape(rows, slots, KVH, HD)
    value_four = cache_values.reshape(rows, slots, KVH, HD)
    scores = jnp.einsum(
        "rtkgd,rckd->rtkgc", query_five, key_four, preferred_element_type=jnp.float32
    ) * HD ** (-0.5)
    limit = lengths[:, None] + jnp.arange(steps, dtype=jnp.int32)[None, :]
    valid = (slot[None, None, :] <= limit[:, :, None])[:, :, None, None, :]
    scores = jnp.where(valid, scores, jnp.float32(-1e30))
    top = jnp.max(scores, axis=-1, keepdims=True)
    expo = jnp.exp(scores - top)
    weights = (expo / jnp.sum(expo, axis=-1, keepdims=True)).astype(jnp.bfloat16)
    result = jnp.einsum(
        "rtkgc,rckd->rtkgd", weights, value_four, preferred_element_type=jnp.float32
    )
    return result.reshape(rows, steps, width).astype(jnp.bfloat16)


def general(
    hidden_in,
    kv_weight,
    factor_a,
    factor_b,
    grad_a,
    grad_b,
    key_gain,
    queries,
    cache_keys,
    cache_values,
    cache_lengths,
    positions,
):
    groups_dp = lax.axis_size("dp")
    rate_a = 2.0 / math.sqrt(groups_dp * D)
    rate_b = 2.0 / math.sqrt(groups_dp * R)
    sum_a, sum_b = (
        lax.psum(grad_a[0].astype(jnp.bfloat16), "dp").astype(jnp.float32),
        lax.psum(grad_b[0].astype(jnp.bfloat16), "dp").astype(jnp.float32),
    )
    new_a = factor_a - rate_a * sum_a
    new_b = factor_b - rate_b * sum_b
    full_b = lax.all_gather(new_b.astype(jnp.bfloat16), "tensor", axis=2, tiled=True).astype(
        new_b.dtype
    )
    delta = jnp.einsum("prd,prk->pdk", new_a, full_b, precision=lax.Precision.HIGHEST)
    merged = (kv_weight.astype(jnp.float32) + 0.25 * delta).astype(jnp.bfloat16)
    joined = jnp.concatenate([merged[0], merged[1]], axis=1)
    rows_here = hidden_in.shape[0] // lax.axis_size("tensor")
    pieces = []
    for step in range(STEPS):
        term = jnp.dot(hidden_in[:, step, :], joined, preferred_element_type=jnp.float32)
        pieces.append(
            lax.psum_scatter(
                term.astype(jnp.bfloat16), "tensor", scatter_dimension=0, tiled=True
            ).astype(jnp.float32)
        )
    projected = jnp.stack(pieces, axis=1)
    kv_width = KVH * HD
    place = positions[:, None] + jnp.arange(STEPS, dtype=jnp.int32)[None, :]
    keys = normed_rotated(
        projected[..., :kv_width].reshape(rows_here, STEPS, KVH, HD), key_gain, place
    )
    new_keys = keys.reshape(rows_here, STEPS, kv_width).astype(jnp.bfloat16)
    new_values = projected[..., kv_width:].astype(jnp.bfloat16)
    attended = attend(queries, cache_keys, cache_values, new_keys, new_values, cache_lengths)
    return (attended, new_a, new_b)


CHUNKS = (4, 4)
GROUP = 12
HEADS_STEP = 2


def params(mib):
    return pltpu.CompilerParams(vmem_limit_bytes=mib * MIB)


def dot(a, b):
    return jnp.dot(a, b, preferred_element_type=F32)


def dot_t(a, b):
    return lax.dot_general(a, b, (((1,), (1,)), ((), ())), preferred_element_type=F32)


def whole(shape):
    return pl.BlockSpec(shape, lambda i, *_: (0,) * len(shape))


def hbm(x):
    return pltpu.with_memory_space_constraint(x, pltpu.HBM)


TILE = 256


def multiply_terms(x, w, outs, ready):
    ksend, kkeep, vsend, vkeep0, vkeep1 = outs
    tokens = x.shape[0] // 4
    steps = x.shape[1] // TILE
    low, high = slice(0, tokens), slice(tokens, 2 * tokens)

    def multiply(*accs):
        accs_k, accs_v = accs[:4], accs[4:]

        @pl.loop(0, w.shape[1])
        def _(i):
            ready(i)

            def push(k):
                for p in range(2):
                    pltpu.matmul_push_rhs(w[p, i, k * TILE : (k + 1) * TILE, :], k % 2, p)

            push(0)
            for k in range(steps):
                if k + 1 < steps:
                    push(k + 1)
                for r in range(4):
                    rows = x[r * tokens : (r + 1) * tokens, k * TILE : (k + 1) * TILE]
                    staged = k % 2 if r == 0 else None
                    pltpu.matmul_acc_lhs(accs_k[r], rows, load_staged_rhs=staged)
                    pltpu.matmul_acc_lhs(accs_v[r], rows, load_staged_rhs=staged)
            at = pl.ds(pl.multiple_of(i * TILE, TILE), TILE)
            kkeep[low, at] = pltpu.matmul_pop(accs_k[0]).astype(BF)
            vkeep0[:, at] = pltpu.matmul_pop(accs_v[0]).astype(BF)
            ksend[high, at] = pltpu.matmul_pop(accs_k[1]).astype(BF)
            vkeep1[:, at] = pltpu.matmul_pop(accs_v[1]).astype(BF)
            kkeep[high, at] = pltpu.matmul_pop(accs_k[2]).astype(BF)
            vsend[low, at] = pltpu.matmul_pop(accs_v[2]).astype(BF)
            ksend[low, at] = pltpu.matmul_pop(accs_k[3]).astype(BF)
            vsend[high, at] = pltpu.matmul_pop(accs_v[3]).astype(BF)

    pl.run_scoped(
        multiply, *[pltpu.ACC(unit)((tokens, TILE), F32) for unit in range(2) for _ in range(4)]
    )


def first_kernel(ids, hidden, weight, grad_a, grad_b, *rest):
    x, *outs = rest[:6]
    send, own, _ = rest[6:9]
    held, w, held_a, held_b, hidden_sems, sems, grad_sems = rest[9:]
    tokens = x.shape[0] // 4
    rows = tokens // STEPS

    def hidden_copy(r):
        at = pl.ds((ids[0] ^ r) * rows, rows)
        return pltpu.make_async_copy(hidden.at[at], held.at[r], hidden_sems.at[r])

    def weight_copy(p, i):
        at = pl.ds(i * TILE, TILE)
        return pltpu.make_async_copy(weight.at[p, :, at], w.at[p, i], sems.at[p, i])

    others = [
        pltpu.make_async_copy(grad_a.at[0], held_a, grad_sems.at[0]),
        pltpu.make_async_copy(grad_b.at[0], held_b, grad_sems.at[1]),
    ]
    for r in range(4):
        hidden_copy(r).start()
    for i in range(w.shape[1]):
        for p in range(2):
            weight_copy(p, i).start()
    for r in range(4):
        hidden_copy(r).wait()
        x[r * tokens : (r + 1) * tokens] = held[r].reshape(tokens, x.shape[1])
    for copy in others:
        copy.start()

    def ready(i):
        for p in range(2):
            weight_copy(p, i).wait()

    multiply_terms(x, w, outs, ready)
    for copy in others:
        copy.wait()
    wide = grad_a.shape[-1]
    for out, p in ((send, ids[2] ^ 1), (own, ids[2])):
        out[:, :wide] = held_a[p].astype(BF)
        out[:, wide:] = held_b[p].astype(BF)


def later_kernel(x, weight, after, *rest):
    del after
    *outs, w, sems = rest
    base = weight.shape[2] - w.shape[1] * TILE

    def weight_copy(p, i):
        at = pl.ds(base + i * TILE, TILE)
        return pltpu.make_async_copy(weight.at[p, :, at], w.at[p, i], sems.at[p, i])

    for i in range(w.shape[1]):
        for p in range(2):
            weight_copy(p, i).start()

    def ready(i):
        for p in range(2):
            weight_copy(p, i).wait()

    multiply_terms(x, w, outs, ready)


def term_shapes(tokens, count):
    return [jax.ShapeDtypeStruct((n * tokens, count * HD), BF) for n in (2, 2, 2, 1, 1)]


def first_terms(ids, hidden, kv_weight, grad_a, grad_b, queries, tokens):
    width = hidden.shape[2]
    rank, wide = grad_a.shape[2], grad_a.shape[3] + grad_b.shape[3]
    here = pl.BlockSpec(memory_space=pl.ANY)
    outs = [jax.ShapeDtypeStruct((4 * tokens, width), BF), *term_shapes(tokens, CHUNKS[0])]
    outs += [jax.ShapeDtypeStruct((rank, wide), BF)] * 2
    tiles = CHUNKS[0] * HD // TILE
    specs = [whole(x.shape) for x in outs] + [here]
    outs.append(jax.ShapeDtypeStruct(queries.shape, BF))
    return pl.pallas_call(
        first_kernel,
        out_shape=outs,
        grid_spec=pltpu.PrefetchScalarGridSpec(
            num_scalar_prefetch=1,
            grid=(1,),
            in_specs=[here] * 4,
            out_specs=specs,
            scratch_shapes=[
                pltpu.VMEM((4, tokens // STEPS, STEPS, width), BF),
                pltpu.VMEM((2, tiles, width, TILE), BF),
                pltpu.VMEM(grad_a.shape[1:], F32),
                pltpu.VMEM(grad_b.shape[1:], F32),
                pltpu.SemaphoreType.DMA((4,)),
                pltpu.SemaphoreType.DMA((2, tiles)),
                pltpu.SemaphoreType.DMA((2,)),
            ],
        ),
        compiler_params=params(16),
        name="first_terms",
    )(ids, *map(hbm, (hidden, kv_weight, grad_a, grad_b)))


def later_terms(x, kv_weight, after):
    outs = term_shapes(x.shape[0] // 4, CHUNKS[1])
    here = pl.BlockSpec(memory_space=pl.ANY)
    tiles = CHUNKS[1] * HD // TILE
    return pl.pallas_call(
        later_kernel,
        out_shape=outs,
        grid=(1,),
        in_specs=[whole(x.shape), here, here],
        out_specs=[whole(out.shape) for out in outs],
        scratch_shapes=[
            pltpu.VMEM((2, tiles, x.shape[1], TILE), BF),
            pltpu.SemaphoreType.DMA((2, tiles)),
        ],
        compiler_params=params(12),
        name="later_terms",
    )(x, hbm(kv_weight), after)


def mid_kernel(kkeep, kcame, vkeep, vcame, after, kout, vout):
    del after
    kout[...] = (kkeep[...].astype(F32) + kcame[...].astype(F32)).astype(BF)
    vout[...] = (vkeep[...].astype(F32) + vcame[...].astype(F32)).astype(BF)


def mid_sums(kkeep, kcame, vkeep, vcame, after):
    shape = vkeep.shape
    low = pl.BlockSpec(shape, lambda i: (0, 0))
    high = pl.BlockSpec(shape, lambda i: (1, 0))
    return pl.pallas_call(
        mid_kernel,
        out_shape=[jax.ShapeDtypeStruct(shape, BF)] * 2,
        grid=(1,),
        in_specs=[high, low, low, high, pl.BlockSpec(memory_space=pl.ANY)],
        out_specs=[low, low],
        compiler_params=params(4),
        name="mid_sums",
    )(kkeep, kcame, vkeep, vcame, after)


def small_call(kernel, name, ids, args, outs, after=(), scratch=(), copied=0):
    count = len(args)

    def body(ids, *refs):
        kernel(ids, *refs[:count], *refs[count + len(after) :])

    return pl.pallas_call(
        body,
        out_shape=outs,
        grid_spec=pltpu.PrefetchScalarGridSpec(
            num_scalar_prefetch=1,
            grid=(1,),
            in_specs=[whole(x.shape) for x in args]
            + [pl.BlockSpec(memory_space=pl.ANY)] * len(after),
            out_specs=[pl.BlockSpec(memory_space=pltpu.HBM)] * copied
            + [whole(x.shape) for x in outs[copied:]],
            scratch_shapes=list(scratch),
        ),
        compiler_params=params(8),
        name=name,
    )(ids, *args, *after)


def core_flip(x, count):
    return lax.ppermute(x, "dp", [(i, i ^ 1) for i in range(count)])


def plus_kernel(a, b, *rest):
    rest[-1][...] = (a[...].astype(F32) + b[...].astype(F32)).astype(BF)


def plus(a, b, *after):
    out = jax.ShapeDtypeStruct(a.shape, BF)
    return pl.pallas_call(
        plus_kernel,
        out_shape=out,
        grid=(1,),
        in_specs=[whole(a.shape)] * 2 + [pl.BlockSpec(memory_space=pl.ANY)] * len(after),
        out_specs=whole(a.shape),
        compiler_params=params(2),
        name="plus",
    )(a, b, *after)


def along_line(x, d, count):
    return lax.ppermute(x, "dp", [(i, i ^ (2 * d)) for i in range(count)])


TOP = 2 * R


def update_kernel(rates, ids, half, other, factor_a, factor_b, x, out_a, out_b, *rest):
    *sends, a, new_a, new_b, sems = rest
    copies = [
        pltpu.make_async_copy(new_a, out_a, sems.at[0]),
        pltpu.make_async_copy(new_b, out_b, sems.at[1]),
    ]
    wide = factor_a.shape[-1]
    for index, part in ((ids[2], half), (ids[2] ^ 1, other)):
        new_a[index] = factor_a[index] - rates[0] * part[:, :wide].astype(F32)
        new_b[index] = factor_b[index] - rates[1] * part[:, wide:].astype(F32)
    for copy in copies:
        copy.start()
    for p in range(2):
        a[p * R : (p + 1) * R] = new_a[p].astype(BF)
    a[TOP:] = jnp.zeros((TILE - TOP, wide), BF)
    tokens = x.shape[0] // 4

    def multiply(*accs):
        steps = wide // TILE

        def push(k):
            for unit in range(2):
                tile = a[:, k * TILE : (k + 1) * TILE]
                pltpu.matmul_push_rhs(tile, k % 2, unit, transpose=True)

        push(0)
        for k in range(steps):
            if k + 1 < steps:
                push(k + 1)
            for r in range(4):
                rows = x[r * tokens : (r + 1) * tokens, k * TILE : (k + 1) * TILE]
                staged = k % 2 if r < 2 else None
                pltpu.matmul_acc_lhs(accs[r], rows, load_staged_rhs=staged)
        for r, send in enumerate(sends):
            u = (0.25 * pltpu.matmul_pop(accs[r])[:, :TOP]).astype(BF)
            for p in range(2):
                send[p * R : (p + 1) * R, :] = new_b[p].astype(BF)
            send[TOP:, :TOP] = u[:TOP]
            send[TOP:tokens, TOP:] = u[TOP:]
            send[tokens:, TOP:] = jnp.zeros((2 * TOP - tokens, TOP), BF)

    pl.run_scoped(multiply, *[pltpu.ACC(r % 2)((tokens, TILE), F32) for r in range(4)])
    for copy in copies:
        copy.wait()


def updated(ids, half, other, factor_a, factor_b, x, dp, after):
    rates = (2.0 / math.sqrt(dp * D), 2.0 / math.sqrt(dp * R))
    outs = [pltpu.HBM(f.shape, F32) for f in (factor_a, factor_b)]
    outs += [jax.ShapeDtypeStruct((2 * TOP, 2 * TOP), BF)] * 4
    return small_call(
        functools.partial(update_kernel, rates),
        "update_factors",
        ids,
        (half, other, factor_a, factor_b, x),
        outs,
        (after,),
        [
            pltpu.VMEM((TILE, factor_a.shape[-1]), BF),
            pltpu.VMEM(factor_a.shape, F32),
            pltpu.VMEM(factor_b.shape, F32),
            pltpu.SemaphoreType.DMA((2,)),
        ],
        2,
    )


def attend_kernel(ids, first, lengths, *refs):
    q, cache_k, cache_v, k0, k1, k2, v0, v1, v2, *ub, cosine, sine = refs[:15]
    out = refs[-1]
    rows, slots, _ = cache_k.shape
    tokens = rows * STEPS
    u_top = sum(x[TOP:, :TOP].astype(F32) for x in ub)
    u_low = sum(x[TOP:tokens, TOP:].astype(F32) for x in ub)
    u = jnp.concatenate([u_top, u_low], axis=0).astype(BF)
    rel = ids[0] ^ (first[0] + pl.program_id(0))
    low = jnp.where(rel == 0, ub[0][:TOP].astype(F32), ub[1][:TOP].astype(F32))
    high = jnp.where(rel == 2, ub[2][:TOP].astype(F32), ub[3][:TOP].astype(F32))
    b = jnp.where(rel < 2, low, high).astype(BF)
    k = k0[...].astype(F32) + k1[...].astype(F32) + k2[...].astype(F32) + dot(u[:, :R], b[:R])
    v = v0[...].astype(F32) + v1[...].astype(F32) + v2[...].astype(F32) + dot(u[:, R:], b[R:])
    v = v.astype(BF)
    keys = []
    for n in range(HEADS_STEP):
        key = k[:, n * HD : (n + 1) * HD]
        scale = lax.rsqrt(jnp.sum(key * key, axis=-1, keepdims=True) * (1.0 / HD) + 1e-06)
        key = scale * (key * cosine[...] + pltpu.roll(key, HD // 2, 1) * sine[...])
        keys.append(key.astype(BF))
    n_q, n_c = GROUP * STEPS, GROUP * slots
    shape = (n_q, n_c + n_q)
    here = lax.broadcasted_iota(jnp.int32, shape, 0)
    col = lax.broadcasted_iota(jnp.int32, shape, 1)
    fresh = col - n_c
    cached = (col < n_c) & (here // STEPS == col // slots)
    new = (col >= n_c) & (here // STEPS == fresh // STEPS) & (fresh % STEPS <= here % STEPS)
    bias_here = jnp.where(cached | new, 0.0, -1e30)
    col = lax.broadcasted_iota(jnp.int32, (1, n_c + n_q), 1)
    ones = jnp.ones((n_c + n_q, HD), BF)
    factor = math.log2(math.e) * HD**-0.5
    heads = QH // KVH
    blocks = rows // GROUP
    query = q[...].reshape(tokens, HEADS_STEP * heads * HD)

    def block(n, g, cache, fresh):
        old = cache[g * GROUP : (g + 1) * GROUP, :, n * HD : (n + 1) * HD].reshape(n_c, HD)
        return jnp.concatenate([old, fresh[g * n_q : (g + 1) * n_q]], axis=0)

    every = [(n, g) for n in range(HEADS_STEP) for g in range(blocks)]
    scores = []
    for n, g in every:
        part = [query[g * n_q : (g + 1) * n_q, h * HD : (h + 1) * HD] for h in range(n * heads, (n + 1) * heads)]
        scores.append(dot_t(jnp.concatenate(part, axis=0), block(n, g, cache_k, keys[n])))
    biases = []
    for g in range(blocks):
        filled = jnp.full(col.shape, lengths[g * GROUP], jnp.int32)
        for i in range(1, GROUP):
            filled = jnp.where(col // slots == i, lengths[g * GROUP + i], filled)
        bias = jnp.where((col >= n_c) | (col % slots < filled), 0.0, -1e30) + bias_here
        biases.append(jnp.concatenate([bias] * heads, axis=0))
    weights = []
    for (n, g), s in zip(every, scores):
        s = s * factor + biases[g]
        top = jnp.max(s, axis=-1, keepdims=True)
        weights.append(jnp.exp2(s - top).astype(BF))
    results = []
    for (n, g), w in zip(every, weights):
        here_v = block(n, g, cache_v, v[:, n * HD : (n + 1) * HD])
        r = dot(w, jnp.concatenate([here_v, ones], axis=1))
        total = r[:, HD:]
        inverse = pl.reciprocal(total, approx=True)
        inverse = inverse * (2.0 - total * inverse)
        results.append((r[:, :HD] * inverse).astype(BF))
    for n in range(HEADS_STEP):
        for h in range(heads):
            part = [r[h * n_q : (h + 1) * n_q] for r in results[n * blocks : (n + 1) * blocks]]
            at = (n * heads + h) * HD
            out[:, :, at : at + HD] = jnp.concatenate(part, axis=0).reshape(rows, STEPS, HD)


def attend_chunk(
    ids, lengths, start, count, queries, cache_keys, cache_values, terms, ub, tables, before
):
    rows, slots, _ = cache_keys.shape
    tokens = rows * STEPS
    heads = QH // KVH
    args = [*map(hbm, (queries, cache_keys, cache_values)), *terms, *ub, *tables]
    assert start % HEADS_STEP == 0 and count % HEADS_STEP == 0
    first = jnp.full((1,), start // HEADS_STEP, jnp.int32)
    size = HEADS_STEP * HD
    part = pl.BlockSpec((tokens, size), lambda i, *_: (0, i))
    low = pl.BlockSpec((tokens, size), lambda i, *_: (1, i))
    cache = pl.BlockSpec((rows, slots, size), lambda i, _, first, *__: (0, 0, first[0] + i))
    wide = pl.BlockSpec((rows, STEPS, heads * size), lambda i, _, first, *__: (0, 0, first[0] + i))
    specs = [wide, cache, cache, part, low, part, part, part, part]
    specs += [whole(x.shape) for x in (*ub, *tables)]
    args.append(before)
    specs.append(pl.BlockSpec(memory_space=pl.ANY))
    return pl.pallas_call(
        attend_kernel,
        out_shape=jax.ShapeDtypeStruct(queries.shape, BF),
        grid_spec=pltpu.PrefetchScalarGridSpec(
            num_scalar_prefetch=3, grid=(count // HEADS_STEP,), in_specs=specs, out_specs=wide
        ),
        input_output_aliases={len(args) + 2: 0},
        compiler_params=params(14),
        name="attend_chunk",
    )(ids, first, lengths, *args)


def rotary_tables(key_gain, positions):
    half = HD // 2
    place = positions[:, None] + jnp.arange(STEPS, dtype=jnp.int32)[None, :]
    freq = jnp.exp(-math.log(1000000.0) * (jnp.arange(half, dtype=F32) * 2.0 / HD))
    angle = place.reshape(-1).astype(F32)[:, None] * jnp.concatenate([freq, freq])
    turned = jnp.concatenate([-key_gain[half:], key_gain[:half]])
    return jnp.cos(angle) * key_gain, jnp.sin(angle) * turned


def across(x, r):
    return lax.ppermute(x, "tensor", [(i, i ^ r) for i in range(4)])


def square(
    hidden_in,
    kv_weight,
    factor_a,
    factor_b,
    grad_a,
    grad_b,
    key_gain,
    queries,
    cache_keys,
    cache_values,
    cache_lengths,
    positions,
):
    tokens = cache_keys.shape[0] * STEPS
    count_dp = lax.axis_size("dp")
    dp = lax.axis_index("dp")
    ids = jnp.stack([lax.axis_index("tensor"), dp // 2, dp % 2]).astype(jnp.int32)
    tables = rotary_tables(key_gain, positions)

    x, *first, packed, own, attended = first_terms(
        ids, hidden_in, kv_weight, grad_a, grad_b, queries, tokens
    )
    half = plus(own, core_flip(packed, count_dp))

    def first_exchange(term, after):
        ksend, kkeep, vsend, vkeep0, vkeep1 = term
        kcame, vcame = across(ksend, 1), across(vsend, 2)
        mids = mid_sums(kkeep, kcame, vkeep1, vcame, after)
        return mids, (kkeep, kcame, vkeep0, vcame)

    def second_exchange(mids, parts):
        kkeep, kcame, vkeep0, vcame = parts
        return kkeep, kcame, across(mids[0], 2), vkeep0, vcame, across(mids[1], 1)

    second = later_terms(x, kv_weight, half)
    step, after = 1, second[:1]
    while 2 * step < count_dp:
        half = plus(half, along_line(half, step, count_dp), *after)
        step *= 2
        if step == 2:
            mids, parts = first_exchange(first, half)
            after = (mids[0], tables[0])
    if step == 1:
        mids, parts = first_exchange(first, half)
    first = second_exchange(mids, parts)
    other = core_flip(half, count_dp)
    new_a, new_b, *sends = updated(
        ids, half, other, factor_a, factor_b, x, count_dp, mids[0]
    )
    ub = [sends[0]] + [across(sends[r], r) for r in (1, 2, 3)]
    second = second_exchange(*first_exchange(second, ub[1]))
    for start, count, came in ((0, CHUNKS[0], first), (CHUNKS[0], CHUNKS[1], second)):
        attended = attend_chunk(
            ids,
            cache_lengths,
            start,
            count,
            queries,
            cache_keys,
            cache_values,
            came,
            ub,
            tables,
            attended,
        )
    return attended, new_a, new_b


def solution(mesh):
    fits = mesh.shape["tensor"] == 4 and mesh.shape["dp"] in (2, 4, 8)
    return jax.shard_map(
        square if fits else general,
        mesh=mesh,
        in_specs=(
            P("dp", None, "tensor"),
            P(None, "tensor", None),
            P(None, None, "tensor"),
            P(None, None, "tensor"),
            P("dp", None, None, "tensor"),
            P("dp", None, None, "tensor"),
            P(),
            P(("dp", "tensor"), None, None),
            P(("dp", "tensor"), None, None),
            P(("dp", "tensor"), None, None),
            P(("dp", "tensor")),
            P(("dp", "tensor")),
        ),
        out_specs=(
            P(("dp", "tensor"), None, None),
            P(None, None, "tensor"),
            P(None, None, "tensor"),
        ),
        check_vma=False,
    )
```

```python
import functools
import math

import jax
import jax.numpy as jnp
from jax import lax
from jax.experimental import pallas as pl
from jax.experimental.pallas import tpu as pltpu
from jax.sharding import PartitionSpec as P

D = 5120
KVH = 8
HD = 128
QH = 32
R = 64
STEPS = 4
BF = jnp.bfloat16
F32 = jnp.float32
MIB = 1024 * 1024


def normed_rotated(keys, gain, position):
    scale = lax.rsqrt(jnp.mean(keys * keys, axis=-1, keepdims=True) + 1e-06)
    keys = keys * scale * gain
    half = keys.shape[-1] // 2
    freq = jnp.exp(
        -math.log(1000000.0) * (jnp.arange(half, dtype=jnp.float32) * 2.0 / keys.shape[-1])
    )
    angle = position.astype(jnp.float32)[..., None] * freq
    cosine = jnp.concatenate([jnp.cos(angle), jnp.cos(angle)], axis=-1)[..., None, :]
    sine = jnp.concatenate([jnp.sin(angle), jnp.sin(angle)], axis=-1)[..., None, :]
    turned = jnp.concatenate([-keys[..., half:], keys[..., :half]], axis=-1)
    return keys * cosine + turned * sine


def attend(queries, cache_keys, cache_values, new_keys, new_values, lengths):
    rows, steps, width = queries.shape
    slots = cache_keys.shape[1]
    slot = jnp.arange(slots, dtype=jnp.int32)
    for step in range(steps):
        hit = (slot[None, :] == lengths[:, None] + step)[:, :, None]
        cache_keys = jnp.where(hit, new_keys[:, step][:, None, :], cache_keys)
        cache_values = jnp.where(hit, new_values[:, step][:, None, :], cache_values)
    groups = QH // KVH
    query_five = queries.reshape(rows, steps, KVH, groups, HD)
    key_four = cache_keys.reshape(rows, slots, KVH, HD)
    value_four = cache_values.reshape(rows, slots, KVH, HD)
    scores = jnp.einsum(
        "rtkgd,rckd->rtkgc", query_five, key_four, preferred_element_type=jnp.float32
    ) * HD ** (-0.5)
    limit = lengths[:, None] + jnp.arange(steps, dtype=jnp.int32)[None, :]
    valid = (slot[None, None, :] <= limit[:, :, None])[:, :, None, None, :]
    scores = jnp.where(valid, scores, jnp.float32(-1e30))
    top = jnp.max(scores, axis=-1, keepdims=True)
    expo = jnp.exp(scores - top)
    weights = (expo / jnp.sum(expo, axis=-1, keepdims=True)).astype(jnp.bfloat16)
    result = jnp.einsum(
        "rtkgc,rckd->rtkgd", weights, value_four, preferred_element_type=jnp.float32
    )
    return result.reshape(rows, steps, width).astype(jnp.bfloat16)


def general(
    hidden_in,
    kv_weight,
    factor_a,
    factor_b,
    grad_a,
    grad_b,
    key_gain,
    queries,
    cache_keys,
    cache_values,
    cache_lengths,
    positions,
):
    groups_dp = lax.axis_size("dp")
    rate_a = 2.0 / math.sqrt(groups_dp * D)
    rate_b = 2.0 / math.sqrt(groups_dp * R)
    sum_a, sum_b = (
        lax.psum(grad_a[0].astype(jnp.bfloat16), "dp").astype(jnp.float32),
        lax.psum(grad_b[0].astype(jnp.bfloat16), "dp").astype(jnp.float32),
    )
    new_a = factor_a - rate_a * sum_a
    new_b = factor_b - rate_b * sum_b
    full_b = lax.all_gather(new_b.astype(jnp.bfloat16), "tensor", axis=2, tiled=True).astype(
        new_b.dtype
    )
    delta = jnp.einsum("prd,prk->pdk", new_a, full_b, precision=lax.Precision.HIGHEST)
    merged = (kv_weight.astype(jnp.float32) + 0.25 * delta).astype(jnp.bfloat16)
    joined = jnp.concatenate([merged[0], merged[1]], axis=1)
    rows_here = hidden_in.shape[0] // lax.axis_size("tensor")
    pieces = []
    for step in range(STEPS):
        term = jnp.dot(hidden_in[:, step, :], joined, preferred_element_type=jnp.float32)
        pieces.append(
            lax.psum_scatter(
                term.astype(jnp.bfloat16), "tensor", scatter_dimension=0, tiled=True
            ).astype(jnp.float32)
        )
    projected = jnp.stack(pieces, axis=1)
    kv_width = KVH * HD
    place = positions[:, None] + jnp.arange(STEPS, dtype=jnp.int32)[None, :]
    keys = normed_rotated(
        projected[..., :kv_width].reshape(rows_here, STEPS, KVH, HD), key_gain, place
    )
    new_keys = keys.reshape(rows_here, STEPS, kv_width).astype(jnp.bfloat16)
    new_values = projected[..., kv_width:].astype(jnp.bfloat16)
    attended = attend(queries, cache_keys, cache_values, new_keys, new_values, cache_lengths)
    return (attended, new_a, new_b)


CHUNKS = (4, 4)
GROUP = 12
HEADS_STEP = 2


def params(mib):
    return pltpu.CompilerParams(vmem_limit_bytes=mib * MIB)


def dot(a, b):
    return jnp.dot(a, b, preferred_element_type=F32)


def dot_t(a, b):
    return lax.dot_general(a, b, (((1,), (1,)), ((), ())), preferred_element_type=F32)


def whole(shape):
    return pl.BlockSpec(shape, lambda i, *_: (0,) * len(shape))


def hbm(x):
    return pltpu.with_memory_space_constraint(x, pltpu.HBM)


TILE = 256


def multiply_terms(x, w, outs, ready):
    ksend, kkeep, vsend, vkeep0, vkeep1 = outs
    tokens = x.shape[0] // 4
    steps = x.shape[1] // TILE
    low, high = slice(0, tokens), slice(tokens, 2 * tokens)

    def multiply(*accs):
        accs_k, accs_v = accs[:4], accs[4:]

        @pl.loop(0, w.shape[1])
        def _(i):
            ready(i)

            def push(k):
                for p in range(2):
                    pltpu.matmul_push_rhs(w[p, i, k * TILE : (k + 1) * TILE, :], k % 2, p)

            push(0)
            for k in range(steps):
                if k + 1 < steps:
                    push(k + 1)
                for r in range(4):
                    rows = x[r * tokens : (r + 1) * tokens, k * TILE : (k + 1) * TILE]
                    staged = k % 2 if r == 0 else None
                    pltpu.matmul_acc_lhs(accs_k[r], rows, load_staged_rhs=staged)
                    pltpu.matmul_acc_lhs(accs_v[r], rows, load_staged_rhs=staged)
            at = pl.ds(pl.multiple_of(i * TILE, TILE), TILE)
            kkeep[low, at] = pltpu.matmul_pop(accs_k[0]).astype(BF)
            vkeep0[:, at] = pltpu.matmul_pop(accs_v[0]).astype(BF)
            ksend[high, at] = pltpu.matmul_pop(accs_k[1]).astype(BF)
            vkeep1[:, at] = pltpu.matmul_pop(accs_v[1]).astype(BF)
            kkeep[high, at] = pltpu.matmul_pop(accs_k[2]).astype(BF)
            vsend[low, at] = pltpu.matmul_pop(accs_v[2]).astype(BF)
            ksend[low, at] = pltpu.matmul_pop(accs_k[3]).astype(BF)
            vsend[high, at] = pltpu.matmul_pop(accs_v[3]).astype(BF)

    pl.run_scoped(
        multiply, *[pltpu.ACC(unit)((tokens, TILE), F32) for unit in range(2) for _ in range(4)]
    )


def first_kernel(ids, hidden, weight, grad_a, grad_b, *rest):
    x, *outs = rest[:6]
    send, own, _ = rest[6:9]
    held, w, held_a, held_b, hidden_sems, sems, grad_sems = rest[9:]
    tokens = x.shape[0] // 4
    rows = tokens // STEPS

    def hidden_copy(r):
        at = pl.ds((ids[0] ^ r) * rows, rows)
        return pltpu.make_async_copy(hidden.at[at], held.at[r], hidden_sems.at[r])

    def weight_copy(p, i):
        at = pl.ds(i * TILE, TILE)
        return pltpu.make_async_copy(weight.at[p, :, at], w.at[p, i], sems.at[p, i])

    others = [
        pltpu.make_async_copy(grad_a.at[0], held_a, grad_sems.at[0]),
        pltpu.make_async_copy(grad_b.at[0], held_b, grad_sems.at[1]),
    ]
    for r in range(4):
        hidden_copy(r).start()
    for i in range(w.shape[1]):
        for p in range(2):
            weight_copy(p, i).start()
    for r in range(4):
        hidden_copy(r).wait()
        x[r * tokens : (r + 1) * tokens] = held[r].reshape(tokens, x.shape[1])
    for copy in others:
        copy.start()

    def ready(i):
        for p in range(2):
            weight_copy(p, i).wait()

    multiply_terms(x, w, outs, ready)
    for copy in others:
        copy.wait()
    wide = grad_a.shape[-1]
    for out, p in ((send, ids[2] ^ 1), (own, ids[2])):
        out[:, :wide] = held_a[p].astype(BF)
        out[:, wide:] = held_b[p].astype(BF)


def later_kernel(x, weight, after, *rest):
    del after
    *outs, w, sems = rest
    base = weight.shape[2] - w.shape[1] * TILE

    def weight_copy(p, i):
        at = pl.ds(base + i * TILE, TILE)
        return pltpu.make_async_copy(weight.at[p, :, at], w.at[p, i], sems.at[p, i])

    for i in range(w.shape[1]):
        for p in range(2):
            weight_copy(p, i).start()

    def ready(i):
        for p in range(2):
            weight_copy(p, i).wait()

    multiply_terms(x, w, outs, ready)


def term_shapes(tokens, count):
    return [jax.ShapeDtypeStruct((n * tokens, count * HD), BF) for n in (2, 2, 2, 1, 1)]


def first_terms(ids, hidden, kv_weight, grad_a, grad_b, queries, tokens):
    width = hidden.shape[2]
    rank, wide = grad_a.shape[2], grad_a.shape[3] + grad_b.shape[3]
    here = pl.BlockSpec(memory_space=pl.ANY)
    outs = [jax.ShapeDtypeStruct((4 * tokens, width), BF), *term_shapes(tokens, CHUNKS[0])]
    outs[4:] = [pltpu.HBM(x.shape, BF) for x in outs[4:]]
    outs += [jax.ShapeDtypeStruct((rank, wide), BF), pltpu.VMEM((rank, wide), BF)]
    tiles = CHUNKS[0] * HD // TILE
    specs = [whole(x.shape) for x in outs] + [here]
    outs.append(jax.ShapeDtypeStruct(queries.shape, BF))
    return pl.pallas_call(
        first_kernel,
        out_shape=outs,
        grid_spec=pltpu.PrefetchScalarGridSpec(
            num_scalar_prefetch=1,
            grid=(1,),
            in_specs=[here] * 4,
            out_specs=specs,
            scratch_shapes=[
                pltpu.VMEM((4, tokens // STEPS, STEPS, width), BF),
                pltpu.VMEM((2, tiles, width, TILE), BF),
                pltpu.VMEM(grad_a.shape[1:], F32),
                pltpu.VMEM(grad_b.shape[1:], F32),
                pltpu.SemaphoreType.DMA((4,)),
                pltpu.SemaphoreType.DMA((2, tiles)),
                pltpu.SemaphoreType.DMA((2,)),
            ],
        ),
        compiler_params=params(16),
        name="first_terms",
    )(ids, *map(hbm, (hidden, kv_weight, grad_a, grad_b)))


def later_terms(x, kv_weight, after):
    outs = term_shapes(x.shape[0] // 4, CHUNKS[1])
    here = pl.BlockSpec(memory_space=pl.ANY)
    tiles = CHUNKS[1] * HD // TILE
    return pl.pallas_call(
        later_kernel,
        out_shape=outs,
        grid=(1,),
        in_specs=[whole(x.shape), here, here],
        out_specs=[whole(out.shape) for out in outs],
        scratch_shapes=[
            pltpu.VMEM((2, tiles, x.shape[1], TILE), BF),
            pltpu.SemaphoreType.DMA((2, tiles)),
        ],
        compiler_params=params(12),
        name="later_terms",
    )(x, hbm(kv_weight), after)


def mid_kernel(kkeep, kcame, vkeep, vcame, *rest):
    kout, vout = rest[-2:]
    kout[...] = (kkeep[...].astype(F32) + kcame[...].astype(F32)).astype(BF)
    vout[...] = (vkeep[...].astype(F32) + vcame[...].astype(F32)).astype(BF)


def mid_sums(kkeep, kcame, vkeep, vcame, *after):
    shape = vkeep.shape
    low = pl.BlockSpec(shape, lambda i: (0, 0))
    high = pl.BlockSpec(shape, lambda i: (1, 0))
    return pl.pallas_call(
        mid_kernel,
        out_shape=[jax.ShapeDtypeStruct(shape, BF)] * 2,
        grid=(1,),
        in_specs=[high, low, low, high] + [pl.BlockSpec(memory_space=pl.ANY)] * len(after),
        out_specs=[low, low],
        compiler_params=params(4),
        name="mid_sums",
    )(kkeep, kcame, vkeep, vcame, *after)


def small_call(kernel, name, ids, args, outs, after=(), scratch=(), copied=0):
    count = len(args)

    def body(ids, *refs):
        kernel(ids, *refs[:count], *refs[count + len(after) :])

    return pl.pallas_call(
        body,
        out_shape=outs,
        grid_spec=pltpu.PrefetchScalarGridSpec(
            num_scalar_prefetch=1,
            grid=(1,),
            in_specs=[whole(x.shape) for x in args]
            + [pl.BlockSpec(memory_space=pl.ANY)] * len(after),
            out_specs=[pl.BlockSpec(memory_space=pltpu.HBM)] * copied
            + [whole(x.shape) for x in outs[copied:]],
            scratch_shapes=list(scratch),
        ),
        compiler_params=params(8),
        name=name,
    )(ids, *args, *after)


def core_flip(x, count):
    return lax.ppermute(x, "dp", [(i, i ^ 1) for i in range(count)])


def plus_kernel(a, b, *rest):
    rest[-1][...] = (a[...].astype(F32) + b[...].astype(F32)).astype(BF)


def plus(a, b, *after):
    out = jax.ShapeDtypeStruct(a.shape, BF)
    return pl.pallas_call(
        plus_kernel,
        out_shape=out,
        grid=(1,),
        in_specs=[whole(a.shape)] * 2 + [pl.BlockSpec(memory_space=pl.ANY)] * len(after),
        out_specs=whole(a.shape),
        compiler_params=params(2),
        name="plus",
    )(a, b, *after)


def along_line(x, d, count):
    return lax.ppermute(x, "dp", [(i, i ^ (2 * d)) for i in range(count)])


TOP = 2 * R


def update_kernel(rates, ids, half, other, factor_a, factor_b, x, out_a, out_b, *rest):
    *sends, a, new_a, new_b, sems = rest
    copies = [
        pltpu.make_async_copy(new_a, out_a, sems.at[0]),
        pltpu.make_async_copy(new_b, out_b, sems.at[1]),
    ]
    wide = factor_a.shape[-1]
    for index, part in ((ids[2], half), (ids[2] ^ 1, other)):
        new_a[index] = factor_a[index] - rates[0] * part[:, :wide].astype(F32)
        new_b[index] = factor_b[index] - rates[1] * part[:, wide:].astype(F32)
    for copy in copies:
        copy.start()
    for p in range(2):
        a[p * R : (p + 1) * R] = new_a[p].astype(BF)
    a[TOP:] = jnp.zeros((TILE - TOP, wide), BF)
    tokens = x.shape[0] // 4

    def multiply(*accs):
        steps = wide // TILE

        def push(k):
            for unit in range(2):
                tile = a[:, k * TILE : (k + 1) * TILE]
                pltpu.matmul_push_rhs(tile, k % 2, unit, transpose=True)

        push(0)
        for k in range(steps):
            if k + 1 < steps:
                push(k + 1)
            for r in range(4):
                rows = x[r * tokens : (r + 1) * tokens, k * TILE : (k + 1) * TILE]
                staged = k % 2 if r < 2 else None
                pltpu.matmul_acc_lhs(accs[r], rows, load_staged_rhs=staged)
        for r, send in enumerate(sends):
            u = (0.25 * pltpu.matmul_pop(accs[r])[:, :TOP]).astype(BF)
            for p in range(2):
                send[p * R : (p + 1) * R, :] = new_b[p].astype(BF)
            send[TOP:, :TOP] = u[:TOP]
            send[TOP:tokens, TOP:] = u[TOP:]
            send[tokens:, TOP:] = jnp.zeros((2 * TOP - tokens, TOP), BF)

    pl.run_scoped(multiply, *[pltpu.ACC(r % 2)((tokens, TILE), F32) for r in range(4)])
    for copy in copies:
        copy.wait()


def updated(ids, half, other, factor_a, factor_b, x, dp, *after):
    rates = (2.0 / math.sqrt(dp * D), 2.0 / math.sqrt(dp * R))
    outs = [pltpu.HBM(f.shape, F32) for f in (factor_a, factor_b)]
    outs += [jax.ShapeDtypeStruct((2 * TOP, 2 * TOP), BF)] * 4
    return small_call(
        functools.partial(update_kernel, rates),
        "update_factors",
        ids,
        (half, other, factor_a, factor_b, x),
        outs,
        after,
        [
            pltpu.VMEM((TILE, factor_a.shape[-1]), BF),
            pltpu.VMEM(factor_a.shape, F32),
            pltpu.VMEM(factor_b.shape, F32),
            pltpu.SemaphoreType.DMA((2,)),
        ],
        2,
    )


def attend_kernel(ids, first, lengths, *refs):
    q, cache_k, cache_v, k0, k1, k2, v0, v1, v2, *ub, cosine, sine = refs[:15]
    out = refs[-1]
    rows, slots, _ = cache_k.shape
    tokens = rows * STEPS
    u_top = sum(x[TOP:, :TOP].astype(F32) for x in ub)
    u_low = sum(x[TOP:tokens, TOP:].astype(F32) for x in ub)
    u = jnp.concatenate([u_top, u_low], axis=0).astype(BF)
    rel = ids[0] ^ (first[0] + pl.program_id(0))
    low = jnp.where(rel == 0, ub[0][:TOP].astype(F32), ub[1][:TOP].astype(F32))
    high = jnp.where(rel == 2, ub[2][:TOP].astype(F32), ub[3][:TOP].astype(F32))
    b = jnp.where(rel < 2, low, high).astype(BF)
    k = k0[...].astype(F32) + k1[...].astype(F32) + k2[...].astype(F32) + dot(u[:, :R], b[:R])
    v = v0[...].astype(F32) + v1[...].astype(F32) + v2[...].astype(F32) + dot(u[:, R:], b[R:])
    v = v.astype(BF)
    keys = []
    for n in range(HEADS_STEP):
        key = k[:, n * HD : (n + 1) * HD]
        scale = lax.rsqrt(jnp.sum(key * key, axis=-1, keepdims=True) * (1.0 / HD) + 1e-06)
        key = scale * (key * cosine[...] + pltpu.roll(key, HD // 2, 1) * sine[...])
        keys.append(key.astype(BF))
    n_q, n_c = GROUP * STEPS, GROUP * slots
    shape = (n_q, n_c + n_q)
    here = lax.broadcasted_iota(jnp.int32, shape, 0)
    col = lax.broadcasted_iota(jnp.int32, shape, 1)
    fresh = col - n_c
    cached = (col < n_c) & (here // STEPS == col // slots)
    new = (col >= n_c) & (here // STEPS == fresh // STEPS) & (fresh % STEPS <= here % STEPS)
    bias_here = jnp.where(cached | new, 0.0, -1e30)
    col = lax.broadcasted_iota(jnp.int32, (1, n_c + n_q), 1)
    ones = jnp.ones((n_c + n_q, HD), BF)
    factor = math.log2(math.e) * HD**-0.5
    heads = QH // KVH
    blocks = rows // GROUP
    query = q[...].reshape(tokens, HEADS_STEP * heads * HD)

    def block(n, g, cache, fresh):
        old = cache[g * GROUP : (g + 1) * GROUP, :, n * HD : (n + 1) * HD].reshape(n_c, HD)
        return jnp.concatenate([old, fresh[g * n_q : (g + 1) * n_q]], axis=0)

    every = [(n, g) for n in range(HEADS_STEP) for g in range(blocks)]
    scores = []
    for n, g in every:
        part = [query[g * n_q : (g + 1) * n_q, h * HD : (h + 1) * HD] for h in range(n * heads, (n + 1) * heads)]
        scores.append(dot_t(jnp.concatenate(part, axis=0), block(n, g, cache_k, keys[n])))
    biases = []
    for g in range(blocks):
        filled = jnp.full(col.shape, lengths[g * GROUP], jnp.int32)
        for i in range(1, GROUP):
            filled = jnp.where(col // slots == i, lengths[g * GROUP + i], filled)
        bias = jnp.where((col >= n_c) | (col % slots < filled), 0.0, -1e30) + bias_here
        biases.append(jnp.concatenate([bias] * heads, axis=0))
    weights = []
    for (n, g), s in zip(every, scores):
        s = s * factor + biases[g]
        top = jnp.max(s, axis=-1, keepdims=True)
        weights.append(jnp.exp2(s - top).astype(BF))
    results = []
    for (n, g), w in zip(every, weights):
        here_v = block(n, g, cache_v, v[:, n * HD : (n + 1) * HD])
        r = dot(w, jnp.concatenate([here_v, ones], axis=1))
        total = r[:, HD:]
        inverse = pl.reciprocal(total, approx=True)
        inverse = inverse * (2.0 - total * inverse)
        results.append((r[:, :HD] * inverse).astype(BF))
    for n in range(HEADS_STEP):
        for h in range(heads):
            part = [r[h * n_q : (h + 1) * n_q] for r in results[n * blocks : (n + 1) * blocks]]
            at = (n * heads + h) * HD
            out[:, :, at : at + HD] = jnp.concatenate(part, axis=0).reshape(rows, STEPS, HD)


def attend_chunk(
    ids, lengths, start, count, queries, cache_keys, cache_values, terms, ub, tables, before
):
    rows, slots, _ = cache_keys.shape
    tokens = rows * STEPS
    heads = QH // KVH
    args = [*map(hbm, (queries, cache_keys, cache_values)), *terms, *ub, *tables]
    assert start % HEADS_STEP == 0 and count % HEADS_STEP == 0
    first = jnp.full((1,), start // HEADS_STEP, jnp.int32)
    size = HEADS_STEP * HD
    part = pl.BlockSpec((tokens, size), lambda i, *_: (0, i))
    low = pl.BlockSpec((tokens, size), lambda i, *_: (1, i))
    cache = pl.BlockSpec((rows, slots, size), lambda i, _, first, *__: (0, 0, first[0] + i))
    wide = pl.BlockSpec((rows, STEPS, heads * size), lambda i, _, first, *__: (0, 0, first[0] + i))
    specs = [wide, cache, cache, part, low, part, part, part, part]
    specs += [whole(x.shape) for x in (*ub, *tables)]
    args.append(before)
    specs.append(pl.BlockSpec(memory_space=pl.ANY))
    return pl.pallas_call(
        attend_kernel,
        out_shape=jax.ShapeDtypeStruct(queries.shape, BF),
        grid_spec=pltpu.PrefetchScalarGridSpec(
            num_scalar_prefetch=3, grid=(count // HEADS_STEP,), in_specs=specs, out_specs=wide
        ),
        input_output_aliases={len(args) + 2: 0},
        compiler_params=params(14),
        name="attend_chunk",
    )(ids, first, lengths, *args)


def rotary_tables(key_gain, positions):
    half = HD // 2
    place = positions[:, None] + jnp.arange(STEPS, dtype=jnp.int32)[None, :]
    freq = jnp.exp(-math.log(1000000.0) * (jnp.arange(half, dtype=F32) * 2.0 / HD))
    angle = place.reshape(-1).astype(F32)[:, None] * jnp.concatenate([freq, freq])
    turned = jnp.concatenate([-key_gain[half:], key_gain[:half]])
    return jnp.cos(angle) * key_gain, jnp.sin(angle) * turned


def across(x, r):
    return lax.ppermute(x, "tensor", [(i, i ^ r) for i in range(4)])


def square(
    hidden_in,
    kv_weight,
    factor_a,
    factor_b,
    grad_a,
    grad_b,
    key_gain,
    queries,
    cache_keys,
    cache_values,
    cache_lengths,
    positions,
):
    tokens = cache_keys.shape[0] * STEPS
    count_dp = lax.axis_size("dp")
    dp = lax.axis_index("dp")
    ids = jnp.stack([lax.axis_index("tensor"), dp // 2, dp % 2]).astype(jnp.int32)
    tables = rotary_tables(key_gain, positions)

    x, *first, packed, own, attended = first_terms(
        ids, hidden_in, kv_weight, grad_a, grad_b, queries, tokens
    )
    own = pltpu.with_memory_space_constraint(own, pltpu.VMEM)
    half = plus(own, core_flip(packed, count_dp))

    def first_exchange(term, *after):
        ksend, kkeep, vsend, vkeep0, vkeep1 = term
        kcame, vcame = across(ksend, 1), across(vsend, 2)
        mids = mid_sums(kkeep, kcame, vkeep1, vcame, *after)
        return mids, (kkeep, kcame, vkeep0, vcame)

    def second_exchange(mids, parts):
        kkeep, kcame, vkeep0, vcame = parts
        return kkeep, kcame, across(mids[0], 2), vkeep0, vcame, across(mids[1], 1)

    second = later_terms(x, kv_weight, half)
    step, after = 1, second[:1]
    while 2 * step < count_dp:
        half = plus(half, along_line(half, step, count_dp), *after)
        step *= 2
        if step == 2:
            mids, parts = first_exchange(first, half)
            after = (mids[0], tables[0])
    if step == 1:
        mids, parts = first_exchange(first, half)
    first = second_exchange(mids, parts)
    other = core_flip(half, count_dp)
    new_a, new_b, *sends = updated(
        ids, half, other, factor_a, factor_b, x, count_dp, first[2], first[5]
    )
    ub = [sends[0]] + [across(sends[r], r) for r in (1, 2, 3)]
    second = second_exchange(*first_exchange(second, *ub[1:]))
    for start, count, came in ((0, CHUNKS[0], first), (CHUNKS[0], CHUNKS[1], second)):
        attended = attend_chunk(
            ids,
            cache_lengths,
            start,
            count,
            queries,
            cache_keys,
            cache_values,
            came,
            ub,
            tables,
            attended,
        )
    return attended, new_a, new_b


def solution(mesh):
    fits = mesh.shape["tensor"] == 4 and mesh.shape["dp"] in (2, 4, 8)
    return jax.shard_map(
        square if fits else general,
        mesh=mesh,
        in_specs=(
            P("dp", None, "tensor"),
            P(None, "tensor", None),
            P(None, None, "tensor"),
            P(None, None, "tensor"),
            P("dp", None, None, "tensor"),
            P("dp", None, None, "tensor"),
            P(),
            P(("dp", "tensor"), None, None),
            P(("dp", "tensor"), None, None),
            P(("dp", "tensor"), None, None),
            P(("dp", "tensor")),
            P(("dp", "tensor")),
        ),
        out_specs=(
            P(("dp", "tensor"), None, None),
            P(None, None, "tensor"),
            P(None, None, "tensor"),
        ),
        check_vma=False,
    )
```

```python
import functools
import math

import jax
import jax.numpy as jnp
from jax import lax
from jax.experimental import pallas as pl
from jax.experimental.pallas import tpu as pltpu
from jax.sharding import PartitionSpec as P

D = 5120
KVH = 8
HD = 128
QH = 32
R = 64
STEPS = 4
BF = jnp.bfloat16
F32 = jnp.float32
MIB = 1024 * 1024


def normed_rotated(keys, gain, position):
    scale = lax.rsqrt(jnp.mean(keys * keys, axis=-1, keepdims=True) + 1e-06)
    keys = keys * scale * gain
    half = keys.shape[-1] // 2
    freq = jnp.exp(
        -math.log(1000000.0) * (jnp.arange(half, dtype=jnp.float32) * 2.0 / keys.shape[-1])
    )
    angle = position.astype(jnp.float32)[..., None] * freq
    cosine = jnp.concatenate([jnp.cos(angle), jnp.cos(angle)], axis=-1)[..., None, :]
    sine = jnp.concatenate([jnp.sin(angle), jnp.sin(angle)], axis=-1)[..., None, :]
    turned = jnp.concatenate([-keys[..., half:], keys[..., :half]], axis=-1)
    return keys * cosine + turned * sine


def attend(queries, cache_keys, cache_values, new_keys, new_values, lengths):
    rows, steps, width = queries.shape
    slots = cache_keys.shape[1]
    slot = jnp.arange(slots, dtype=jnp.int32)
    for step in range(steps):
        hit = (slot[None, :] == lengths[:, None] + step)[:, :, None]
        cache_keys = jnp.where(hit, new_keys[:, step][:, None, :], cache_keys)
        cache_values = jnp.where(hit, new_values[:, step][:, None, :], cache_values)
    groups = QH // KVH
    query_five = queries.reshape(rows, steps, KVH, groups, HD)
    key_four = cache_keys.reshape(rows, slots, KVH, HD)
    value_four = cache_values.reshape(rows, slots, KVH, HD)
    scores = jnp.einsum(
        "rtkgd,rckd->rtkgc", query_five, key_four, preferred_element_type=jnp.float32
    ) * HD ** (-0.5)
    limit = lengths[:, None] + jnp.arange(steps, dtype=jnp.int32)[None, :]
    valid = (slot[None, None, :] <= limit[:, :, None])[:, :, None, None, :]
    scores = jnp.where(valid, scores, jnp.float32(-1e30))
    top = jnp.max(scores, axis=-1, keepdims=True)
    expo = jnp.exp(scores - top)
    weights = (expo / jnp.sum(expo, axis=-1, keepdims=True)).astype(jnp.bfloat16)
    result = jnp.einsum(
        "rtkgc,rckd->rtkgd", weights, value_four, preferred_element_type=jnp.float32
    )
    return result.reshape(rows, steps, width).astype(jnp.bfloat16)


def general(
    hidden_in,
    kv_weight,
    factor_a,
    factor_b,
    grad_a,
    grad_b,
    key_gain,
    queries,
    cache_keys,
    cache_values,
    cache_lengths,
    positions,
):
    groups_dp = lax.axis_size("dp")
    rate_a = 2.0 / math.sqrt(groups_dp * D)
    rate_b = 2.0 / math.sqrt(groups_dp * R)
    sum_a, sum_b = (
        lax.psum(grad_a[0].astype(jnp.bfloat16), "dp").astype(jnp.float32),
        lax.psum(grad_b[0].astype(jnp.bfloat16), "dp").astype(jnp.float32),
    )
    new_a = factor_a - rate_a * sum_a
    new_b = factor_b - rate_b * sum_b
    full_b = lax.all_gather(new_b.astype(jnp.bfloat16), "tensor", axis=2, tiled=True).astype(
        new_b.dtype
    )
    delta = jnp.einsum("prd,prk->pdk", new_a, full_b, precision=lax.Precision.HIGHEST)
    merged = (kv_weight.astype(jnp.float32) + 0.25 * delta).astype(jnp.bfloat16)
    joined = jnp.concatenate([merged[0], merged[1]], axis=1)
    rows_here = hidden_in.shape[0] // lax.axis_size("tensor")
    pieces = []
    for step in range(STEPS):
        term = jnp.dot(hidden_in[:, step, :], joined, preferred_element_type=jnp.float32)
        pieces.append(
            lax.psum_scatter(
                term.astype(jnp.bfloat16), "tensor", scatter_dimension=0, tiled=True
            ).astype(jnp.float32)
        )
    projected = jnp.stack(pieces, axis=1)
    kv_width = KVH * HD
    place = positions[:, None] + jnp.arange(STEPS, dtype=jnp.int32)[None, :]
    keys = normed_rotated(
        projected[..., :kv_width].reshape(rows_here, STEPS, KVH, HD), key_gain, place
    )
    new_keys = keys.reshape(rows_here, STEPS, kv_width).astype(jnp.bfloat16)
    new_values = projected[..., kv_width:].astype(jnp.bfloat16)
    attended = attend(queries, cache_keys, cache_values, new_keys, new_values, cache_lengths)
    return (attended, new_a, new_b)


CHUNKS = (4, 4)
GROUP = 4
HEADS_STEP = 2


def params(mib):
    return pltpu.CompilerParams(vmem_limit_bytes=mib * MIB)


def cost(flops, *arrays):
    size = sum(math.prod(x.shape) * x.dtype.itemsize for x in arrays)
    return pl.CostEstimate(flops=flops, bytes_accessed=size, transcendentals=0)


def dot(a, b):
    return jnp.dot(a, b, preferred_element_type=F32)


def dot_t(a, b):
    return lax.dot_general(a, b, (((1,), (1,)), ((), ())), preferred_element_type=F32)


def whole(shape):
    return pl.BlockSpec(shape, lambda i, *_: (0,) * len(shape))


def hbm(x):
    return pltpu.with_memory_space_constraint(x, pltpu.HBM)


TILE = 256


def multiply_terms(x, w, outs, ready):
    ksend, kkeep, vsend, vkeep0, vkeep1 = outs
    tokens = x.shape[0] // 4
    steps = x.shape[1] // TILE
    low, high = slice(0, tokens), slice(tokens, 2 * tokens)

    def multiply(*accs):
        accs_k, accs_v = accs[:4], accs[4:]

        @pl.loop(0, w.shape[1])
        def _(i):
            ready(i)

            def push(k):
                for p in range(2):
                    pltpu.matmul_push_rhs(w[p, i, k * TILE : (k + 1) * TILE, :], k % 2, p)

            push(0)
            for k in range(steps):
                if k + 1 < steps:
                    push(k + 1)
                for r in range(4):
                    rows = x[r * tokens : (r + 1) * tokens, k * TILE : (k + 1) * TILE]
                    staged = k % 2 if r == 0 else None
                    pltpu.matmul_acc_lhs(accs_k[r], rows, load_staged_rhs=staged)
                    pltpu.matmul_acc_lhs(accs_v[r], rows, load_staged_rhs=staged)
            at = pl.ds(pl.multiple_of(i * TILE, TILE), TILE)
            kkeep[low, at] = pltpu.matmul_pop(accs_k[0]).astype(BF)
            vkeep0[:, at] = pltpu.matmul_pop(accs_v[0]).astype(BF)
            ksend[high, at] = pltpu.matmul_pop(accs_k[1]).astype(BF)
            vkeep1[:, at] = pltpu.matmul_pop(accs_v[1]).astype(BF)
            kkeep[high, at] = pltpu.matmul_pop(accs_k[2]).astype(BF)
            vsend[low, at] = pltpu.matmul_pop(accs_v[2]).astype(BF)
            ksend[low, at] = pltpu.matmul_pop(accs_k[3]).astype(BF)
            vsend[high, at] = pltpu.matmul_pop(accs_v[3]).astype(BF)

    pl.run_scoped(
        multiply, *[pltpu.ACC(unit)((tokens, TILE), F32) for unit in range(2) for _ in range(4)]
    )


def first_kernel(ids, hidden, weight, grad_a, grad_b, *rest):
    x, *outs = rest[:6]
    send, own, _ = rest[6:9]
    held, w, held_a, held_b, hidden_sems, sems, grad_sems = rest[9:]
    tokens = x.shape[0] // 4
    rows = tokens // STEPS

    def hidden_copy(r):
        at = pl.ds((ids[0] ^ r) * rows, rows)
        return pltpu.make_async_copy(hidden.at[at], held.at[r], hidden_sems.at[r])

    def weight_copy(p, i):
        at = pl.ds(i * TILE, TILE)
        return pltpu.make_async_copy(weight.at[p, :, at], w.at[p, i], sems.at[p, i])

    others = [
        pltpu.make_async_copy(grad_a.at[0], held_a, grad_sems.at[0]),
        pltpu.make_async_copy(grad_b.at[0], held_b, grad_sems.at[1]),
    ]
    for r in range(4):
        hidden_copy(r).start()
    for i in range(w.shape[1]):
        for p in range(2):
            weight_copy(p, i).start()
    for r in range(4):
        hidden_copy(r).wait()
        x[r * tokens : (r + 1) * tokens] = held[r].reshape(tokens, x.shape[1])
    for copy in others:
        copy.start()

    def ready(i):
        for p in range(2):
            weight_copy(p, i).wait()

    multiply_terms(x, w, outs, ready)
    for copy in others:
        copy.wait()
    wide = grad_a.shape[-1]
    for out, p in ((send, ids[2] ^ 1), (own, ids[2])):
        out[:, :wide] = held_a[p].astype(BF)
        out[:, wide:] = held_b[p].astype(BF)


def later_kernel(x, weight, after, *rest):
    del after
    *outs, w, sems = rest
    base = weight.shape[2] - w.shape[1] * TILE

    def weight_copy(p, i):
        at = pl.ds(base + i * TILE, TILE)
        return pltpu.make_async_copy(weight.at[p, :, at], w.at[p, i], sems.at[p, i])

    for i in range(w.shape[1]):
        for p in range(2):
            weight_copy(p, i).start()

    def ready(i):
        for p in range(2):
            weight_copy(p, i).wait()

    multiply_terms(x, w, outs, ready)


def term_shapes(tokens, count):
    return [jax.ShapeDtypeStruct((n * tokens, count * HD), BF) for n in (2, 2, 2, 1, 1)]


def first_terms(ids, hidden, kv_weight, grad_a, grad_b, queries, tokens):
    width = hidden.shape[2]
    rank, wide = grad_a.shape[2], grad_a.shape[3] + grad_b.shape[3]
    here = pl.BlockSpec(memory_space=pl.ANY)
    outs = [jax.ShapeDtypeStruct((4 * tokens, width), BF), *term_shapes(tokens, CHUNKS[0])]
    outs += [jax.ShapeDtypeStruct((rank, wide), BF)] * 2
    tiles = CHUNKS[0] * HD // TILE
    specs = [whole(x.shape) for x in outs] + [here]
    outs.append(jax.ShapeDtypeStruct(queries.shape, BF))
    return pl.pallas_call(
        first_kernel,
        out_shape=outs,
        grid_spec=pltpu.PrefetchScalarGridSpec(
            num_scalar_prefetch=1,
            grid=(1,),
            in_specs=[here] * 4,
            out_specs=specs,
            scratch_shapes=[
                pltpu.VMEM((4, tokens // STEPS, STEPS, width), BF),
                pltpu.VMEM((2, tiles, width, TILE), BF),
                pltpu.VMEM(grad_a.shape[1:], F32),
                pltpu.VMEM(grad_b.shape[1:], F32),
                pltpu.SemaphoreType.DMA((4,)),
                pltpu.SemaphoreType.DMA((2, tiles)),
                pltpu.SemaphoreType.DMA((2,)),
            ],
        ),
        compiler_params=params(16),
        cost_estimate=cost(16 * tokens * width * CHUNKS[0] * HD, hidden),
        name="first_terms",
    )(ids, *map(hbm, (hidden, kv_weight, grad_a, grad_b)))


def later_terms(x, kv_weight, after):
    outs = term_shapes(x.shape[0] // 4, CHUNKS[1])
    here = pl.BlockSpec(memory_space=pl.ANY)
    tiles = CHUNKS[1] * HD // TILE
    return pl.pallas_call(
        later_kernel,
        out_shape=outs,
        grid=(1,),
        in_specs=[whole(x.shape), here, here],
        out_specs=[whole(out.shape) for out in outs],
        scratch_shapes=[
            pltpu.VMEM((2, tiles, x.shape[1], TILE), BF),
            pltpu.SemaphoreType.DMA((2, tiles)),
        ],
        compiler_params=params(12),
        cost_estimate=cost(4 * math.prod(x.shape) * CHUNKS[1] * HD, x, *outs),
        name="later_terms",
    )(x, hbm(kv_weight), after)


def mid_kernel(kkeep, kcame, vkeep, vcame, *rest):
    kout, vout = rest[-2:]
    kout[...] = (kkeep[...].astype(F32) + kcame[...].astype(F32)).astype(BF)
    vout[...] = (vkeep[...].astype(F32) + vcame[...].astype(F32)).astype(BF)


def mid_sums(kkeep, kcame, vkeep, vcame, *after):
    shape = vkeep.shape
    low = pl.BlockSpec(shape, lambda i: (0, 0))
    high = pl.BlockSpec(shape, lambda i: (1, 0))
    return pl.pallas_call(
        mid_kernel,
        out_shape=[jax.ShapeDtypeStruct(shape, BF)] * 2,
        grid=(1,),
        in_specs=[high, low, low, high] + [pl.BlockSpec(memory_space=pl.ANY)] * len(after),
        out_specs=[low, low],
        compiler_params=params(4),
        cost_estimate=cost(0, *[vkeep] * 6),
        name="mid_sums",
    )(kkeep, kcame, vkeep, vcame, *after)


def small_call(kernel, name, ids, args, outs, after=(), scratch=(), copied=0):
    count = len(args)

    def body(ids, *refs):
        kernel(ids, *refs[:count], *refs[count + len(after) :])

    return pl.pallas_call(
        body,
        out_shape=outs,
        grid_spec=pltpu.PrefetchScalarGridSpec(
            num_scalar_prefetch=1,
            grid=(1,),
            in_specs=[whole(x.shape) for x in args]
            + [pl.BlockSpec(memory_space=pl.ANY)] * len(after),
            out_specs=[pl.BlockSpec(memory_space=pltpu.HBM)] * copied
            + [whole(x.shape) for x in outs[copied:]],
            scratch_shapes=list(scratch),
        ),
        compiler_params=params(8),
        cost_estimate=cost(0, *args),
        name=name,
    )(ids, *args, *after)


def core_flip(x, count):
    return lax.ppermute(x, "dp", [(i, i ^ 1) for i in range(count)])


def plus_kernel(a, b, *rest):
    rest[-1][...] = (a[...].astype(F32) + b[...].astype(F32)).astype(BF)


def plus(a, b, *after):
    out = jax.ShapeDtypeStruct(a.shape, BF)
    return pl.pallas_call(
        plus_kernel,
        out_shape=out,
        grid=(1,),
        in_specs=[whole(a.shape)] * 2 + [pl.BlockSpec(memory_space=pl.ANY)] * len(after),
        out_specs=whole(a.shape),
        compiler_params=params(2),
        cost_estimate=cost(0, a, b, out),
        name="plus",
    )(a, b, *after)


def along_line(x, d, count):
    return lax.ppermute(x, "dp", [(i, i ^ (2 * d)) for i in range(count)])


TOP = 2 * R


def update_kernel(rates, ids, half, other, factor_a, factor_b, x, out_a, out_b, *rest):
    *sends, a, new_a, new_b, sems = rest
    copies = [
        pltpu.make_async_copy(new_a, out_a, sems.at[0]),
        pltpu.make_async_copy(new_b, out_b, sems.at[1]),
    ]
    wide = factor_a.shape[-1]
    for index, part in ((ids[2], half), (ids[2] ^ 1, other)):
        new_a[index] = factor_a[index] - rates[0] * part[:, :wide].astype(F32)
        new_b[index] = factor_b[index] - rates[1] * part[:, wide:].astype(F32)
    for copy in copies:
        copy.start()
    for p in range(2):
        a[p * R : (p + 1) * R] = new_a[p].astype(BF)
    a[TOP:] = jnp.zeros((TILE - TOP, wide), BF)
    tokens = x.shape[0] // 4

    def multiply(*accs):
        steps = wide // TILE

        def push(k):
            for unit in range(2):
                tile = a[:, k * TILE : (k + 1) * TILE]
                pltpu.matmul_push_rhs(tile, k % 2, unit, transpose=True)

        push(0)
        for k in range(steps):
            if k + 1 < steps:
                push(k + 1)
            for r in range(4):
                rows = x[r * tokens : (r + 1) * tokens, k * TILE : (k + 1) * TILE]
                staged = k % 2 if r < 2 else None
                pltpu.matmul_acc_lhs(accs[r], rows, load_staged_rhs=staged)
        for r, send in enumerate(sends):
            u = (0.25 * pltpu.matmul_pop(accs[r])[:, :TOP]).astype(BF)
            for p in range(2):
                send[p * R : (p + 1) * R, :] = new_b[p].astype(BF)
            send[TOP:, :TOP] = u[:TOP]
            send[TOP:tokens, TOP:] = u[TOP:]
            send[tokens:, TOP:] = jnp.zeros((2 * TOP - tokens, TOP), BF)

    pl.run_scoped(multiply, *[pltpu.ACC(r % 2)((tokens, TILE), F32) for r in range(4)])
    for copy in copies:
        copy.wait()


def updated(ids, half, other, factor_a, factor_b, x, dp, *after):
    rates = (2.0 / math.sqrt(dp * D), 2.0 / math.sqrt(dp * R))
    outs = [pltpu.HBM(f.shape, F32) for f in (factor_a, factor_b)]
    outs += [jax.ShapeDtypeStruct((2 * TOP, 2 * TOP), BF)] * 4
    return small_call(
        functools.partial(update_kernel, rates),
        "update_factors",
        ids,
        (half, other, factor_a, factor_b, x),
        outs,
        after,
        [
            pltpu.VMEM((TILE, factor_a.shape[-1]), BF),
            pltpu.VMEM(factor_a.shape, F32),
            pltpu.VMEM(factor_b.shape, F32),
            pltpu.SemaphoreType.DMA((2,)),
        ],
        2,
    )


def attend_kernel(ids, first, lengths, *refs):
    q, cache_k, cache_v, k0, k1, k2, v0, v1, v2, *ub, cosine, sine = refs[:15]
    out = refs[-3]
    rows, slots, _ = cache_k.shape
    tokens = rows * STEPS
    u_held, b_held = refs[-2:]

    @pl.when(pl.program_id(0) == 0)
    def _():
        u_held[:TOP] = sum(x[TOP:, :TOP].astype(F32) for x in ub).astype(BF)
        u_held[TOP:] = sum(x[TOP:tokens, TOP:].astype(F32) for x in ub).astype(BF)

    rel = ids[0] ^ (first[0] + pl.program_id(0))
    for r, x in enumerate(ub):

        @pl.when(rel == r)
        def _():
            b_held[...] = x[:TOP]

    u, b = u_held[...], b_held[...]
    k = k0[...].astype(F32) + k1[...].astype(F32) + k2[...].astype(F32) + dot(u[:, :R], b[:R])
    v = v0[...].astype(F32) + v1[...].astype(F32) + v2[...].astype(F32) + dot(u[:, R:], b[R:])
    v = v.astype(BF)
    keys = []
    for n in range(HEADS_STEP):
        key = k[:, n * HD : (n + 1) * HD]
        scale = lax.rsqrt(jnp.sum(key * key, axis=-1, keepdims=True) * (1.0 / HD) + 1e-06)
        key = scale * (key * cosine[...] + pltpu.roll(key, HD // 2, 1) * sine[...])
        keys.append(key.astype(BF))
    n_q, n_c = GROUP * STEPS, GROUP * slots
    shape = (n_q, n_c + n_q)
    here = lax.broadcasted_iota(jnp.int32, shape, 0)
    col = lax.broadcasted_iota(jnp.int32, shape, 1)
    fresh = col - n_c
    cached = (col < n_c) & (here // STEPS == col // slots)
    new = (col >= n_c) & (here // STEPS == fresh // STEPS) & (fresh % STEPS <= here % STEPS)
    bias_here = jnp.where(cached | new, 0.0, -1e30)
    col = lax.broadcasted_iota(jnp.int32, (1, n_c + n_q), 1)
    ones = jnp.ones((n_c + n_q, HD), BF)
    factor = math.log2(math.e) * HD**-0.5
    heads = QH // KVH
    blocks = rows // GROUP
    query = q[...].reshape(tokens, HEADS_STEP * heads * HD)

    def block(n, g, cache, fresh):
        old = cache[g * GROUP : (g + 1) * GROUP, :, n * HD : (n + 1) * HD].reshape(n_c, HD)
        return jnp.concatenate([old, fresh[g * n_q : (g + 1) * n_q]], axis=0)

    every = [(n, g) for n in range(HEADS_STEP) for g in range(blocks)]
    scores = []
    for n, g in every:
        part = [query[g * n_q : (g + 1) * n_q, h * HD : (h + 1) * HD] for h in range(n * heads, (n + 1) * heads)]
        scores.append(dot_t(jnp.concatenate(part, axis=0), block(n, g, cache_k, keys[n])))
    biases = []
    for g in range(blocks):
        filled = jnp.full(col.shape, lengths[g * GROUP], jnp.int32)
        for i in range(1, GROUP):
            filled = jnp.where(col // slots == i, lengths[g * GROUP + i], filled)
        bias = jnp.where((col >= n_c) | (col % slots < filled), 0.0, -1e30) + bias_here
        biases.append(jnp.concatenate([bias] * heads, axis=0))
    weights = []
    for (n, g), s in zip(every, scores):
        s = s * factor + biases[g]
        top = jnp.max(s, axis=-1, keepdims=True)
        weights.append(jnp.exp2(s - top).astype(BF))
    results = []
    for (n, g), w in zip(every, weights):
        here_v = block(n, g, cache_v, v[:, n * HD : (n + 1) * HD])
        r = dot(w, jnp.concatenate([here_v, ones], axis=1))
        total = r[:, HD:]
        inverse = pl.reciprocal(total, approx=True)
        inverse = inverse * (2.0 - total * inverse)
        results.append((r[:, :HD] * inverse).astype(BF))
    for n in range(HEADS_STEP):
        for h in range(heads):
            part = [r[h * n_q : (h + 1) * n_q] for r in results[n * blocks : (n + 1) * blocks]]
            at = (n * heads + h) * HD
            out[:, :, at : at + HD] = jnp.concatenate(part, axis=0).reshape(rows, STEPS, HD)


def attend_chunk(
    ids, lengths, start, count, queries, cache_keys, cache_values, terms, ub, tables, before
):
    rows, slots, _ = cache_keys.shape
    tokens = rows * STEPS
    heads = QH // KVH
    args = [queries, cache_keys, cache_values, *terms, *ub, *tables]
    assert start % HEADS_STEP == 0 and count % HEADS_STEP == 0
    first = jnp.full((1,), start // HEADS_STEP, jnp.int32)
    size = HEADS_STEP * HD
    part = pl.BlockSpec((tokens, size), lambda i, *_: (0, i))
    low = pl.BlockSpec((tokens, size), lambda i, *_: (1, i))
    cache = pl.BlockSpec((rows, slots, size), lambda i, _, first, *__: (0, 0, first[0] + i))
    wide = pl.BlockSpec((rows, STEPS, heads * size), lambda i, _, first, *__: (0, 0, first[0] + i))
    specs = [wide, cache, cache, part, low, part, part, part, part]
    specs += [whole(x.shape) for x in (*ub, *tables)]
    args.append(before)
    specs.append(pl.BlockSpec(memory_space=pl.ANY))
    return pl.pallas_call(
        attend_kernel,
        out_shape=jax.ShapeDtypeStruct(queries.shape, BF),
        grid_spec=pltpu.PrefetchScalarGridSpec(
            num_scalar_prefetch=3, grid=(count // HEADS_STEP,), in_specs=specs, out_specs=wide,
            scratch_shapes=[pltpu.VMEM((tokens, TOP), BF), pltpu.VMEM((TOP, size), BF)],
        ),
        input_output_aliases={len(args) + 2: 0},
        compiler_params=params(14),
        cost_estimate=cost(count * 4 * 10**9, *args),
        name="attend_chunk",
    )(ids, first, lengths, *args)


def rotary_tables(key_gain, positions):
    half = HD // 2
    place = positions[:, None] + jnp.arange(STEPS, dtype=jnp.int32)[None, :]
    freq = jnp.exp(-math.log(1000000.0) * (jnp.arange(half, dtype=F32) * 2.0 / HD))
    angle = place.reshape(-1).astype(F32)[:, None] * jnp.concatenate([freq, freq])
    turned = jnp.concatenate([-key_gain[half:], key_gain[:half]])
    return jnp.cos(angle) * key_gain, jnp.sin(angle) * turned


def across(x, r):
    return lax.ppermute(x, "tensor", [(i, i ^ r) for i in range(4)])


def square(
    hidden_in,
    kv_weight,
    factor_a,
    factor_b,
    grad_a,
    grad_b,
    key_gain,
    queries,
    cache_keys,
    cache_values,
    cache_lengths,
    positions,
):
    tokens = cache_keys.shape[0] * STEPS
    count_dp = lax.axis_size("dp")
    dp = lax.axis_index("dp")
    ids = jnp.stack([lax.axis_index("tensor"), dp // 2, dp % 2]).astype(jnp.int32)
    tables = rotary_tables(key_gain, positions)

    x, *first, packed, own, attended = first_terms(
        ids, hidden_in, kv_weight, grad_a, grad_b, queries, tokens
    )
    half = plus(own, core_flip(packed, count_dp))

    def first_exchange(term, *after):
        ksend, kkeep, vsend, vkeep0, vkeep1 = term
        kcame, vcame = across(ksend, 1), across(vsend, 2)
        mids = mid_sums(kkeep, kcame, vkeep1, vcame, *after)
        return mids, (kkeep, kcame, vkeep0, vcame)

    def second_exchange(mids, parts):
        kkeep, kcame, vkeep0, vcame = parts
        return kkeep, kcame, across(mids[0], 2), vkeep0, vcame, across(mids[1], 1)

    second = later_terms(x, kv_weight, half)
    step, after = 1, second[:1]
    while 2 * step < count_dp:
        half = plus(half, along_line(half, step, count_dp), *after)
        step *= 2
        if step == 2:
            mids, parts = first_exchange(first, half)
            after = (mids[0], tables[0])
    if step == 1:
        mids, parts = first_exchange(first, half)
    first = second_exchange(mids, parts)
    other = core_flip(half, count_dp)
    new_a, new_b, *sends = updated(
        ids, half, other, factor_a, factor_b, x, count_dp
    )
    ub = [sends[0]] + [across(sends[r], r) for r in (1, 2, 3)]
    second = second_exchange(*first_exchange(second, *ub[1:]))
    for start, count, came in ((0, CHUNKS[0], first), (CHUNKS[0], CHUNKS[1], second)):
        attended = attend_chunk(
            ids,
            cache_lengths,
            start,
            count,
            queries,
            cache_keys,
            cache_values,
            came,
            ub,
            tables,
            attended,
        )
    return attended, new_a, new_b


def solution(mesh):
    fits = mesh.shape["tensor"] == 4 and mesh.shape["dp"] in (2, 4, 8)
    return jax.shard_map(
        square if fits else general,
        mesh=mesh,
        in_specs=(
            P("dp", None, "tensor"),
            P(None, "tensor", None),
            P(None, None, "tensor"),
            P(None, None, "tensor"),
            P("dp", None, None, "tensor"),
            P("dp", None, None, "tensor"),
            P(),
            P(("dp", "tensor"), None, None),
            P(("dp", "tensor"), None, None),
            P(("dp", "tensor"), None, None),
            P(("dp", "tensor")),
            P(("dp", "tensor")),
        ),
        out_specs=(
            P(("dp", "tensor"), None, None),
            P(None, None, "tensor"),
            P(None, None, "tensor"),
        ),
        check_vma=False,
    )
```

```python
import functools
import math

import jax
import jax.numpy as jnp
from jax import lax
from jax.experimental import pallas as pl
from jax.experimental.pallas import tpu as pltpu
from jax.sharding import PartitionSpec as P

D = 5120
KVH = 8
HD = 128
QH = 32
R = 64
STEPS = 4
BF = jnp.bfloat16
F32 = jnp.float32
MIB = 1024 * 1024


def normed_rotated(keys, gain, position):
    scale = lax.rsqrt(jnp.mean(keys * keys, axis=-1, keepdims=True) + 1e-06)
    keys = keys * scale * gain
    half = keys.shape[-1] // 2
    freq = jnp.exp(
        -math.log(1000000.0) * (jnp.arange(half, dtype=jnp.float32) * 2.0 / keys.shape[-1])
    )
    angle = position.astype(jnp.float32)[..., None] * freq
    cosine = jnp.concatenate([jnp.cos(angle), jnp.cos(angle)], axis=-1)[..., None, :]
    sine = jnp.concatenate([jnp.sin(angle), jnp.sin(angle)], axis=-1)[..., None, :]
    turned = jnp.concatenate([-keys[..., half:], keys[..., :half]], axis=-1)
    return keys * cosine + turned * sine


def attend(queries, cache_keys, cache_values, new_keys, new_values, lengths):
    rows, steps, width = queries.shape
    slots = cache_keys.shape[1]
    slot = jnp.arange(slots, dtype=jnp.int32)
    for step in range(steps):
        hit = (slot[None, :] == lengths[:, None] + step)[:, :, None]
        cache_keys = jnp.where(hit, new_keys[:, step][:, None, :], cache_keys)
        cache_values = jnp.where(hit, new_values[:, step][:, None, :], cache_values)
    groups = QH // KVH
    query_five = queries.reshape(rows, steps, KVH, groups, HD)
    key_four = cache_keys.reshape(rows, slots, KVH, HD)
    value_four = cache_values.reshape(rows, slots, KVH, HD)
    scores = jnp.einsum(
        "rtkgd,rckd->rtkgc", query_five, key_four, preferred_element_type=jnp.float32
    ) * HD ** (-0.5)
    limit = lengths[:, None] + jnp.arange(steps, dtype=jnp.int32)[None, :]
    valid = (slot[None, None, :] <= limit[:, :, None])[:, :, None, None, :]
    scores = jnp.where(valid, scores, jnp.float32(-1e30))
    top = jnp.max(scores, axis=-1, keepdims=True)
    expo = jnp.exp(scores - top)
    weights = (expo / jnp.sum(expo, axis=-1, keepdims=True)).astype(jnp.bfloat16)
    result = jnp.einsum(
        "rtkgc,rckd->rtkgd", weights, value_four, preferred_element_type=jnp.float32
    )
    return result.reshape(rows, steps, width).astype(jnp.bfloat16)


def general(
    hidden_in,
    kv_weight,
    factor_a,
    factor_b,
    grad_a,
    grad_b,
    key_gain,
    queries,
    cache_keys,
    cache_values,
    cache_lengths,
    positions,
):
    groups_dp = lax.axis_size("dp")
    rate_a = 2.0 / math.sqrt(groups_dp * D)
    rate_b = 2.0 / math.sqrt(groups_dp * R)
    sum_a, sum_b = (
        lax.psum(grad_a[0].astype(jnp.bfloat16), "dp").astype(jnp.float32),
        lax.psum(grad_b[0].astype(jnp.bfloat16), "dp").astype(jnp.float32),
    )
    new_a = factor_a - rate_a * sum_a
    new_b = factor_b - rate_b * sum_b
    full_b = lax.all_gather(new_b.astype(jnp.bfloat16), "tensor", axis=2, tiled=True).astype(
        new_b.dtype
    )
    delta = jnp.einsum("prd,prk->pdk", new_a, full_b, precision=lax.Precision.HIGHEST)
    merged = (kv_weight.astype(jnp.float32) + 0.25 * delta).astype(jnp.bfloat16)
    joined = jnp.concatenate([merged[0], merged[1]], axis=1)
    rows_here = hidden_in.shape[0] // lax.axis_size("tensor")
    pieces = []
    for step in range(STEPS):
        term = jnp.dot(hidden_in[:, step, :], joined, preferred_element_type=jnp.float32)
        pieces.append(
            lax.psum_scatter(
                term.astype(jnp.bfloat16), "tensor", scatter_dimension=0, tiled=True
            ).astype(jnp.float32)
        )
    projected = jnp.stack(pieces, axis=1)
    kv_width = KVH * HD
    place = positions[:, None] + jnp.arange(STEPS, dtype=jnp.int32)[None, :]
    keys = normed_rotated(
        projected[..., :kv_width].reshape(rows_here, STEPS, KVH, HD), key_gain, place
    )
    new_keys = keys.reshape(rows_here, STEPS, kv_width).astype(jnp.bfloat16)
    new_values = projected[..., kv_width:].astype(jnp.bfloat16)
    attended = attend(queries, cache_keys, cache_values, new_keys, new_values, cache_lengths)
    return (attended, new_a, new_b)


CHUNKS = (4, 4)
GROUP = 4
HEADS_STEP = 2


def params(mib):
    return pltpu.CompilerParams(vmem_limit_bytes=mib * MIB)


def cost(flops, *arrays):
    size = sum(math.prod(x.shape) * x.dtype.itemsize for x in arrays)
    return pl.CostEstimate(flops=flops, bytes_accessed=size, transcendentals=0)


def dot(a, b):
    return jnp.dot(a, b, preferred_element_type=F32)


def dot_t(a, b):
    return lax.dot_general(a, b, (((1,), (1,)), ((), ())), preferred_element_type=F32)


def whole(shape):
    return pl.BlockSpec(shape, lambda i, *_: (0,) * len(shape))


def hbm(x):
    return pltpu.with_memory_space_constraint(x, pltpu.HBM)


TILE = 256


def multiply_terms(x, weight, base, w, sems, keys, values):
    tokens = x.shape[0] // 4
    steps = x.shape[1] // TILE
    units = (keys, values)

    def copy(p, i):
        at = pl.ds(base + i * TILE, TILE)
        return pltpu.make_async_copy(weight.at[p, :, at], w.at[p, i], sems.at[p, i])

    def start():
        for i in range(w.shape[1]):
            for p in range(2):
                copy(p, i).start()

    def multiply(*accs):
        accs = (accs[: len(keys)], accs[len(keys) :])

        @pl.loop(0, w.shape[1])
        def _(i):
            for p in range(2):
                copy(p, i).wait()

            def push(k):
                for p in range(2):
                    pltpu.matmul_push_rhs(w[p, i, k * TILE : (k + 1) * TILE, :], k % 2, p)

            push(0)
            for k in range(steps):
                if k + 1 < steps:
                    push(k + 1)
                for n in range(len(keys)):
                    for p in range(2):
                        r = units[p][n][0]
                        rows = x[r * tokens : (r + 1) * tokens, k * TILE : (k + 1) * TILE]
                        staged = k % 2 if n == 0 else None
                        pltpu.matmul_acc_lhs(accs[p][n], rows, load_staged_rhs=staged)
            at = pl.ds(pl.multiple_of(i * TILE, TILE), TILE)
            for n in range(len(keys)):
                for p in range(2):
                    _, out, row = units[p][n]
                    out[row : row + tokens, at] = pltpu.matmul_pop(accs[p][n]).astype(BF)

    def run():
        pl.run_scoped(
            multiply,
            *[pltpu.ACC(p)((tokens, TILE), F32) for p in range(2) for _ in units[p]],
        )

    return start, run


def send_parts(tokens, ksend, vsend):
    return [(3, ksend, 0), (1, ksend, tokens)], [(2, vsend, 0), (3, vsend, tokens)]


def keep_parts(tokens, kkeep, vkeep0, vkeep1):
    return [(0, kkeep, 0), (2, kkeep, tokens)], [(0, vkeep0, 0), (1, vkeep1, 0)]


def first_kernel(ids, hidden, weight, x, ksend, vsend, held, w, hidden_sems, sems):
    tokens = x.shape[0] // 4
    rows = tokens // STEPS
    start, run = multiply_terms(x, weight, 0, w, sems, *send_parts(tokens, ksend, vsend))

    def hidden_copy(r):
        at = pl.ds((ids[0] ^ r) * rows, rows)
        return pltpu.make_async_copy(hidden.at[at], held.at[r], hidden_sems.at[r])

    for r in (3, 1, 2, 0):
        hidden_copy(r).start()
    start()
    for r in (3, 1, 2, 0):
        hidden_copy(r).wait()
        x[r * tokens : (r + 1) * tokens] = held[r].reshape(tokens, x.shape[1])
    run()


def keep_kernel(x, weight, after, kkeep, vkeep0, vkeep1, _, w, sems):
    del after
    tokens = x.shape[0] // 4
    start, run = multiply_terms(x, weight, 0, w, sems, *keep_parts(tokens, kkeep, vkeep0, vkeep1))
    start()
    run()


def later_kernel(x, weight, after, *rest):
    del after
    ksend, vsend, kkeep, vkeep0, vkeep1, w, sems = rest
    tokens = x.shape[0] // 4
    sends = send_parts(tokens, ksend, vsend)
    keeps = keep_parts(tokens, kkeep, vkeep0, vkeep1)
    base = weight.shape[2] - w.shape[1] * TILE
    parts = [a + b for a, b in zip(sends, keeps)]
    start, run = multiply_terms(x, weight, base, w, sems, *parts)
    start()
    run()


SEND, KEEP = (2, 2), (2, 1, 1)


def term_shapes(rows, tokens, count):
    return [jax.ShapeDtypeStruct((n * tokens, count * HD), BF) for n in rows]


def weight_scratch(width, count):
    tiles = count * HD // TILE
    return [pltpu.VMEM((2, tiles, width, TILE), BF), pltpu.SemaphoreType.DMA((2, tiles))]


def first_terms(ids, hidden, kv_weight, tokens):
    width = hidden.shape[2]
    here = pl.BlockSpec(memory_space=pl.ANY)
    outs = [jax.ShapeDtypeStruct((4 * tokens, width), BF)]
    outs += [pltpu.VMEM(x.shape, BF) for x in term_shapes(SEND, tokens, CHUNKS[0])]
    w, sems = weight_scratch(width, CHUNKS[0])
    return pl.pallas_call(
        first_kernel,
        out_shape=outs,
        grid_spec=pltpu.PrefetchScalarGridSpec(
            num_scalar_prefetch=1,
            grid=(1,),
            in_specs=[here] * 2,
            out_specs=[whole(x.shape) for x in outs],
            scratch_shapes=[
                pltpu.VMEM((4, tokens // STEPS, STEPS, width), BF),
                w,
                pltpu.SemaphoreType.DMA((4,)),
                sems,
            ],
        ),
        compiler_params=params(16),
        cost_estimate=cost(8 * tokens * width * CHUNKS[0] * HD, hidden),
        name="first_terms",
    )(ids, *map(hbm, (hidden, kv_weight)))


def keep_terms(x, kv_weight, queries, after):
    tokens, width = x.shape[0] // 4, x.shape[1]
    here = pl.BlockSpec(memory_space=pl.ANY)
    outs = [pltpu.HBM(out.shape, BF) for out in term_shapes(KEEP, tokens, CHUNKS[0])]
    specs = [whole(out.shape) for out in outs] + [here]
    outs.append(jax.ShapeDtypeStruct(queries.shape, BF))
    return pl.pallas_call(
        keep_kernel,
        out_shape=outs,
        grid=(1,),
        in_specs=[whole(x.shape), here, here],
        out_specs=specs,
        scratch_shapes=weight_scratch(width, CHUNKS[0]),
        compiler_params=params(14),
        cost_estimate=cost(8 * tokens * width * CHUNKS[0] * HD, x),
        name="keep_terms",
    )(x, hbm(kv_weight), after)


def later_terms(x, kv_weight, after):
    outs = term_shapes(SEND + KEEP, x.shape[0] // 4, CHUNKS[1])
    here = pl.BlockSpec(memory_space=pl.ANY)
    return pl.pallas_call(
        later_kernel,
        out_shape=outs,
        grid=(1,),
        in_specs=[whole(x.shape), here, here],
        out_specs=[whole(out.shape) for out in outs],
        scratch_shapes=weight_scratch(x.shape[1], CHUNKS[1]),
        compiler_params=params(12),
        cost_estimate=cost(4 * math.prod(x.shape) * CHUNKS[1] * HD, x, *outs),
        name="later_terms",
    )(x, hbm(kv_weight), after)


def mid_kernel(kkeep, kcame, vkeep, vcame, *rest):
    kout, vout = rest[-2:]
    kout[...] = (kkeep[...].astype(F32) + kcame[...].astype(F32)).astype(BF)
    vout[...] = (vkeep[...].astype(F32) + vcame[...].astype(F32)).astype(BF)


def mid_sums(kkeep, kcame, vkeep, vcame, *after):
    shape = vkeep.shape
    low = pl.BlockSpec(shape, lambda i: (0, 0))
    high = pl.BlockSpec(shape, lambda i: (1, 0))
    return pl.pallas_call(
        mid_kernel,
        out_shape=[jax.ShapeDtypeStruct(shape, BF)] * 2,
        grid=(1,),
        in_specs=[high, low, low, high] + [pl.BlockSpec(memory_space=pl.ANY)] * len(after),
        out_specs=[low, low],
        compiler_params=params(4),
        cost_estimate=cost(0, *[vkeep] * 6),
        name="mid_sums",
    )(kkeep, kcame, vkeep, vcame, *after)


def pack_kernel(ids, grad_a, grad_b, after, out):
    del ids, after
    wide = grad_a.shape[-1]
    out[:, :wide] = grad_a[0, 0].astype(BF)
    out[:, wide:] = grad_b[0, 0].astype(BF)


def chip_kernel(ids, grad_a, grad_b, other, out):
    del ids
    wide = grad_a.shape[-1]
    out[:, :wide] = (grad_a[0, 0] + other[:, :wide].astype(F32)).astype(BF)
    out[:, wide:] = (grad_b[0, 0] + other[:, wide:].astype(F32)).astype(BF)


def grad_half(kernel, name, ids, grad_a, grad_b, flip, more, spec):
    rank, wide = grad_a.shape[2], grad_a.shape[3] + grad_b.shape[3]

    def half(x):
        return pl.BlockSpec((1, 1) + x.shape[2:], lambda i, ids: (0, ids[2] ^ flip, 0, 0))

    out = jax.ShapeDtypeStruct((rank, wide), BF)
    return pl.pallas_call(
        kernel,
        out_shape=out,
        grid_spec=pltpu.PrefetchScalarGridSpec(
            num_scalar_prefetch=1,
            grid=(1,),
            in_specs=[half(grad_a), half(grad_b), spec],
            out_specs=whole(out.shape),
        ),
        compiler_params=params(4),
        cost_estimate=cost(0, *[out] * 4),
        name=name,
    )(ids, hbm(grad_a), hbm(grad_b), more)


def small_call(kernel, name, ids, args, outs, after=(), scratch=(), copied=0):
    count = len(args)

    def body(ids, *refs):
        kernel(ids, *refs[:count], *refs[count + len(after) :])

    return pl.pallas_call(
        body,
        out_shape=outs,
        grid_spec=pltpu.PrefetchScalarGridSpec(
            num_scalar_prefetch=1,
            grid=(1,),
            in_specs=[whole(x.shape) for x in args]
            + [pl.BlockSpec(memory_space=pl.ANY)] * len(after),
            out_specs=[pl.BlockSpec(memory_space=pltpu.HBM)] * copied
            + [whole(x.shape) for x in outs[copied:]],
            scratch_shapes=list(scratch),
        ),
        compiler_params=params(8),
        cost_estimate=cost(0, *args),
        name=name,
    )(ids, *args, *after)


def core_flip(x, count):
    return lax.ppermute(x, "dp", [(i, i ^ 1) for i in range(count)])


def plus_kernel(a, b, *rest):
    rest[-1][...] = (a[...].astype(F32) + b[...].astype(F32)).astype(BF)


def plus(a, b, *after):
    out = jax.ShapeDtypeStruct(a.shape, BF)
    return pl.pallas_call(
        plus_kernel,
        out_shape=out,
        grid=(1,),
        in_specs=[whole(a.shape)] * 2 + [pl.BlockSpec(memory_space=pl.ANY)] * len(after),
        out_specs=whole(a.shape),
        compiler_params=params(2),
        cost_estimate=cost(0, a, b, out),
        name="plus",
    )(a, b, *after)


def along_line(x, d, count):
    return lax.ppermute(x, "dp", [(i, i ^ (2 * d)) for i in range(count)])


TOP = 2 * R


def update_kernel(rates, ids, half, other, factor_a, factor_b, x, out_a, out_b, *rest):
    *sends, a, new_a, new_b, sems = rest
    copies = [
        pltpu.make_async_copy(new_a, out_a, sems.at[0]),
        pltpu.make_async_copy(new_b, out_b, sems.at[1]),
    ]
    wide = factor_a.shape[-1]
    for index, part in ((ids[2], half), (ids[2] ^ 1, other)):
        new_a[index] = factor_a[index] - rates[0] * part[:, :wide].astype(F32)
        new_b[index] = factor_b[index] - rates[1] * part[:, wide:].astype(F32)
    for copy in copies:
        copy.start()
    for p in range(2):
        a[p * R : (p + 1) * R] = new_a[p].astype(BF)
    a[TOP:] = jnp.zeros((TILE - TOP, wide), BF)
    tokens = x.shape[0] // 4

    def multiply(*accs):
        steps = wide // TILE

        def push(k):
            for unit in range(2):
                tile = a[:, k * TILE : (k + 1) * TILE]
                pltpu.matmul_push_rhs(tile, k % 2, unit, transpose=True)

        push(0)
        for k in range(steps):
            if k + 1 < steps:
                push(k + 1)
            for r in range(4):
                rows = x[r * tokens : (r + 1) * tokens, k * TILE : (k + 1) * TILE]
                staged = k % 2 if r < 2 else None
                pltpu.matmul_acc_lhs(accs[r], rows, load_staged_rhs=staged)
        for r, send in enumerate(sends):
            u = (0.25 * pltpu.matmul_pop(accs[r])[:, :TOP]).astype(BF)
            for p in range(2):
                send[p * R : (p + 1) * R, :] = new_b[p].astype(BF)
            send[TOP:, :TOP] = u[:TOP]
            send[TOP:tokens, TOP:] = u[TOP:]
            send[tokens:, TOP:] = jnp.zeros((2 * TOP - tokens, TOP), BF)

    pl.run_scoped(multiply, *[pltpu.ACC(r % 2)((tokens, TILE), F32) for r in range(4)])
    for copy in copies:
        copy.wait()


def updated(ids, half, other, factor_a, factor_b, x, dp, *after):
    rates = (2.0 / math.sqrt(dp * D), 2.0 / math.sqrt(dp * R))
    outs = [pltpu.HBM(f.shape, F32) for f in (factor_a, factor_b)]
    outs += [jax.ShapeDtypeStruct((2 * TOP, 2 * TOP), BF)] * 4
    return small_call(
        functools.partial(update_kernel, rates),
        "update_factors",
        ids,
        (half, other, factor_a, factor_b, x),
        outs,
        after,
        [
            pltpu.VMEM((TILE, factor_a.shape[-1]), BF),
            pltpu.VMEM(factor_a.shape, F32),
            pltpu.VMEM(factor_b.shape, F32),
            pltpu.SemaphoreType.DMA((2,)),
        ],
        2,
    )


def attend_kernel(ids, first, lengths, *refs):
    q, cache_k, cache_v, k0, k1, k2, v0, v1, v2, *ub, cosine, sine = refs[:15]
    out = refs[-3]
    rows, slots, _ = cache_k.shape
    tokens = rows * STEPS
    u_held, b_held = refs[-2:]

    @pl.when(pl.program_id(0) == 0)
    def _():
        u_held[:TOP] = sum(x[TOP:, :TOP].astype(F32) for x in ub).astype(BF)
        u_held[TOP:] = sum(x[TOP:tokens, TOP:].astype(F32) for x in ub).astype(BF)

    rel = ids[0] ^ (first[0] + pl.program_id(0))
    for r, x in enumerate(ub):

        @pl.when(rel == r)
        def _():
            b_held[...] = x[:TOP]

    u, b = u_held[...], b_held[...]
    k = k0[...].astype(F32) + k1[...].astype(F32) + k2[...].astype(F32) + dot(u[:, :R], b[:R])
    v = v0[...].astype(F32) + v1[...].astype(F32) + v2[...].astype(F32) + dot(u[:, R:], b[R:])
    v = v.astype(BF)
    keys = []
    for n in range(HEADS_STEP):
        key = k[:, n * HD : (n + 1) * HD]
        scale = lax.rsqrt(jnp.sum(key * key, axis=-1, keepdims=True) * (1.0 / HD) + 1e-06)
        key = scale * (key * cosine[...] + pltpu.roll(key, HD // 2, 1) * sine[...])
        keys.append(key.astype(BF))
    n_q, n_c = GROUP * STEPS, GROUP * slots
    shape = (n_q, n_c + n_q)
    here = lax.broadcasted_iota(jnp.int32, shape, 0)
    col = lax.broadcasted_iota(jnp.int32, shape, 1)
    fresh = col - n_c
    cached = (col < n_c) & (here // STEPS == col // slots)
    new = (col >= n_c) & (here // STEPS == fresh // STEPS) & (fresh % STEPS <= here % STEPS)
    bias_here = jnp.where(cached | new, 0.0, -1e30)
    col = lax.broadcasted_iota(jnp.int32, (1, n_c + n_q), 1)
    ones = jnp.ones((n_c + n_q, HD), BF)
    factor = math.log2(math.e) * HD**-0.5
    heads = QH // KVH
    blocks = rows // GROUP
    query = q[...].reshape(tokens, HEADS_STEP * heads * HD)

    def block(n, g, cache, fresh):
        old = cache[g * GROUP : (g + 1) * GROUP, :, n * HD : (n + 1) * HD].reshape(n_c, HD)
        return jnp.concatenate([old, fresh[g * n_q : (g + 1) * n_q]], axis=0)

    every = [(n, g) for n in range(HEADS_STEP) for g in range(blocks)]
    scores = []
    for n, g in every:
        part = [query[g * n_q : (g + 1) * n_q, h * HD : (h + 1) * HD] for h in range(n * heads, (n + 1) * heads)]
        scores.append(dot_t(jnp.concatenate(part, axis=0), block(n, g, cache_k, keys[n])))
    biases = []
    for g in range(blocks):
        filled = jnp.full(col.shape, lengths[g * GROUP], jnp.int32)
        for i in range(1, GROUP):
            filled = jnp.where(col // slots == i, lengths[g * GROUP + i], filled)
        bias = jnp.where((col >= n_c) | (col % slots < filled), 0.0, -1e30) + bias_here
        biases.append(jnp.concatenate([bias] * heads, axis=0))
    weights = []
    for (n, g), s in zip(every, scores):
        s = s * factor + biases[g]
        top = jnp.max(s, axis=-1, keepdims=True)
        weights.append(jnp.exp2(s - top).astype(BF))
    results = []
    for (n, g), w in zip(every, weights):
        here_v = block(n, g, cache_v, v[:, n * HD : (n + 1) * HD])
        r = dot(w, jnp.concatenate([here_v, ones], axis=1))
        total = r[:, HD:]
        inverse = pl.reciprocal(total, approx=True)
        inverse = inverse * (2.0 - total * inverse)
        results.append((r[:, :HD] * inverse).astype(BF))
    for n in range(HEADS_STEP):
        for h in range(heads):
            part = [r[h * n_q : (h + 1) * n_q] for r in results[n * blocks : (n + 1) * blocks]]
            at = (n * heads + h) * HD
            out[:, :, at : at + HD] = jnp.concatenate(part, axis=0).reshape(rows, STEPS, HD)


def attend_chunk(
    ids, lengths, start, count, queries, cache_keys, cache_values, terms, ub, tables, before
):
    rows, slots, _ = cache_keys.shape
    tokens = rows * STEPS
    heads = QH // KVH
    args = [queries, cache_keys, cache_values, *terms, *ub, *tables]
    assert start % HEADS_STEP == 0 and count % HEADS_STEP == 0
    first = jnp.full((1,), start // HEADS_STEP, jnp.int32)
    size = HEADS_STEP * HD
    part = pl.BlockSpec((tokens, size), lambda i, *_: (0, i))
    low = pl.BlockSpec((tokens, size), lambda i, *_: (1, i))
    cache = pl.BlockSpec((rows, slots, size), lambda i, _, first, *__: (0, 0, first[0] + i))
    wide = pl.BlockSpec((rows, STEPS, heads * size), lambda i, _, first, *__: (0, 0, first[0] + i))
    specs = [wide, cache, cache, part, low, part, part, part, part]
    specs += [whole(x.shape) for x in (*ub, *tables)]
    args.append(before)
    specs.append(pl.BlockSpec(memory_space=pl.ANY))
    return pl.pallas_call(
        attend_kernel,
        out_shape=jax.ShapeDtypeStruct(queries.shape, BF),
        grid_spec=pltpu.PrefetchScalarGridSpec(
            num_scalar_prefetch=3, grid=(count // HEADS_STEP,), in_specs=specs, out_specs=wide,
            scratch_shapes=[pltpu.VMEM((tokens, TOP), BF), pltpu.VMEM((TOP, size), BF)],
        ),
        input_output_aliases={len(args) + 2: 0},
        compiler_params=params(14),
        cost_estimate=cost(count * 4 * 10**9, *args),
        name="attend_chunk",
    )(ids, first, lengths, *args)


def rotary_tables(key_gain, positions):
    half = HD // 2
    place = positions[:, None] + jnp.arange(STEPS, dtype=jnp.int32)[None, :]
    freq = jnp.exp(-math.log(1000000.0) * (jnp.arange(half, dtype=F32) * 2.0 / HD))
    angle = place.reshape(-1).astype(F32)[:, None] * jnp.concatenate([freq, freq])
    turned = jnp.concatenate([-key_gain[half:], key_gain[:half]])
    return jnp.cos(angle) * key_gain, jnp.sin(angle) * turned


def across(x, r):
    return lax.ppermute(x, "tensor", [(i, i ^ r) for i in range(4)])


def square(
    hidden_in,
    kv_weight,
    factor_a,
    factor_b,
    grad_a,
    grad_b,
    key_gain,
    queries,
    cache_keys,
    cache_values,
    cache_lengths,
    positions,
):
    tokens = cache_keys.shape[0] * STEPS
    count_dp = lax.axis_size("dp")
    dp = lax.axis_index("dp")
    ids = jnp.stack([lax.axis_index("tensor"), dp // 2, dp % 2]).astype(jnp.int32)
    tables = rotary_tables(key_gain, positions)

    x, *first = first_terms(ids, hidden_in, kv_weight, tokens)
    here = pl.BlockSpec(memory_space=pl.ANY)
    packed = grad_half(pack_kernel, "pack_grads", ids, grad_a, grad_b, 1, first[0], here)
    other = core_flip(packed, count_dp)
    half = grad_half(
        chip_kernel, "chip_grads", ids, grad_a, grad_b, 0, other, whole(other.shape)
    )

    def first_exchange(term, *after):
        ksend, vsend, kkeep, vkeep0, vkeep1 = term
        kcame, vcame = across(ksend, 1), across(vsend, 2)
        mids = mid_sums(kkeep, kcame, vkeep1, vcame, *after)
        return mids, (kkeep, kcame, vkeep0, vcame)

    def second_exchange(mids, parts):
        kkeep, kcame, vkeep0, vcame = parts
        return kkeep, kcame, across(mids[0], 2), vkeep0, vcame, across(mids[1], 1)

    second = later_terms(x, kv_weight, half)
    step, after = 1, second[:1]
    while 2 * step < count_dp:
        half = plus(half, along_line(half, step, count_dp), *after)
        step *= 2
        if step == 2:
            *keeps, attended = keep_terms(x, kv_weight, queries, half)
            first += keeps
            mids, parts = first_exchange(first, half)
            after = (mids[0], tables[0])
    if step == 1:
        *keeps, attended = keep_terms(x, kv_weight, queries, half)
        first += keeps
        mids, parts = first_exchange(first, half)
    first = second_exchange(mids, parts)
    other = core_flip(half, count_dp)
    new_a, new_b, *sends = updated(
        ids, half, other, factor_a, factor_b, x, count_dp
    )
    ub = [sends[0]] + [across(sends[r], r) for r in (1, 2, 3)]
    second = second_exchange(*first_exchange(second, *ub[1:]))
    for start, count, came in ((0, CHUNKS[0], first), (CHUNKS[0], CHUNKS[1], second)):
        attended = attend_chunk(
            ids,
            cache_lengths,
            start,
            count,
            queries,
            cache_keys,
            cache_values,
            came,
            ub,
            tables,
            attended,
        )
    return attended, new_a, new_b


def solution(mesh):
    fits = mesh.shape["tensor"] == 4 and mesh.shape["dp"] in (2, 4, 8)
    return jax.shard_map(
        square if fits else general,
        mesh=mesh,
        in_specs=(
            P("dp", None, "tensor"),
            P(None, "tensor", None),
            P(None, None, "tensor"),
            P(None, None, "tensor"),
            P("dp", None, None, "tensor"),
            P("dp", None, None, "tensor"),
            P(),
            P(("dp", "tensor"), None, None),
            P(("dp", "tensor"), None, None),
            P(("dp", "tensor"), None, None),
            P(("dp", "tensor")),
            P(("dp", "tensor")),
        ),
        out_specs=(
            P(("dp", "tensor"), None, None),
            P(None, None, "tensor"),
            P(None, None, "tensor"),
        ),
        check_vma=False,
    )
```

```python
import functools
import math

import jax
import jax.numpy as jnp
from jax import lax
from jax.experimental import pallas as pl
from jax.experimental.pallas import tpu as pltpu
from jax.sharding import PartitionSpec as P

D = 5120
KVH = 8
HD = 128
QH = 32
R = 64
STEPS = 4
BF = jnp.bfloat16
F32 = jnp.float32
MIB = 1024 * 1024


def normed_rotated(keys, gain, position):
    scale = lax.rsqrt(jnp.mean(keys * keys, axis=-1, keepdims=True) + 1e-06)
    keys = keys * scale * gain
    half = keys.shape[-1] // 2
    freq = jnp.exp(
        -math.log(1000000.0) * (jnp.arange(half, dtype=jnp.float32) * 2.0 / keys.shape[-1])
    )
    angle = position.astype(jnp.float32)[..., None] * freq
    cosine = jnp.concatenate([jnp.cos(angle), jnp.cos(angle)], axis=-1)[..., None, :]
    sine = jnp.concatenate([jnp.sin(angle), jnp.sin(angle)], axis=-1)[..., None, :]
    turned = jnp.concatenate([-keys[..., half:], keys[..., :half]], axis=-1)
    return keys * cosine + turned * sine


def attend(queries, cache_keys, cache_values, new_keys, new_values, lengths):
    rows, steps, width = queries.shape
    slots = cache_keys.shape[1]
    slot = jnp.arange(slots, dtype=jnp.int32)
    for step in range(steps):
        hit = (slot[None, :] == lengths[:, None] + step)[:, :, None]
        cache_keys = jnp.where(hit, new_keys[:, step][:, None, :], cache_keys)
        cache_values = jnp.where(hit, new_values[:, step][:, None, :], cache_values)
    groups = QH // KVH
    query_five = queries.reshape(rows, steps, KVH, groups, HD)
    key_four = cache_keys.reshape(rows, slots, KVH, HD)
    value_four = cache_values.reshape(rows, slots, KVH, HD)
    scores = jnp.einsum(
        "rtkgd,rckd->rtkgc", query_five, key_four, preferred_element_type=jnp.float32
    ) * HD ** (-0.5)
    limit = lengths[:, None] + jnp.arange(steps, dtype=jnp.int32)[None, :]
    valid = (slot[None, None, :] <= limit[:, :, None])[:, :, None, None, :]
    scores = jnp.where(valid, scores, jnp.float32(-1e30))
    top = jnp.max(scores, axis=-1, keepdims=True)
    expo = jnp.exp(scores - top)
    weights = (expo / jnp.sum(expo, axis=-1, keepdims=True)).astype(jnp.bfloat16)
    result = jnp.einsum(
        "rtkgc,rckd->rtkgd", weights, value_four, preferred_element_type=jnp.float32
    )
    return result.reshape(rows, steps, width).astype(jnp.bfloat16)


def general(
    hidden_in,
    kv_weight,
    factor_a,
    factor_b,
    grad_a,
    grad_b,
    key_gain,
    queries,
    cache_keys,
    cache_values,
    cache_lengths,
    positions,
):
    groups_dp = lax.axis_size("dp")
    rate_a = 2.0 / math.sqrt(groups_dp * D)
    rate_b = 2.0 / math.sqrt(groups_dp * R)
    sum_a, sum_b = (
        lax.psum(grad_a[0].astype(jnp.bfloat16), "dp").astype(jnp.float32),
        lax.psum(grad_b[0].astype(jnp.bfloat16), "dp").astype(jnp.float32),
    )
    new_a = factor_a - rate_a * sum_a
    new_b = factor_b - rate_b * sum_b
    full_b = lax.all_gather(new_b.astype(jnp.bfloat16), "tensor", axis=2, tiled=True).astype(
        new_b.dtype
    )
    delta = jnp.einsum("prd,prk->pdk", new_a, full_b, precision=lax.Precision.HIGHEST)
    merged = (kv_weight.astype(jnp.float32) + 0.25 * delta).astype(jnp.bfloat16)
    joined = jnp.concatenate([merged[0], merged[1]], axis=1)
    rows_here = hidden_in.shape[0] // lax.axis_size("tensor")
    pieces = []
    for step in range(STEPS):
        term = jnp.dot(hidden_in[:, step, :], joined, preferred_element_type=jnp.float32)
        pieces.append(
            lax.psum_scatter(
                term.astype(jnp.bfloat16), "tensor", scatter_dimension=0, tiled=True
            ).astype(jnp.float32)
        )
    projected = jnp.stack(pieces, axis=1)
    kv_width = KVH * HD
    place = positions[:, None] + jnp.arange(STEPS, dtype=jnp.int32)[None, :]
    keys = normed_rotated(
        projected[..., :kv_width].reshape(rows_here, STEPS, KVH, HD), key_gain, place
    )
    new_keys = keys.reshape(rows_here, STEPS, kv_width).astype(jnp.bfloat16)
    new_values = projected[..., kv_width:].astype(jnp.bfloat16)
    attended = attend(queries, cache_keys, cache_values, new_keys, new_values, cache_lengths)
    return (attended, new_a, new_b)


CHUNKS = (4, 4)
GROUP = 4
HEADS_STEP = 2


def params(mib):
    return pltpu.CompilerParams(vmem_limit_bytes=mib * MIB)


def cost(flops, *arrays):
    size = sum(math.prod(x.shape) * x.dtype.itemsize for x in arrays)
    return pl.CostEstimate(flops=flops, bytes_accessed=size, transcendentals=0)


def dot(a, b):
    return jnp.dot(a, b, preferred_element_type=F32)


def dot_t(a, b):
    return lax.dot_general(a, b, (((1,), (1,)), ((), ())), preferred_element_type=F32)


def whole(shape):
    return pl.BlockSpec(shape, lambda i, *_: (0,) * len(shape))


def hbm(x):
    return pltpu.with_memory_space_constraint(x, pltpu.HBM)


TILE = 256


def multiply_terms(x, weight, base, w, sems, keys, values):
    tokens = x.shape[0] // 4
    steps = x.shape[1] // TILE
    units = (keys, values)

    def copy(p, i):
        at = pl.ds(base + i * TILE, TILE)
        return pltpu.make_async_copy(weight.at[p, :, at], w.at[p, i], sems.at[p, i])

    def start():
        for i in range(w.shape[1]):
            for p in range(2):
                copy(p, i).start()

    def multiply(*accs):
        accs = (accs[: len(keys)], accs[len(keys) :])

        @pl.loop(0, w.shape[1])
        def _(i):
            for p in range(2):
                copy(p, i).wait()

            def push(k):
                for p in range(2):
                    pltpu.matmul_push_rhs(w[p, i, k * TILE : (k + 1) * TILE, :], k % 2, p)

            push(0)
            for k in range(steps):
                if k + 1 < steps:
                    push(k + 1)
                for n in range(len(keys)):
                    for p in range(2):
                        r = units[p][n][0]
                        rows = x[r * tokens : (r + 1) * tokens, k * TILE : (k + 1) * TILE]
                        staged = k % 2 if n == 0 else None
                        pltpu.matmul_acc_lhs(accs[p][n], rows, load_staged_rhs=staged)
            at = pl.ds(pl.multiple_of(i * TILE, TILE), TILE)
            for n in range(len(keys)):
                for p in range(2):
                    _, out, row = units[p][n]
                    out[row : row + tokens, at] = pltpu.matmul_pop(accs[p][n]).astype(BF)

    def run():
        pl.run_scoped(
            multiply,
            *[pltpu.ACC(p)((tokens, TILE), F32) for p in range(2) for _ in units[p]],
        )

    return start, run


def send_parts(tokens, ksend, vsend):
    return [(3, ksend, 0), (1, ksend, tokens)], [(2, vsend, 0), (3, vsend, tokens)]


def keep_parts(tokens, kkeep, vkeep0, vkeep1):
    return [(0, kkeep, 0), (2, kkeep, tokens)], [(0, vkeep0, 0), (1, vkeep1, 0)]


def first_kernel(ids, hidden, weight, grad_a, grad_b, x, ksend, vsend, packed, *scratch):
    held, w, held_a, held_b, hidden_sems, sems, grad_sems = scratch
    tokens = x.shape[0] // 4
    rows = tokens // STEPS
    start, run = multiply_terms(x, weight, 0, w, sems, *send_parts(tokens, ksend, vsend))

    def hidden_copy(r):
        at = pl.ds((ids[0] ^ r) * rows, rows)
        return pltpu.make_async_copy(hidden.at[at], held.at[r], hidden_sems.at[r])

    grads = [
        pltpu.make_async_copy(grad_a.at[0, ids[2] ^ 1], held_a, grad_sems.at[0]),
        pltpu.make_async_copy(grad_b.at[0, ids[2] ^ 1], held_b, grad_sems.at[1]),
    ]
    for copy in grads:
        copy.start()
    for r in (3, 1, 2, 0):
        hidden_copy(r).start()
    start()
    for copy in grads:
        copy.wait()
    wide = grad_a.shape[-1]
    packed[:, :wide] = held_a[...].astype(BF)
    packed[:, wide:] = held_b[...].astype(BF)
    for r in (3, 1, 2, 0):
        hidden_copy(r).wait()
        x[r * tokens : (r + 1) * tokens] = held[r].reshape(tokens, x.shape[1])
    run()


def keep_kernel(x, weight, after, kkeep, vkeep0, vkeep1, _, w, sems):
    del after
    tokens = x.shape[0] // 4
    start, run = multiply_terms(x, weight, 0, w, sems, *keep_parts(tokens, kkeep, vkeep0, vkeep1))
    start()
    run()


def later_kernel(x, weight, after, *rest):
    del after
    ksend, vsend, kkeep, vkeep0, vkeep1, w, sems = rest
    tokens = x.shape[0] // 4
    sends = send_parts(tokens, ksend, vsend)
    keeps = keep_parts(tokens, kkeep, vkeep0, vkeep1)
    base = weight.shape[2] - w.shape[1] * TILE
    parts = [a + b for a, b in zip(sends, keeps)]
    start, run = multiply_terms(x, weight, base, w, sems, *parts)
    start()
    run()


SEND, KEEP = (2, 2), (2, 1, 1)


def term_shapes(rows, tokens, count):
    return [jax.ShapeDtypeStruct((n * tokens, count * HD), BF) for n in rows]


def weight_scratch(width, count):
    tiles = count * HD // TILE
    return [pltpu.VMEM((2, tiles, width, TILE), BF), pltpu.SemaphoreType.DMA((2, tiles))]


def first_terms(ids, hidden, kv_weight, grad_a, grad_b, tokens):
    width = hidden.shape[2]
    here = pl.BlockSpec(memory_space=pl.ANY)
    outs = [jax.ShapeDtypeStruct((4 * tokens, width), BF)]
    outs += [pltpu.VMEM(x.shape, BF) for x in term_shapes(SEND, tokens, CHUNKS[0])]
    outs.append(jax.ShapeDtypeStruct((grad_a.shape[2], grad_a.shape[3] + grad_b.shape[3]), BF))
    w, sems = weight_scratch(width, CHUNKS[0])
    return pl.pallas_call(
        first_kernel,
        out_shape=outs,
        grid_spec=pltpu.PrefetchScalarGridSpec(
            num_scalar_prefetch=1,
            grid=(1,),
            in_specs=[here] * 4,
            out_specs=[whole(x.shape) for x in outs],
            scratch_shapes=[
                pltpu.VMEM((4, tokens // STEPS, STEPS, width), BF),
                w,
                pltpu.VMEM(grad_a.shape[2:], F32),
                pltpu.VMEM(grad_b.shape[2:], F32),
                pltpu.SemaphoreType.DMA((4,)),
                sems,
                pltpu.SemaphoreType.DMA((2,)),
            ],
        ),
        compiler_params=params(16),
        cost_estimate=cost(8 * tokens * width * CHUNKS[0] * HD, hidden),
        name="first_terms",
    )(ids, *map(hbm, (hidden, kv_weight, grad_a, grad_b)))


def keep_terms(x, kv_weight, queries, after):
    tokens, width = x.shape[0] // 4, x.shape[1]
    here = pl.BlockSpec(memory_space=pl.ANY)
    outs = [pltpu.HBM(out.shape, BF) for out in term_shapes(KEEP, tokens, CHUNKS[0])]
    specs = [whole(out.shape) for out in outs] + [here]
    outs.append(jax.ShapeDtypeStruct(queries.shape, BF))
    return pl.pallas_call(
        keep_kernel,
        out_shape=outs,
        grid=(1,),
        in_specs=[whole(x.shape), here, here],
        out_specs=specs,
        scratch_shapes=weight_scratch(width, CHUNKS[0]),
        compiler_params=params(14),
        cost_estimate=cost(8 * tokens * width * CHUNKS[0] * HD, x),
        name="keep_terms",
    )(x, hbm(kv_weight), after)


def later_terms(x, kv_weight, after):
    outs = term_shapes(SEND + KEEP, x.shape[0] // 4, CHUNKS[1])
    here = pl.BlockSpec(memory_space=pl.ANY)
    return pl.pallas_call(
        later_kernel,
        out_shape=outs,
        grid=(1,),
        in_specs=[whole(x.shape), here, here],
        out_specs=[whole(out.shape) for out in outs],
        scratch_shapes=weight_scratch(x.shape[1], CHUNKS[1]),
        compiler_params=params(12),
        cost_estimate=cost(4 * math.prod(x.shape) * CHUNKS[1] * HD, x, *outs),
        name="later_terms",
    )(x, hbm(kv_weight), after)


def mid_kernel(kkeep, kcame, vkeep, vcame, *rest):
    kout, vout = rest[-2:]
    kout[...] = (kkeep[...].astype(F32) + kcame[...].astype(F32)).astype(BF)
    vout[...] = (vkeep[...].astype(F32) + vcame[...].astype(F32)).astype(BF)


def mid_sums(kkeep, kcame, vkeep, vcame, *after):
    shape = vkeep.shape
    low = pl.BlockSpec(shape, lambda i: (0, 0))
    high = pl.BlockSpec(shape, lambda i: (1, 0))
    return pl.pallas_call(
        mid_kernel,
        out_shape=[jax.ShapeDtypeStruct(shape, BF)] * 2,
        grid=(1,),
        in_specs=[high, low, low, high] + [pl.BlockSpec(memory_space=pl.ANY)] * len(after),
        out_specs=[low, low],
        compiler_params=params(4),
        cost_estimate=cost(0, *[vkeep] * 6),
        name="mid_sums",
    )(kkeep, kcame, vkeep, vcame, *after)


def chip_kernel(ids, grad_a, grad_b, other, out):
    del ids
    wide = grad_a.shape[-1]
    out[:, :wide] = (grad_a[0, 0] + other[:, :wide].astype(F32)).astype(BF)
    out[:, wide:] = (grad_b[0, 0] + other[:, wide:].astype(F32)).astype(BF)


def chip_grads(ids, grad_a, grad_b, other):
    def half(x):
        return pl.BlockSpec((1, 1) + x.shape[2:], lambda i, ids: (0, ids[2], 0, 0))

    return pl.pallas_call(
        chip_kernel,
        out_shape=jax.ShapeDtypeStruct(other.shape, BF),
        grid_spec=pltpu.PrefetchScalarGridSpec(
            num_scalar_prefetch=1,
            grid=(1,),
            in_specs=[half(grad_a), half(grad_b), whole(other.shape)],
            out_specs=whole(other.shape),
        ),
        compiler_params=params(4),
        cost_estimate=cost(0, *[other] * 4),
        name="chip_grads",
    )(ids, hbm(grad_a), hbm(grad_b), other)


def small_call(kernel, name, ids, args, outs, after=(), scratch=(), copied=0):
    count = len(args)

    def body(ids, *refs):
        kernel(ids, *refs[:count], *refs[count + len(after) :])

    return pl.pallas_call(
        body,
        out_shape=outs,
        grid_spec=pltpu.PrefetchScalarGridSpec(
            num_scalar_prefetch=1,
            grid=(1,),
            in_specs=[whole(x.shape) for x in args]
            + [pl.BlockSpec(memory_space=pl.ANY)] * len(after),
            out_specs=[pl.BlockSpec(memory_space=pltpu.HBM)] * copied
            + [whole(x.shape) for x in outs[copied:]],
            scratch_shapes=list(scratch),
        ),
        compiler_params=params(8),
        cost_estimate=cost(0, *args),
        name=name,
    )(ids, *args, *after)


def core_flip(x, count):
    return lax.ppermute(x, "dp", [(i, i ^ 1) for i in range(count)])


def plus_kernel(a, b, *rest):
    rest[-1][...] = (a[...].astype(F32) + b[...].astype(F32)).astype(BF)


def plus(a, b, *after):
    out = jax.ShapeDtypeStruct(a.shape, BF)
    return pl.pallas_call(
        plus_kernel,
        out_shape=out,
        grid=(1,),
        in_specs=[whole(a.shape)] * 2 + [pl.BlockSpec(memory_space=pl.ANY)] * len(after),
        out_specs=whole(a.shape),
        compiler_params=params(2),
        cost_estimate=cost(0, a, b, out),
        name="plus",
    )(a, b, *after)


def along_line(x, d, count):
    return lax.ppermute(x, "dp", [(i, i ^ (2 * d)) for i in range(count)])


TOP = 2 * R


def update_kernel(rates, ids, half, other, factor_a, factor_b, x, out_a, out_b, *rest):
    *sends, a, new_a, new_b, sems = rest
    copies = [
        pltpu.make_async_copy(new_a, out_a, sems.at[0]),
        pltpu.make_async_copy(new_b, out_b, sems.at[1]),
    ]
    wide = factor_a.shape[-1]
    for index, part in ((ids[2], half), (ids[2] ^ 1, other)):
        new_a[index] = factor_a[index] - rates[0] * part[:, :wide].astype(F32)
        new_b[index] = factor_b[index] - rates[1] * part[:, wide:].astype(F32)
    for copy in copies:
        copy.start()
    for p in range(2):
        a[p * R : (p + 1) * R] = new_a[p].astype(BF)
    a[TOP:] = jnp.zeros((TILE - TOP, wide), BF)
    tokens = x.shape[0] // 4

    def multiply(*accs):
        steps = wide // TILE

        def push(k):
            for unit in range(2):
                tile = a[:, k * TILE : (k + 1) * TILE]
                pltpu.matmul_push_rhs(tile, k % 2, unit, transpose=True)

        push(0)
        for k in range(steps):
            if k + 1 < steps:
                push(k + 1)
            for r in range(4):
                rows = x[r * tokens : (r + 1) * tokens, k * TILE : (k + 1) * TILE]
                staged = k % 2 if r < 2 else None
                pltpu.matmul_acc_lhs(accs[r], rows, load_staged_rhs=staged)
        for r, send in enumerate(sends):
            u = (0.25 * pltpu.matmul_pop(accs[r])[:, :TOP]).astype(BF)
            for p in range(2):
                send[p * R : (p + 1) * R, :] = new_b[p].astype(BF)
            send[TOP:, :TOP] = u[:TOP]
            send[TOP:tokens, TOP:] = u[TOP:]
            send[tokens:, TOP:] = jnp.zeros((2 * TOP - tokens, TOP), BF)

    pl.run_scoped(multiply, *[pltpu.ACC(r % 2)((tokens, TILE), F32) for r in range(4)])
    for copy in copies:
        copy.wait()


def updated(ids, half, other, factor_a, factor_b, x, dp, *after):
    rates = (2.0 / math.sqrt(dp * D), 2.0 / math.sqrt(dp * R))
    outs = [pltpu.HBM(f.shape, F32) for f in (factor_a, factor_b)]
    outs += [jax.ShapeDtypeStruct((2 * TOP, 2 * TOP), BF)] * 4
    return small_call(
        functools.partial(update_kernel, rates),
        "update_factors",
        ids,
        (half, other, factor_a, factor_b, x),
        outs,
        after,
        [
            pltpu.VMEM((TILE, factor_a.shape[-1]), BF),
            pltpu.VMEM(factor_a.shape, F32),
            pltpu.VMEM(factor_b.shape, F32),
            pltpu.SemaphoreType.DMA((2,)),
        ],
        2,
    )


def attend_kernel(ids, first, lengths, *refs):
    q, cache_k, cache_v, k0, k1, k2, v0, v1, v2, *ub, cosine, sine = refs[:15]
    out = refs[-3]
    rows, slots, _ = cache_k.shape
    tokens = rows * STEPS
    u_held, b_held = refs[-2:]

    @pl.when(pl.program_id(0) == 0)
    def _():
        u_held[:TOP] = sum(x[TOP:, :TOP].astype(F32) for x in ub).astype(BF)
        u_held[TOP:] = sum(x[TOP:tokens, TOP:].astype(F32) for x in ub).astype(BF)

    rel = ids[0] ^ (first[0] + pl.program_id(0))
    for r, x in enumerate(ub):

        @pl.when(rel == r)
        def _():
            b_held[...] = x[:TOP]

    u, b = u_held[...], b_held[...]
    k = k0[...].astype(F32) + k1[...].astype(F32) + k2[...].astype(F32) + dot(u[:, :R], b[:R])
    v = v0[...].astype(F32) + v1[...].astype(F32) + v2[...].astype(F32) + dot(u[:, R:], b[R:])
    v = v.astype(BF)
    keys = []
    for n in range(HEADS_STEP):
        key = k[:, n * HD : (n + 1) * HD]
        scale = lax.rsqrt(jnp.sum(key * key, axis=-1, keepdims=True) * (1.0 / HD) + 1e-06)
        key = scale * (key * cosine[...] + pltpu.roll(key, HD // 2, 1) * sine[...])
        keys.append(key.astype(BF))
    n_q, n_c = GROUP * STEPS, GROUP * slots
    shape = (n_q, n_c + n_q)
    here = lax.broadcasted_iota(jnp.int32, shape, 0)
    col = lax.broadcasted_iota(jnp.int32, shape, 1)
    fresh = col - n_c
    cached = (col < n_c) & (here // STEPS == col // slots)
    new = (col >= n_c) & (here // STEPS == fresh // STEPS) & (fresh % STEPS <= here % STEPS)
    bias_here = jnp.where(cached | new, 0.0, -1e30)
    col = lax.broadcasted_iota(jnp.int32, (1, n_c + n_q), 1)
    ones = jnp.ones((n_c + n_q, HD), BF)
    factor = math.log2(math.e) * HD**-0.5
    heads = QH // KVH
    blocks = rows // GROUP
    query = q[...].reshape(tokens, HEADS_STEP * heads * HD)

    def block(n, g, cache, fresh):
        old = cache[g * GROUP : (g + 1) * GROUP, :, n * HD : (n + 1) * HD].reshape(n_c, HD)
        return jnp.concatenate([old, fresh[g * n_q : (g + 1) * n_q]], axis=0)

    every = [(n, g) for n in range(HEADS_STEP) for g in range(blocks)]
    scores = []
    for n, g in every:
        part = [query[g * n_q : (g + 1) * n_q, h * HD : (h + 1) * HD] for h in range(n * heads, (n + 1) * heads)]
        scores.append(dot_t(jnp.concatenate(part, axis=0), block(n, g, cache_k, keys[n])))
    biases = []
    for g in range(blocks):
        filled = jnp.full(col.shape, lengths[g * GROUP], jnp.int32)
        for i in range(1, GROUP):
            filled = jnp.where(col // slots == i, lengths[g * GROUP + i], filled)
        bias = jnp.where((col >= n_c) | (col % slots < filled), 0.0, -1e30) + bias_here
        biases.append(jnp.concatenate([bias] * heads, axis=0))
    weights = []
    for (n, g), s in zip(every, scores):
        s = s * factor + biases[g]
        top = jnp.max(s, axis=-1, keepdims=True)
        weights.append(jnp.exp2(s - top).astype(BF))
    results = []
    for (n, g), w in zip(every, weights):
        here_v = block(n, g, cache_v, v[:, n * HD : (n + 1) * HD])
        r = dot(w, jnp.concatenate([here_v, ones], axis=1))
        total = r[:, HD:]
        inverse = pl.reciprocal(total, approx=True)
        inverse = inverse * (2.0 - total * inverse)
        results.append((r[:, :HD] * inverse).astype(BF))
    for n in range(HEADS_STEP):
        for h in range(heads):
            part = [r[h * n_q : (h + 1) * n_q] for r in results[n * blocks : (n + 1) * blocks]]
            at = (n * heads + h) * HD
            out[:, :, at : at + HD] = jnp.concatenate(part, axis=0).reshape(rows, STEPS, HD)


def attend_chunk(
    ids, lengths, start, count, queries, cache_keys, cache_values, terms, ub, tables, before
):
    rows, slots, _ = cache_keys.shape
    tokens = rows * STEPS
    heads = QH // KVH
    args = [queries, cache_keys, cache_values, *terms, *ub, *tables]
    assert start % HEADS_STEP == 0 and count % HEADS_STEP == 0
    first = jnp.full((1,), start // HEADS_STEP, jnp.int32)
    size = HEADS_STEP * HD
    part = pl.BlockSpec((tokens, size), lambda i, *_: (0, i))
    low = pl.BlockSpec((tokens, size), lambda i, *_: (1, i))
    cache = pl.BlockSpec((rows, slots, size), lambda i, _, first, *__: (0, 0, first[0] + i))
    wide = pl.BlockSpec((rows, STEPS, heads * size), lambda i, _, first, *__: (0, 0, first[0] + i))
    specs = [wide, cache, cache, part, low, part, part, part, part]
    specs += [whole(x.shape) for x in (*ub, *tables)]
    args.append(before)
    specs.append(pl.BlockSpec(memory_space=pl.ANY))
    return pl.pallas_call(
        attend_kernel,
        out_shape=jax.ShapeDtypeStruct(queries.shape, BF),
        grid_spec=pltpu.PrefetchScalarGridSpec(
            num_scalar_prefetch=3, grid=(count // HEADS_STEP,), in_specs=specs, out_specs=wide,
            scratch_shapes=[pltpu.VMEM((tokens, TOP), BF), pltpu.VMEM((TOP, size), BF)],
        ),
        input_output_aliases={len(args) + 2: 0},
        compiler_params=params(14),
        cost_estimate=cost(count * 4 * 10**9, *args),
        name="attend_chunk",
    )(ids, first, lengths, *args)


def rotary_tables(key_gain, positions):
    half = HD // 2
    place = positions[:, None] + jnp.arange(STEPS, dtype=jnp.int32)[None, :]
    freq = jnp.exp(-math.log(1000000.0) * (jnp.arange(half, dtype=F32) * 2.0 / HD))
    angle = place.reshape(-1).astype(F32)[:, None] * jnp.concatenate([freq, freq])
    turned = jnp.concatenate([-key_gain[half:], key_gain[:half]])
    return jnp.cos(angle) * key_gain, jnp.sin(angle) * turned


def across(x, r):
    return lax.ppermute(x, "tensor", [(i, i ^ r) for i in range(4)])


def square(
    hidden_in,
    kv_weight,
    factor_a,
    factor_b,
    grad_a,
    grad_b,
    key_gain,
    queries,
    cache_keys,
    cache_values,
    cache_lengths,
    positions,
):
    tokens = cache_keys.shape[0] * STEPS
    count_dp = lax.axis_size("dp")
    dp = lax.axis_index("dp")
    ids = jnp.stack([lax.axis_index("tensor"), dp // 2, dp % 2]).astype(jnp.int32)
    tables = rotary_tables(key_gain, positions)

    x, *first, packed = first_terms(ids, hidden_in, kv_weight, grad_a, grad_b, tokens)
    half = chip_grads(ids, grad_a, grad_b, core_flip(packed, count_dp))

    def first_exchange(term, *after):
        ksend, vsend, kkeep, vkeep0, vkeep1 = term
        kcame, vcame = across(ksend, 1), across(vsend, 2)
        mids = mid_sums(kkeep, kcame, vkeep1, vcame, *after)
        return mids, (kkeep, kcame, vkeep0, vcame)

    def second_exchange(mids, parts):
        kkeep, kcame, vkeep0, vcame = parts
        return kkeep, kcame, across(mids[0], 2), vkeep0, vcame, across(mids[1], 1)

    second = later_terms(x, kv_weight, half)
    step, after = 1, second[:1]
    while 2 * step < count_dp:
        half = plus(half, along_line(half, step, count_dp), *after)
        step *= 2
        if step == 2:
            *keeps, attended = keep_terms(x, kv_weight, queries, half)
            first += keeps
            mids, parts = first_exchange(first, half)
            after = (mids[0], tables[0])
    if step == 1:
        *keeps, attended = keep_terms(x, kv_weight, queries, half)
        first += keeps
        mids, parts = first_exchange(first, half)
    first = second_exchange(mids, parts)
    other = core_flip(half, count_dp)
    new_a, new_b, *sends = updated(
        ids, half, other, factor_a, factor_b, x, count_dp
    )
    ub = [sends[0]] + [across(sends[r], r) for r in (1, 2, 3)]
    second = second_exchange(*first_exchange(second, ub[1]))
    for start, count, came in ((0, CHUNKS[0], first), (CHUNKS[0], CHUNKS[1], second)):
        attended = attend_chunk(
            ids,
            cache_lengths,
            start,
            count,
            queries,
            cache_keys,
            cache_values,
            came,
            ub,
            tables,
            attended,
        )
    return attended, new_a, new_b


def solution(mesh):
    fits = mesh.shape["tensor"] == 4 and mesh.shape["dp"] in (2, 4, 8)
    return jax.shard_map(
        square if fits else general,
        mesh=mesh,
        in_specs=(
            P("dp", None, "tensor"),
            P(None, "tensor", None),
            P(None, None, "tensor"),
            P(None, None, "tensor"),
            P("dp", None, None, "tensor"),
            P("dp", None, None, "tensor"),
            P(),
            P(("dp", "tensor"), None, None),
            P(("dp", "tensor"), None, None),
            P(("dp", "tensor"), None, None),
            P(("dp", "tensor")),
            P(("dp", "tensor")),
        ),
        out_specs=(
            P(("dp", "tensor"), None, None),
            P(None, None, "tensor"),
            P(None, None, "tensor"),
        ),
        check_vma=False,
    )
```

```python
import functools
import math

import jax
import jax.numpy as jnp
from jax import lax
from jax.experimental import pallas as pl
from jax.experimental.pallas import tpu as pltpu
from jax.sharding import PartitionSpec as P

D = 5120
KVH = 8
HD = 128
QH = 32
R = 64
STEPS = 4
BF = jnp.bfloat16
F32 = jnp.float32
MIB = 1024 * 1024


def normed_rotated(keys, gain, position):
    scale = lax.rsqrt(jnp.mean(keys * keys, axis=-1, keepdims=True) + 1e-06)
    keys = keys * scale * gain
    half = keys.shape[-1] // 2
    freq = jnp.exp(
        -math.log(1000000.0) * (jnp.arange(half, dtype=jnp.float32) * 2.0 / keys.shape[-1])
    )
    angle = position.astype(jnp.float32)[..., None] * freq
    cosine = jnp.concatenate([jnp.cos(angle), jnp.cos(angle)], axis=-1)[..., None, :]
    sine = jnp.concatenate([jnp.sin(angle), jnp.sin(angle)], axis=-1)[..., None, :]
    turned = jnp.concatenate([-keys[..., half:], keys[..., :half]], axis=-1)
    return keys * cosine + turned * sine


def attend(queries, cache_keys, cache_values, new_keys, new_values, lengths):
    rows, steps, width = queries.shape
    slots = cache_keys.shape[1]
    slot = jnp.arange(slots, dtype=jnp.int32)
    for step in range(steps):
        hit = (slot[None, :] == lengths[:, None] + step)[:, :, None]
        cache_keys = jnp.where(hit, new_keys[:, step][:, None, :], cache_keys)
        cache_values = jnp.where(hit, new_values[:, step][:, None, :], cache_values)
    groups = QH // KVH
    query_five = queries.reshape(rows, steps, KVH, groups, HD)
    key_four = cache_keys.reshape(rows, slots, KVH, HD)
    value_four = cache_values.reshape(rows, slots, KVH, HD)
    scores = jnp.einsum(
        "rtkgd,rckd->rtkgc", query_five, key_four, preferred_element_type=jnp.float32
    ) * HD ** (-0.5)
    limit = lengths[:, None] + jnp.arange(steps, dtype=jnp.int32)[None, :]
    valid = (slot[None, None, :] <= limit[:, :, None])[:, :, None, None, :]
    scores = jnp.where(valid, scores, jnp.float32(-1e30))
    top = jnp.max(scores, axis=-1, keepdims=True)
    expo = jnp.exp(scores - top)
    weights = (expo / jnp.sum(expo, axis=-1, keepdims=True)).astype(jnp.bfloat16)
    result = jnp.einsum(
        "rtkgc,rckd->rtkgd", weights, value_four, preferred_element_type=jnp.float32
    )
    return result.reshape(rows, steps, width).astype(jnp.bfloat16)


def general(
    hidden_in,
    kv_weight,
    factor_a,
    factor_b,
    grad_a,
    grad_b,
    key_gain,
    queries,
    cache_keys,
    cache_values,
    cache_lengths,
    positions,
):
    groups_dp = lax.axis_size("dp")
    rate_a = 2.0 / math.sqrt(groups_dp * D)
    rate_b = 2.0 / math.sqrt(groups_dp * R)
    sum_a, sum_b = (
        lax.psum(grad_a[0].astype(jnp.bfloat16), "dp").astype(jnp.float32),
        lax.psum(grad_b[0].astype(jnp.bfloat16), "dp").astype(jnp.float32),
    )
    new_a = factor_a - rate_a * sum_a
    new_b = factor_b - rate_b * sum_b
    full_b = lax.all_gather(new_b.astype(jnp.bfloat16), "tensor", axis=2, tiled=True).astype(
        new_b.dtype
    )
    delta = jnp.einsum("prd,prk->pdk", new_a, full_b, precision=lax.Precision.HIGHEST)
    merged = (kv_weight.astype(jnp.float32) + 0.25 * delta).astype(jnp.bfloat16)
    joined = jnp.concatenate([merged[0], merged[1]], axis=1)
    rows_here = hidden_in.shape[0] // lax.axis_size("tensor")
    pieces = []
    for step in range(STEPS):
        term = jnp.dot(hidden_in[:, step, :], joined, preferred_element_type=jnp.float32)
        pieces.append(
            lax.psum_scatter(
                term.astype(jnp.bfloat16), "tensor", scatter_dimension=0, tiled=True
            ).astype(jnp.float32)
        )
    projected = jnp.stack(pieces, axis=1)
    kv_width = KVH * HD
    place = positions[:, None] + jnp.arange(STEPS, dtype=jnp.int32)[None, :]
    keys = normed_rotated(
        projected[..., :kv_width].reshape(rows_here, STEPS, KVH, HD), key_gain, place
    )
    new_keys = keys.reshape(rows_here, STEPS, kv_width).astype(jnp.bfloat16)
    new_values = projected[..., kv_width:].astype(jnp.bfloat16)
    attended = attend(queries, cache_keys, cache_values, new_keys, new_values, cache_lengths)
    return (attended, new_a, new_b)


CHUNKS = (4, 4)
GROUP = 4
HEADS_STEP = 2


def params(mib):
    return pltpu.CompilerParams(vmem_limit_bytes=mib * MIB)


def cost(flops, *arrays):
    size = sum(math.prod(x.shape) * x.dtype.itemsize for x in arrays)
    return pl.CostEstimate(flops=flops, bytes_accessed=size, transcendentals=0)


def dot(a, b):
    return jnp.dot(a, b, preferred_element_type=F32)


def dot_t(a, b):
    return lax.dot_general(a, b, (((1,), (1,)), ((), ())), preferred_element_type=F32)


def whole(shape):
    return pl.BlockSpec(shape, lambda i, *_: (0,) * len(shape))


def hbm(x):
    return pltpu.with_memory_space_constraint(x, pltpu.HBM)


TILE = 256


def rel_rows(x, x0):
    def rows(r, at):
        if r == 0:
            return x0[:, at]
        tokens = x.shape[0] // 3
        return x[(r - 1) * tokens : r * tokens, at]

    return rows


def multiply_terms(rows_of, tokens, width, weight, base, w, sems, keys, values):
    steps = width // TILE
    units = (keys, values)

    def copy(p, i):
        at = pl.ds(base + i * TILE, TILE)
        return pltpu.make_async_copy(weight.at[p, :, at], w.at[p, i], sems.at[p, i])

    def start():
        for i in range(w.shape[1]):
            for p in range(2):
                copy(p, i).start()

    def multiply(*accs):
        accs = (accs[: len(keys)], accs[len(keys) :])

        @pl.loop(0, w.shape[1])
        def _(i):
            for p in range(2):
                copy(p, i).wait()

            def push(k):
                for p in range(2):
                    pltpu.matmul_push_rhs(w[p, i, k * TILE : (k + 1) * TILE, :], k % 2, p)

            push(0)
            for k in range(steps):
                if k + 1 < steps:
                    push(k + 1)
                for n in range(len(keys)):
                    for p in range(2):
                        rows = rows_of(units[p][n][0], slice(k * TILE, (k + 1) * TILE))
                        staged = k % 2 if n == 0 else None
                        pltpu.matmul_acc_lhs(accs[p][n], rows, load_staged_rhs=staged)
            at = pl.ds(pl.multiple_of(i * TILE, TILE), TILE)
            for n in range(len(keys)):
                for p in range(2):
                    _, out, row = units[p][n]
                    out[row : row + tokens, at] = pltpu.matmul_pop(accs[p][n]).astype(BF)

    def run():
        pl.run_scoped(
            multiply,
            *[pltpu.ACC(p)((tokens, TILE), F32) for p in range(2) for _ in units[p]],
        )

    return start, run


def send_parts(tokens, ksend, vsend):
    return [(3, ksend, 0), (1, ksend, tokens)], [(2, vsend, 0), (3, vsend, tokens)]


def keep_parts(tokens, kkeep, vkeep0, vkeep1):
    return [(0, kkeep, 0), (2, kkeep, tokens)], [(0, vkeep0, 0), (1, vkeep1, 0)]


def first_kernel(ids, hidden, weight, grad_a, grad_b, x, ksend, vsend, packed, *scratch):
    held, w, held_a, held_b, hidden_sems, sems, grad_sems = scratch
    tokens, width = x.shape[0] // 3, x.shape[1]
    rows = tokens // STEPS
    parts = send_parts(tokens, ksend, vsend)
    start, run = multiply_terms(rel_rows(x, None), tokens, width, weight, 0, w, sems, *parts)

    def hidden_copy(r):
        at = pl.ds((ids[0] ^ r) * rows, rows)
        return pltpu.make_async_copy(hidden.at[at], held.at[r - 1], hidden_sems.at[r - 1])

    grads = [
        pltpu.make_async_copy(grad_a.at[0, ids[2] ^ 1], held_a, grad_sems.at[0]),
        pltpu.make_async_copy(grad_b.at[0, ids[2] ^ 1], held_b, grad_sems.at[1]),
    ]
    for r in (3, 1, 2):
        hidden_copy(r).start()
    start()
    for copy in grads:
        copy.start()
    for r in (3, 1, 2):
        hidden_copy(r).wait()
        x[(r - 1) * tokens : r * tokens] = held[r - 1].reshape(tokens, width)
    for copy in grads:
        copy.wait()
    wide = grad_a.shape[-1]
    packed[:, :wide] = held_a[...].astype(BF)
    packed[:, wide:] = held_b[...].astype(BF)
    run()


def keep_kernel(x, x0, weight, after, kkeep, vkeep0, vkeep1, _, w, sems):
    del after
    tokens, width = x0.shape
    parts = keep_parts(tokens, kkeep, vkeep0, vkeep1)
    start, run = multiply_terms(rel_rows(x, x0), tokens, width, weight, 0, w, sems, *parts)
    start()
    run()


def later_kernel(ids, x, hidden, weight, after, x0, *rest):
    del after
    ksend, vsend, kkeep, vkeep0, vkeep1, w, sems, held, hidden_sem = rest
    tokens, width = x0.shape
    at = pl.ds(ids[0] * (tokens // STEPS), tokens // STEPS)
    own = pltpu.make_async_copy(hidden.at[at], held, hidden_sem)
    own.start()
    sends = send_parts(tokens, ksend, vsend)
    keeps = keep_parts(tokens, kkeep, vkeep0, vkeep1)
    base = weight.shape[2] - w.shape[1] * TILE
    parts = [a + b for a, b in zip(sends, keeps)]
    start, run = multiply_terms(rel_rows(x, x0), tokens, width, weight, base, w, sems, *parts)
    start()
    own.wait()
    x0[...] = held[...].reshape(tokens, width)
    run()


SEND, KEEP = (2, 2), (2, 1, 1)


def term_shapes(rows, tokens, count):
    return [jax.ShapeDtypeStruct((n * tokens, count * HD), BF) for n in rows]


def weight_scratch(width, count):
    tiles = count * HD // TILE
    return [pltpu.VMEM((2, tiles, width, TILE), BF), pltpu.SemaphoreType.DMA((2, tiles))]


def first_terms(ids, hidden, kv_weight, grad_a, grad_b, tokens):
    width = hidden.shape[2]
    here = pl.BlockSpec(memory_space=pl.ANY)
    outs = [jax.ShapeDtypeStruct((3 * tokens, width), BF)]
    outs += [pltpu.VMEM(x.shape, BF) for x in term_shapes(SEND, tokens, CHUNKS[0])]
    outs.append(jax.ShapeDtypeStruct((grad_a.shape[2], grad_a.shape[3] + grad_b.shape[3]), BF))
    w, sems = weight_scratch(width, CHUNKS[0])
    return pl.pallas_call(
        first_kernel,
        out_shape=outs,
        grid_spec=pltpu.PrefetchScalarGridSpec(
            num_scalar_prefetch=1,
            grid=(1,),
            in_specs=[here] * 4,
            out_specs=[whole(x.shape) for x in outs],
            scratch_shapes=[
                pltpu.VMEM((3, tokens // STEPS, STEPS, width), BF),
                w,
                pltpu.VMEM(grad_a.shape[2:], F32),
                pltpu.VMEM(grad_b.shape[2:], F32),
                pltpu.SemaphoreType.DMA((3,)),
                sems,
                pltpu.SemaphoreType.DMA((2,)),
            ],
        ),
        compiler_params=params(16),
        cost_estimate=cost(8 * tokens * width * CHUNKS[0] * HD, hidden),
        name="first_terms",
    )(ids, *map(hbm, (hidden, kv_weight, grad_a, grad_b)))


def keep_terms(x, x0, kv_weight, queries, after):
    tokens, width = x0.shape
    here = pl.BlockSpec(memory_space=pl.ANY)
    outs = [pltpu.HBM(out.shape, BF) for out in term_shapes(KEEP, tokens, CHUNKS[0])]
    specs = [whole(out.shape) for out in outs] + [here]
    outs.append(jax.ShapeDtypeStruct(queries.shape, BF))
    return pl.pallas_call(
        keep_kernel,
        out_shape=outs,
        grid=(1,),
        in_specs=[whole(x.shape), whole(x0.shape), here, here],
        out_specs=specs,
        scratch_shapes=weight_scratch(width, CHUNKS[0]),
        compiler_params=params(14),
        cost_estimate=cost(8 * tokens * width * CHUNKS[0] * HD, x),
        name="keep_terms",
    )(x, x0, hbm(kv_weight), after)


def later_terms(ids, x, hidden, kv_weight, after):
    tokens, width = x.shape[0] // 3, x.shape[1]
    outs = [jax.ShapeDtypeStruct((tokens, width), BF)]
    outs += term_shapes(SEND + KEEP, tokens, CHUNKS[1])
    here = pl.BlockSpec(memory_space=pl.ANY)
    return pl.pallas_call(
        later_kernel,
        out_shape=outs,
        grid_spec=pltpu.PrefetchScalarGridSpec(
            num_scalar_prefetch=1,
            grid=(1,),
            in_specs=[whole(x.shape), here, here, here],
            out_specs=[whole(out.shape) for out in outs],
            scratch_shapes=[
                *weight_scratch(width, CHUNKS[1]),
                pltpu.VMEM((tokens // STEPS, STEPS, width), BF),
                pltpu.SemaphoreType.DMA,
            ],
        ),
        compiler_params=params(13),
        cost_estimate=cost(16 * tokens * width * CHUNKS[1] * HD, x, *outs),
        name="later_terms",
    )(ids, x, hbm(hidden), hbm(kv_weight), after)


def mid_kernel(kkeep, kcame, vkeep, vcame, *rest):
    kout, vout = rest[-2:]
    kout[...] = (kkeep[...].astype(F32) + kcame[...].astype(F32)).astype(BF)
    vout[...] = (vkeep[...].astype(F32) + vcame[...].astype(F32)).astype(BF)


def mid_sums(kkeep, kcame, vkeep, vcame, *after):
    shape = vkeep.shape
    low = pl.BlockSpec(shape, lambda i: (0, 0))
    high = pl.BlockSpec(shape, lambda i: (1, 0))
    return pl.pallas_call(
        mid_kernel,
        out_shape=[jax.ShapeDtypeStruct(shape, BF)] * 2,
        grid=(1,),
        in_specs=[high, low, low, high] + [pl.BlockSpec(memory_space=pl.ANY)] * len(after),
        out_specs=[low, low],
        compiler_params=params(4),
        cost_estimate=cost(0, *[vkeep] * 6),
        name="mid_sums",
    )(kkeep, kcame, vkeep, vcame, *after)


def chip_kernel(ids, grad_a, grad_b, other, out):
    del ids
    wide = grad_a.shape[-1]
    out[:, :wide] = (grad_a[0, 0] + other[:, :wide].astype(F32)).astype(BF)
    out[:, wide:] = (grad_b[0, 0] + other[:, wide:].astype(F32)).astype(BF)


def chip_grads(ids, grad_a, grad_b, other):
    def half(x):
        return pl.BlockSpec((1, 1) + x.shape[2:], lambda i, ids: (0, ids[2], 0, 0))

    return pl.pallas_call(
        chip_kernel,
        out_shape=jax.ShapeDtypeStruct(other.shape, BF),
        grid_spec=pltpu.PrefetchScalarGridSpec(
            num_scalar_prefetch=1,
            grid=(1,),
            in_specs=[half(grad_a), half(grad_b), whole(other.shape)],
            out_specs=whole(other.shape),
        ),
        compiler_params=params(4),
        cost_estimate=cost(0, *[other] * 4),
        name="chip_grads",
    )(ids, hbm(grad_a), hbm(grad_b), other)


def small_call(kernel, name, ids, args, outs, after=(), scratch=(), copied=0):
    count = len(args)

    def body(ids, *refs):
        kernel(ids, *refs[:count], *refs[count + len(after) :])

    return pl.pallas_call(
        body,
        out_shape=outs,
        grid_spec=pltpu.PrefetchScalarGridSpec(
            num_scalar_prefetch=1,
            grid=(1,),
            in_specs=[whole(x.shape) for x in args]
            + [pl.BlockSpec(memory_space=pl.ANY)] * len(after),
            out_specs=[pl.BlockSpec(memory_space=pltpu.HBM)] * copied
            + [whole(x.shape) for x in outs[copied:]],
            scratch_shapes=list(scratch),
        ),
        compiler_params=params(8),
        cost_estimate=cost(0, *args),
        name=name,
    )(ids, *args, *after)


def core_flip(x, count):
    return lax.ppermute(x, "dp", [(i, i ^ 1) for i in range(count)])


def plus_kernel(a, b, *rest):
    rest[-1][...] = (a[...].astype(F32) + b[...].astype(F32)).astype(BF)


def plus(a, b, *after):
    out = jax.ShapeDtypeStruct(a.shape, BF)
    return pl.pallas_call(
        plus_kernel,
        out_shape=out,
        grid=(1,),
        in_specs=[whole(a.shape)] * 2 + [pl.BlockSpec(memory_space=pl.ANY)] * len(after),
        out_specs=whole(a.shape),
        compiler_params=params(2),
        cost_estimate=cost(0, a, b, out),
        name="plus",
    )(a, b, *after)


def along_line(x, d, count):
    return lax.ppermute(x, "dp", [(i, i ^ (2 * d)) for i in range(count)])


TOP = 2 * R


def update_kernel(rates, ids, half, other, factor_a, factor_b, x, x0, out_a, out_b, *rest):
    *sends, a, new_a, new_b, sems = rest
    copies = [
        pltpu.make_async_copy(new_a, out_a, sems.at[0]),
        pltpu.make_async_copy(new_b, out_b, sems.at[1]),
    ]
    wide = factor_a.shape[-1]
    for index, part in ((ids[2], half), (ids[2] ^ 1, other)):
        new_a[index] = factor_a[index] - rates[0] * part[:, :wide].astype(F32)
        new_b[index] = factor_b[index] - rates[1] * part[:, wide:].astype(F32)
    for copy in copies:
        copy.start()
    for p in range(2):
        a[p * R : (p + 1) * R] = new_a[p].astype(BF)
    a[TOP:] = jnp.zeros((TILE - TOP, wide), BF)
    tokens = x0.shape[0]
    rows_of = rel_rows(x, x0)

    def multiply(*accs):
        steps = wide // TILE

        def push(k):
            for unit in range(2):
                tile = a[:, k * TILE : (k + 1) * TILE]
                pltpu.matmul_push_rhs(tile, k % 2, unit, transpose=True)

        push(0)
        for k in range(steps):
            if k + 1 < steps:
                push(k + 1)
            for r in range(4):
                rows = rows_of(r, slice(k * TILE, (k + 1) * TILE))
                staged = k % 2 if r < 2 else None
                pltpu.matmul_acc_lhs(accs[r], rows, load_staged_rhs=staged)
        for r, send in enumerate(sends):
            u = (0.25 * pltpu.matmul_pop(accs[r])[:, :TOP]).astype(BF)
            for p in range(2):
                send[p * R : (p + 1) * R, :] = new_b[p].astype(BF)
            send[TOP:, :TOP] = u[:TOP]
            send[TOP:tokens, TOP:] = u[TOP:]
            send[tokens:, TOP:] = jnp.zeros((2 * TOP - tokens, TOP), BF)

    pl.run_scoped(multiply, *[pltpu.ACC(r % 2)((tokens, TILE), F32) for r in range(4)])
    for copy in copies:
        copy.wait()


def updated(ids, half, other, factor_a, factor_b, x, x0, dp, *after):
    rates = (2.0 / math.sqrt(dp * D), 2.0 / math.sqrt(dp * R))
    outs = [pltpu.HBM(f.shape, F32) for f in (factor_a, factor_b)]
    outs += [jax.ShapeDtypeStruct((2 * TOP, 2 * TOP), BF)] * 4
    return small_call(
        functools.partial(update_kernel, rates),
        "update_factors",
        ids,
        (half, other, factor_a, factor_b, x, x0),
        outs,
        after,
        [
            pltpu.VMEM((TILE, factor_a.shape[-1]), BF),
            pltpu.VMEM(factor_a.shape, F32),
            pltpu.VMEM(factor_b.shape, F32),
            pltpu.SemaphoreType.DMA((2,)),
        ],
        2,
    )


def attend_kernel(ids, first, lengths, *refs):
    q, cache_k, cache_v, k0, k1, k2, v0, v1, v2, *ub, cosine, sine = refs[:15]
    out = refs[-3]
    rows, slots, _ = cache_k.shape
    tokens = rows * STEPS
    u_held, b_held = refs[-2:]

    @pl.when(pl.program_id(0) == 0)
    def _():
        u_held[:TOP] = sum(x[TOP:, :TOP].astype(F32) for x in ub).astype(BF)
        u_held[TOP:] = sum(x[TOP:tokens, TOP:].astype(F32) for x in ub).astype(BF)

    rel = ids[0] ^ (first[0] + pl.program_id(0))
    for r, x in enumerate(ub):

        @pl.when(rel == r)
        def _():
            b_held[...] = x[:TOP]

    u, b = u_held[...], b_held[...]
    k = k0[...].astype(F32) + k1[...].astype(F32) + k2[...].astype(F32) + dot(u[:, :R], b[:R])
    v = v0[...].astype(F32) + v1[...].astype(F32) + v2[...].astype(F32) + dot(u[:, R:], b[R:])
    v = v.astype(BF)
    keys = []
    for n in range(HEADS_STEP):
        key = k[:, n * HD : (n + 1) * HD]
        scale = lax.rsqrt(jnp.sum(key * key, axis=-1, keepdims=True) * (1.0 / HD) + 1e-06)
        key = scale * (key * cosine[...] + pltpu.roll(key, HD // 2, 1) * sine[...])
        keys.append(key.astype(BF))
    n_q, n_c = GROUP * STEPS, GROUP * slots
    shape = (n_q, n_c + n_q)
    here = lax.broadcasted_iota(jnp.int32, shape, 0)
    col = lax.broadcasted_iota(jnp.int32, shape, 1)
    fresh = col - n_c
    cached = (col < n_c) & (here // STEPS == col // slots)
    new = (col >= n_c) & (here // STEPS == fresh // STEPS) & (fresh % STEPS <= here % STEPS)
    bias_here = jnp.where(cached | new, 0.0, -1e30)
    col = lax.broadcasted_iota(jnp.int32, (1, n_c + n_q), 1)
    ones = jnp.ones((n_c + n_q, HD), BF)
    factor = math.log2(math.e) * HD**-0.5
    heads = QH // KVH
    blocks = rows // GROUP
    query = q[...].reshape(tokens, HEADS_STEP * heads * HD)

    def block(n, g, cache, fresh):
        old = cache[g * GROUP : (g + 1) * GROUP, :, n * HD : (n + 1) * HD].reshape(n_c, HD)
        return jnp.concatenate([old, fresh[g * n_q : (g + 1) * n_q]], axis=0)

    every = [(n, g) for n in range(HEADS_STEP) for g in range(blocks)]
    scores = []
    for n, g in every:
        part = [query[g * n_q : (g + 1) * n_q, h * HD : (h + 1) * HD] for h in range(n * heads, (n + 1) * heads)]
        scores.append(dot_t(jnp.concatenate(part, axis=0), block(n, g, cache_k, keys[n])))
    biases = []
    for g in range(blocks):
        filled = jnp.full(col.shape, lengths[g * GROUP], jnp.int32)
        for i in range(1, GROUP):
            filled = jnp.where(col // slots == i, lengths[g * GROUP + i], filled)
        bias = jnp.where((col >= n_c) | (col % slots < filled), 0.0, -1e30) + bias_here
        biases.append(jnp.concatenate([bias] * heads, axis=0))
    weights = []
    for (n, g), s in zip(every, scores):
        s = s * factor + biases[g]
        top = jnp.max(s, axis=-1, keepdims=True)
        weights.append(jnp.exp2(s - top).astype(BF))
    results = []
    for (n, g), w in zip(every, weights):
        here_v = block(n, g, cache_v, v[:, n * HD : (n + 1) * HD])
        r = dot(w, jnp.concatenate([here_v, ones], axis=1))
        total = r[:, HD:]
        inverse = pl.reciprocal(total, approx=True)
        inverse = inverse * (2.0 - total * inverse)
        results.append((r[:, :HD] * inverse).astype(BF))
    for n in range(HEADS_STEP):
        for h in range(heads):
            part = [r[h * n_q : (h + 1) * n_q] for r in results[n * blocks : (n + 1) * blocks]]
            at = (n * heads + h) * HD
            out[:, :, at : at + HD] = jnp.concatenate(part, axis=0).reshape(rows, STEPS, HD)


def attend_chunk(
    ids, lengths, start, count, queries, cache_keys, cache_values, terms, ub, tables, before
):
    rows, slots, _ = cache_keys.shape
    tokens = rows * STEPS
    heads = QH // KVH
    args = [queries, cache_keys, cache_values, *terms, *ub, *tables]
    assert start % HEADS_STEP == 0 and count % HEADS_STEP == 0
    first = jnp.full((1,), start // HEADS_STEP, jnp.int32)
    size = HEADS_STEP * HD
    part = pl.BlockSpec((tokens, size), lambda i, *_: (0, i))
    low = pl.BlockSpec((tokens, size), lambda i, *_: (1, i))
    cache = pl.BlockSpec((rows, slots, size), lambda i, _, first, *__: (0, 0, first[0] + i))
    wide = pl.BlockSpec((rows, STEPS, heads * size), lambda i, _, first, *__: (0, 0, first[0] + i))
    specs = [wide, cache, cache, part, low, part, part, part, part]
    specs += [whole(x.shape) for x in (*ub, *tables)]
    args.append(before)
    specs.append(pl.BlockSpec(memory_space=pl.ANY))
    return pl.pallas_call(
        attend_kernel,
        out_shape=jax.ShapeDtypeStruct(queries.shape, BF),
        grid_spec=pltpu.PrefetchScalarGridSpec(
            num_scalar_prefetch=3, grid=(count // HEADS_STEP,), in_specs=specs, out_specs=wide,
            scratch_shapes=[pltpu.VMEM((tokens, TOP), BF), pltpu.VMEM((TOP, size), BF)],
        ),
        input_output_aliases={len(args) + 2: 0},
        compiler_params=params(14),
        cost_estimate=cost(count * 4 * 10**9, *args),
        name="attend_chunk",
    )(ids, first, lengths, *args)


def rotary_tables(key_gain, positions):
    half = HD // 2
    place = positions[:, None] + jnp.arange(STEPS, dtype=jnp.int32)[None, :]
    freq = jnp.exp(-math.log(1000000.0) * (jnp.arange(half, dtype=F32) * 2.0 / HD))
    angle = place.reshape(-1).astype(F32)[:, None] * jnp.concatenate([freq, freq])
    turned = jnp.concatenate([-key_gain[half:], key_gain[:half]])
    return jnp.cos(angle) * key_gain, jnp.sin(angle) * turned


def across(x, r):
    return lax.ppermute(x, "tensor", [(i, i ^ r) for i in range(4)])


def square(
    hidden_in,
    kv_weight,
    factor_a,
    factor_b,
    grad_a,
    grad_b,
    key_gain,
    queries,
    cache_keys,
    cache_values,
    cache_lengths,
    positions,
):
    tokens = cache_keys.shape[0] * STEPS
    count_dp = lax.axis_size("dp")
    dp = lax.axis_index("dp")
    ids = jnp.stack([lax.axis_index("tensor"), dp // 2, dp % 2]).astype(jnp.int32)
    tables = rotary_tables(key_gain, positions)

    x, *first, packed = first_terms(ids, hidden_in, kv_weight, grad_a, grad_b, tokens)
    half = chip_grads(ids, grad_a, grad_b, core_flip(packed, count_dp))

    def first_exchange(term, *after):
        ksend, vsend, kkeep, vkeep0, vkeep1 = term
        kcame, vcame = across(ksend, 1), across(vsend, 2)
        mids = mid_sums(kkeep, kcame, vkeep1, vcame, *after)
        return mids, (kkeep, kcame, vkeep0, vcame)

    def second_exchange(mids, parts):
        kkeep, kcame, vkeep0, vcame = parts
        return kkeep, kcame, across(mids[0], 2), vkeep0, vcame, across(mids[1], 1)

    x0, *second = later_terms(ids, x, hidden_in, kv_weight, half)
    step, after = 1, second[:1]
    while 2 * step < count_dp:
        half = plus(half, along_line(half, step, count_dp), *after)
        step *= 2
        if step == 2:
            *keeps, attended = keep_terms(x, x0, kv_weight, queries, half)
            first += keeps
            mids, parts = first_exchange(first, half)
            after = (mids[0], tables[0])
    if step == 1:
        *keeps, attended = keep_terms(x, x0, kv_weight, queries, half)
        first += keeps
        mids, parts = first_exchange(first, half)
    first = second_exchange(mids, parts)
    other = core_flip(half, count_dp)
    new_a, new_b, *sends = updated(
        ids, half, other, factor_a, factor_b, x, x0, count_dp
    )
    ub = [sends[0]] + [across(sends[r], r) for r in (1, 2, 3)]
    second = second_exchange(*first_exchange(second, ub[1]))
    for start, count, came in ((0, CHUNKS[0], first), (CHUNKS[0], CHUNKS[1], second)):
        attended = attend_chunk(
            ids,
            cache_lengths,
            start,
            count,
            queries,
            cache_keys,
            cache_values,
            came,
            ub,
            tables,
            attended,
        )
    return attended, new_a, new_b


def solution(mesh):
    fits = mesh.shape["tensor"] == 4 and mesh.shape["dp"] in (2, 4, 8)
    return jax.shard_map(
        square if fits else general,
        mesh=mesh,
        in_specs=(
            P("dp", None, "tensor"),
            P(None, "tensor", None),
            P(None, None, "tensor"),
            P(None, None, "tensor"),
            P("dp", None, None, "tensor"),
            P("dp", None, None, "tensor"),
            P(),
            P(("dp", "tensor"), None, None),
            P(("dp", "tensor"), None, None),
            P(("dp", "tensor"), None, None),
            P(("dp", "tensor")),
            P(("dp", "tensor")),
        ),
        out_specs=(
            P(("dp", "tensor"), None, None),
            P(None, None, "tensor"),
            P(None, None, "tensor"),
        ),
        check_vma=False,
    )
```

```python
import functools
import math

import jax
import jax.numpy as jnp
from jax import lax
from jax.experimental import pallas as pl
from jax.experimental.pallas import tpu as pltpu
from jax.sharding import PartitionSpec as P

D = 5120
KVH = 8
HD = 128
QH = 32
R = 64
STEPS = 4
BF = jnp.bfloat16
F32 = jnp.float32
MIB = 1024 * 1024


def normed_rotated(keys, gain, position):
    scale = lax.rsqrt(jnp.mean(keys * keys, axis=-1, keepdims=True) + 1e-06)
    keys = keys * scale * gain
    half = keys.shape[-1] // 2
    freq = jnp.exp(
        -math.log(1000000.0) * (jnp.arange(half, dtype=jnp.float32) * 2.0 / keys.shape[-1])
    )
    angle = position.astype(jnp.float32)[..., None] * freq
    cosine = jnp.concatenate([jnp.cos(angle), jnp.cos(angle)], axis=-1)[..., None, :]
    sine = jnp.concatenate([jnp.sin(angle), jnp.sin(angle)], axis=-1)[..., None, :]
    turned = jnp.concatenate([-keys[..., half:], keys[..., :half]], axis=-1)
    return keys * cosine + turned * sine


def attend(queries, cache_keys, cache_values, new_keys, new_values, lengths):
    rows, steps, width = queries.shape
    slots = cache_keys.shape[1]
    slot = jnp.arange(slots, dtype=jnp.int32)
    for step in range(steps):
        hit = (slot[None, :] == lengths[:, None] + step)[:, :, None]
        cache_keys = jnp.where(hit, new_keys[:, step][:, None, :], cache_keys)
        cache_values = jnp.where(hit, new_values[:, step][:, None, :], cache_values)
    groups = QH // KVH
    query_five = queries.reshape(rows, steps, KVH, groups, HD)
    key_four = cache_keys.reshape(rows, slots, KVH, HD)
    value_four = cache_values.reshape(rows, slots, KVH, HD)
    scores = jnp.einsum(
        "rtkgd,rckd->rtkgc", query_five, key_four, preferred_element_type=jnp.float32
    ) * HD ** (-0.5)
    limit = lengths[:, None] + jnp.arange(steps, dtype=jnp.int32)[None, :]
    valid = (slot[None, None, :] <= limit[:, :, None])[:, :, None, None, :]
    scores = jnp.where(valid, scores, jnp.float32(-1e30))
    top = jnp.max(scores, axis=-1, keepdims=True)
    expo = jnp.exp(scores - top)
    weights = (expo / jnp.sum(expo, axis=-1, keepdims=True)).astype(jnp.bfloat16)
    result = jnp.einsum(
        "rtkgc,rckd->rtkgd", weights, value_four, preferred_element_type=jnp.float32
    )
    return result.reshape(rows, steps, width).astype(jnp.bfloat16)


def general(
    hidden_in,
    kv_weight,
    factor_a,
    factor_b,
    grad_a,
    grad_b,
    key_gain,
    queries,
    cache_keys,
    cache_values,
    cache_lengths,
    positions,
):
    groups_dp = lax.axis_size("dp")
    rate_a = 2.0 / math.sqrt(groups_dp * D)
    rate_b = 2.0 / math.sqrt(groups_dp * R)
    sum_a, sum_b = (
        lax.psum(grad_a[0].astype(jnp.bfloat16), "dp").astype(jnp.float32),
        lax.psum(grad_b[0].astype(jnp.bfloat16), "dp").astype(jnp.float32),
    )
    new_a = factor_a - rate_a * sum_a
    new_b = factor_b - rate_b * sum_b
    full_b = lax.all_gather(new_b.astype(jnp.bfloat16), "tensor", axis=2, tiled=True).astype(
        new_b.dtype
    )
    delta = jnp.einsum("prd,prk->pdk", new_a, full_b, precision=lax.Precision.HIGHEST)
    merged = (kv_weight.astype(jnp.float32) + 0.25 * delta).astype(jnp.bfloat16)
    joined = jnp.concatenate([merged[0], merged[1]], axis=1)
    rows_here = hidden_in.shape[0] // lax.axis_size("tensor")
    pieces = []
    for step in range(STEPS):
        term = jnp.dot(hidden_in[:, step, :], joined, preferred_element_type=jnp.float32)
        pieces.append(
            lax.psum_scatter(
                term.astype(jnp.bfloat16), "tensor", scatter_dimension=0, tiled=True
            ).astype(jnp.float32)
        )
    projected = jnp.stack(pieces, axis=1)
    kv_width = KVH * HD
    place = positions[:, None] + jnp.arange(STEPS, dtype=jnp.int32)[None, :]
    keys = normed_rotated(
        projected[..., :kv_width].reshape(rows_here, STEPS, KVH, HD), key_gain, place
    )
    new_keys = keys.reshape(rows_here, STEPS, kv_width).astype(jnp.bfloat16)
    new_values = projected[..., kv_width:].astype(jnp.bfloat16)
    attended = attend(queries, cache_keys, cache_values, new_keys, new_values, cache_lengths)
    return (attended, new_a, new_b)


CHUNKS = (4, 4)
GROUP = 4
HEADS_STEP = 2


def params(mib):
    return pltpu.CompilerParams(vmem_limit_bytes=mib * MIB)


def cost(flops, *arrays):
    size = sum(math.prod(x.shape) * x.dtype.itemsize for x in arrays)
    return pl.CostEstimate(flops=flops, bytes_accessed=size, transcendentals=0)


def dot(a, b):
    return jnp.dot(a, b, preferred_element_type=F32)


def dot_t(a, b):
    return lax.dot_general(a, b, (((1,), (1,)), ((), ())), preferred_element_type=F32)


def whole(shape):
    return pl.BlockSpec(shape, lambda i, *_: (0,) * len(shape))


def hbm(x):
    return pltpu.with_memory_space_constraint(x, pltpu.HBM)


TILE = 256


def multiply_terms(x, weight, base, w, sems, keys, values):
    tokens = x.shape[0] // 4
    steps = x.shape[1] // TILE
    units = (keys, values)

    def copy(p, i):
        at = pl.ds(base + i * TILE, TILE)
        return pltpu.make_async_copy(weight.at[p, :, at], w.at[p, i], sems.at[p, i])

    def start():
        for i in range(w.shape[1]):
            for p in range(2):
                copy(p, i).start()

    def multiply(*accs):
        accs = (accs[: len(keys)], accs[len(keys) :])

        @pl.loop(0, w.shape[1])
        def _(i):
            for p in range(2):
                copy(p, i).wait()

            def push(k):
                for p in range(2):
                    pltpu.matmul_push_rhs(w[p, i, k * TILE : (k + 1) * TILE, :], k % 2, p)

            push(0)
            for k in range(steps):
                if k + 1 < steps:
                    push(k + 1)
                for n in range(len(keys)):
                    for p in range(2):
                        r = units[p][n][0]
                        rows = x[r * tokens : (r + 1) * tokens, k * TILE : (k + 1) * TILE]
                        staged = k % 2 if n == 0 else None
                        pltpu.matmul_acc_lhs(accs[p][n], rows, load_staged_rhs=staged)
            at = pl.ds(pl.multiple_of(i * TILE, TILE), TILE)
            for n in range(len(keys)):
                for p in range(2):
                    _, out, row = units[p][n]
                    out[row : row + tokens, at] = pltpu.matmul_pop(accs[p][n]).astype(BF)

    def run():
        pl.run_scoped(
            multiply,
            *[pltpu.ACC(p)((tokens, TILE), F32) for p in range(2) for _ in units[p]],
        )

    return start, run


def send_parts(tokens, ksend, vsend):
    return [(3, ksend, 0), (1, ksend, tokens)], [(2, vsend, 0), (3, vsend, tokens)]


def keep_parts(tokens, kkeep, vkeep0, vkeep1):
    return [(0, kkeep, 0), (2, kkeep, tokens)], [(0, vkeep0, 0), (1, vkeep1, 0)]


def first_kernel(ids, hidden, weight, grad_a, grad_b, x, ksend, vsend, packed, *scratch):
    held, w, held_a, held_b, hidden_sems, sems, grad_sems = scratch
    tokens = x.shape[0] // 4
    rows = tokens // STEPS
    start, run = multiply_terms(x, weight, 0, w, sems, *send_parts(tokens, ksend, vsend))

    def hidden_copy(r):
        at = pl.ds((ids[0] ^ r) * rows, rows)
        return pltpu.make_async_copy(hidden.at[at], held.at[r], hidden_sems.at[r])

    grads = [
        pltpu.make_async_copy(grad_a.at[0, ids[2] ^ 1], held_a, grad_sems.at[0]),
        pltpu.make_async_copy(grad_b.at[0, ids[2] ^ 1], held_b, grad_sems.at[1]),
    ]
    for copy in grads:
        copy.start()
    for r in (3, 1, 2, 0):
        hidden_copy(r).start()
    start()
    for copy in grads:
        copy.wait()
    wide = grad_a.shape[-1]
    packed[:, :wide] = held_a[...].astype(BF)
    packed[:, wide:] = held_b[...].astype(BF)
    for r in (3, 1, 2, 0):
        hidden_copy(r).wait()
        x[r * tokens : (r + 1) * tokens] = held[r].reshape(tokens, x.shape[1])
    run()


def keep_kernel(x, weight, after, kkeep, vkeep0, vkeep1, _, w, sems):
    del after
    tokens = x.shape[0] // 4
    start, run = multiply_terms(x, weight, 0, w, sems, *keep_parts(tokens, kkeep, vkeep0, vkeep1))
    start()
    run()


def later_kernel(x, weight, after, *rest):
    del after
    ksend, vsend, kkeep, vkeep0, vkeep1, w, sems = rest
    tokens = x.shape[0] // 4
    sends = send_parts(tokens, ksend, vsend)
    keeps = keep_parts(tokens, kkeep, vkeep0, vkeep1)
    base = weight.shape[2] - w.shape[1] * TILE
    parts = [a + b for a, b in zip(sends, keeps)]
    start, run = multiply_terms(x, weight, base, w, sems, *parts)
    start()
    run()


SEND, KEEP = (2, 2), (2, 1, 1)


def term_shapes(rows, tokens, count):
    return [jax.ShapeDtypeStruct((n * tokens, count * HD), BF) for n in rows]


def weight_scratch(width, count):
    tiles = count * HD // TILE
    return [pltpu.VMEM((2, tiles, width, TILE), BF), pltpu.SemaphoreType.DMA((2, tiles))]


def first_terms(ids, hidden, kv_weight, grad_a, grad_b, tokens):
    width = hidden.shape[2]
    here = pl.BlockSpec(memory_space=pl.ANY)
    outs = [jax.ShapeDtypeStruct((4 * tokens, width), BF)]
    outs += [pltpu.VMEM(x.shape, BF) for x in term_shapes(SEND, tokens, CHUNKS[0])]
    outs.append(jax.ShapeDtypeStruct((grad_a.shape[2], grad_a.shape[3] + grad_b.shape[3]), BF))
    w, sems = weight_scratch(width, CHUNKS[0])
    return pl.pallas_call(
        first_kernel,
        out_shape=outs,
        grid_spec=pltpu.PrefetchScalarGridSpec(
            num_scalar_prefetch=1,
            grid=(1,),
            in_specs=[here] * 4,
            out_specs=[whole(x.shape) for x in outs],
            scratch_shapes=[
                pltpu.VMEM((4, tokens // STEPS, STEPS, width), BF),
                w,
                pltpu.VMEM(grad_a.shape[2:], F32),
                pltpu.VMEM(grad_b.shape[2:], F32),
                pltpu.SemaphoreType.DMA((4,)),
                sems,
                pltpu.SemaphoreType.DMA((2,)),
            ],
        ),
        compiler_params=params(16),
        cost_estimate=cost(8 * tokens * width * CHUNKS[0] * HD, hidden),
        name="first_terms",
    )(ids, *map(hbm, (hidden, kv_weight, grad_a, grad_b)))


def keep_terms(x, kv_weight, queries, after):
    tokens, width = x.shape[0] // 4, x.shape[1]
    here = pl.BlockSpec(memory_space=pl.ANY)
    outs = [pltpu.HBM(out.shape, BF) for out in term_shapes(KEEP, tokens, CHUNKS[0])]
    specs = [whole(out.shape) for out in outs] + [here]
    outs.append(jax.ShapeDtypeStruct(queries.shape, BF))
    return pl.pallas_call(
        keep_kernel,
        out_shape=outs,
        grid=(1,),
        in_specs=[whole(x.shape), here, here],
        out_specs=specs,
        scratch_shapes=weight_scratch(width, CHUNKS[0]),
        compiler_params=params(14),
        cost_estimate=cost(8 * tokens * width * CHUNKS[0] * HD, x),
        name="keep_terms",
    )(x, hbm(kv_weight), after)


def later_terms(x, kv_weight, after):
    outs = term_shapes(SEND + KEEP, x.shape[0] // 4, CHUNKS[1])
    here = pl.BlockSpec(memory_space=pl.ANY)
    return pl.pallas_call(
        later_kernel,
        out_shape=outs,
        grid=(1,),
        in_specs=[whole(x.shape), here, here],
        out_specs=[whole(out.shape) for out in outs],
        scratch_shapes=weight_scratch(x.shape[1], CHUNKS[1]),
        compiler_params=params(12),
        cost_estimate=cost(4 * math.prod(x.shape) * CHUNKS[1] * HD, x, *outs),
        name="later_terms",
    )(x, hbm(kv_weight), after)


def mid_kernel(kkeep, kcame, vkeep, vcame, *rest):
    kout, vout = rest[-2:]
    kout[...] = (kkeep[...].astype(F32) + kcame[...].astype(F32)).astype(BF)
    vout[...] = (vkeep[...].astype(F32) + vcame[...].astype(F32)).astype(BF)


def mid_sums(kkeep, kcame, vkeep, vcame, *after):
    shape = vkeep.shape
    low = pl.BlockSpec(shape, lambda i: (0, 0))
    high = pl.BlockSpec(shape, lambda i: (1, 0))
    return pl.pallas_call(
        mid_kernel,
        out_shape=[jax.ShapeDtypeStruct(shape, BF)] * 2,
        grid=(1,),
        in_specs=[high, low, low, high] + [pl.BlockSpec(memory_space=pl.ANY)] * len(after),
        out_specs=[low, low],
        compiler_params=params(4),
        cost_estimate=cost(0, *[vkeep] * 6),
        name="mid_sums",
    )(kkeep, kcame, vkeep, vcame, *after)


def chip_kernel(ids, grad_a, grad_b, other, out):
    del ids
    wide = grad_a.shape[-1]
    out[:, :wide] = (grad_a[0, 0] + other[:, :wide].astype(F32)).astype(BF)
    out[:, wide:] = (grad_b[0, 0] + other[:, wide:].astype(F32)).astype(BF)


def chip_grads(ids, grad_a, grad_b, other):
    def half(x):
        return pl.BlockSpec((1, 1) + x.shape[2:], lambda i, ids: (0, ids[2], 0, 0))

    return pl.pallas_call(
        chip_kernel,
        out_shape=jax.ShapeDtypeStruct(other.shape, BF),
        grid_spec=pltpu.PrefetchScalarGridSpec(
            num_scalar_prefetch=1,
            grid=(1,),
            in_specs=[half(grad_a), half(grad_b), whole(other.shape)],
            out_specs=whole(other.shape),
        ),
        compiler_params=params(4),
        cost_estimate=cost(0, *[other] * 4),
        name="chip_grads",
    )(ids, hbm(grad_a), hbm(grad_b), other)


def small_call(kernel, name, ids, args, outs, after=(), scratch=(), copied=0):
    count = len(args)

    def body(ids, *refs):
        kernel(ids, *refs[:count], *refs[count + len(after) :])

    return pl.pallas_call(
        body,
        out_shape=outs,
        grid_spec=pltpu.PrefetchScalarGridSpec(
            num_scalar_prefetch=1,
            grid=(1,),
            in_specs=[whole(x.shape) for x in args]
            + [pl.BlockSpec(memory_space=pl.ANY)] * len(after),
            out_specs=[pl.BlockSpec(memory_space=pltpu.HBM)] * copied
            + [whole(x.shape) for x in outs[copied:]],
            scratch_shapes=list(scratch),
        ),
        compiler_params=params(8),
        cost_estimate=cost(0, *args),
        name=name,
    )(ids, *args, *after)


def core_flip(x, count):
    return lax.ppermute(x, "dp", [(i, i ^ 1) for i in range(count)])


def plus_kernel(a, b, *rest):
    rest[-1][...] = (a[...].astype(F32) + b[...].astype(F32)).astype(BF)


def plus(a, b, *after):
    return plus_handing(a, b, *after)[0]


def plus_handing(a, b, *after, handed=()):
    out = jax.ShapeDtypeStruct(a.shape, BF)
    here = pl.BlockSpec(memory_space=pl.ANY)
    count = 2 + len(after)

    def kernel(a, b, *rest):
        plus_kernel(a, b, rest[len(after) + len(handed)])

    return pl.pallas_call(
        kernel,
        out_shape=[out] + [jax.ShapeDtypeStruct(x.shape, x.dtype) for x in handed],
        grid=(1,),
        in_specs=[whole(a.shape)] * 2 + [here] * (len(after) + len(handed)),
        out_specs=[whole(a.shape)] + [here] * len(handed),
        input_output_aliases={count + n: 1 + n for n in range(len(handed))},
        compiler_params=params(2),
        cost_estimate=cost(0, a, b, out),
        name="plus",
    )(a, b, *after, *handed)


def along_line(x, d, count):
    return lax.ppermute(x, "dp", [(i, i ^ (2 * d)) for i in range(count)])


TOP = 2 * R


def update_kernel(rates, ids, half, other, factor_a, factor_b, x, out_a, out_b, *rest):
    *sends, a, new_a, new_b, sems = rest
    copies = [
        pltpu.make_async_copy(new_a, out_a, sems.at[0]),
        pltpu.make_async_copy(new_b, out_b, sems.at[1]),
    ]
    wide = factor_a.shape[-1]
    for index, part in ((ids[2], half), (ids[2] ^ 1, other)):
        new_a[index] = factor_a[index] - rates[0] * part[:, :wide].astype(F32)
        new_b[index] = factor_b[index] - rates[1] * part[:, wide:].astype(F32)
    for copy in copies:
        copy.start()
    for p in range(2):
        a[p * R : (p + 1) * R] = new_a[p].astype(BF)
    a[TOP:] = jnp.zeros((TILE - TOP, wide), BF)
    tokens = x.shape[0] // 4

    def multiply(*accs):
        steps = wide // TILE

        def push(k):
            for unit in range(2):
                tile = a[:, k * TILE : (k + 1) * TILE]
                pltpu.matmul_push_rhs(tile, k % 2, unit, transpose=True)

        push(0)
        for k in range(steps):
            if k + 1 < steps:
                push(k + 1)
            for r in range(4):
                rows = x[r * tokens : (r + 1) * tokens, k * TILE : (k + 1) * TILE]
                staged = k % 2 if r < 2 else None
                pltpu.matmul_acc_lhs(accs[r], rows, load_staged_rhs=staged)
        for r, send in enumerate(sends):
            u = (0.25 * pltpu.matmul_pop(accs[r])[:, :TOP]).astype(BF)
            for p in range(2):
                send[p * R : (p + 1) * R, :] = new_b[p].astype(BF)
            send[TOP:, :TOP] = u[:TOP]
            send[TOP:tokens, TOP:] = u[TOP:]
            send[tokens:, TOP:] = jnp.zeros((2 * TOP - tokens, TOP), BF)

    pl.run_scoped(multiply, *[pltpu.ACC(r % 2)((tokens, TILE), F32) for r in range(4)])
    for copy in copies:
        copy.wait()


def updated(ids, half, other, factor_a, factor_b, x, dp, *after):
    rates = (2.0 / math.sqrt(dp * D), 2.0 / math.sqrt(dp * R))
    outs = [pltpu.HBM(f.shape, F32) for f in (factor_a, factor_b)]
    outs += [jax.ShapeDtypeStruct((2 * TOP, 2 * TOP), BF)] * 4
    return small_call(
        functools.partial(update_kernel, rates),
        "update_factors",
        ids,
        (half, other, factor_a, factor_b, x),
        outs,
        after,
        [
            pltpu.VMEM((TILE, factor_a.shape[-1]), BF),
            pltpu.VMEM(factor_a.shape, F32),
            pltpu.VMEM(factor_b.shape, F32),
            pltpu.SemaphoreType.DMA((2,)),
        ],
        2,
    )


def attend_kernel(ids, first, lengths, *refs):
    q, cache_k, cache_v, k0, k1, k2, v0, v1, v2, *ub, cosine, sine = refs[:15]
    out = refs[-3]
    rows, slots, _ = cache_k.shape
    tokens = rows * STEPS
    u_held, b_held = refs[-2:]

    @pl.when(pl.program_id(0) == 0)
    def _():
        u_held[:TOP] = sum(x[TOP:, :TOP].astype(F32) for x in ub).astype(BF)
        u_held[TOP:] = sum(x[TOP:tokens, TOP:].astype(F32) for x in ub).astype(BF)

    rel = ids[0] ^ (first[0] + pl.program_id(0))
    for r, x in enumerate(ub):

        @pl.when(rel == r)
        def _():
            b_held[...] = x[:TOP]

    u, b = u_held[...], b_held[...]
    k = k0[...].astype(F32) + k1[...].astype(F32) + k2[...].astype(F32) + dot(u[:, :R], b[:R])
    v = v0[...].astype(F32) + v1[...].astype(F32) + v2[...].astype(F32) + dot(u[:, R:], b[R:])
    v = v.astype(BF)
    keys = []
    for n in range(HEADS_STEP):
        key = k[:, n * HD : (n + 1) * HD]
        scale = lax.rsqrt(jnp.sum(key * key, axis=-1, keepdims=True) * (1.0 / HD) + 1e-06)
        key = scale * (key * cosine[...] + pltpu.roll(key, HD // 2, 1) * sine[...])
        keys.append(key.astype(BF))
    n_q, n_c = GROUP * STEPS, GROUP * slots
    shape = (n_q, n_c + n_q)
    here = lax.broadcasted_iota(jnp.int32, shape, 0)
    col = lax.broadcasted_iota(jnp.int32, shape, 1)
    fresh = col - n_c
    cached = (col < n_c) & (here // STEPS == col // slots)
    new = (col >= n_c) & (here // STEPS == fresh // STEPS) & (fresh % STEPS <= here % STEPS)
    bias_here = jnp.where(cached | new, 0.0, -1e30)
    col = lax.broadcasted_iota(jnp.int32, (1, n_c + n_q), 1)
    ones = jnp.ones((n_c + n_q, HD), BF)
    factor = math.log2(math.e) * HD**-0.5
    heads = QH // KVH
    blocks = rows // GROUP
    query = q[...].reshape(tokens, HEADS_STEP * heads * HD)

    def block(n, g, cache, fresh):
        old = cache[g * GROUP : (g + 1) * GROUP, :, n * HD : (n + 1) * HD].reshape(n_c, HD)
        return jnp.concatenate([old, fresh[g * n_q : (g + 1) * n_q]], axis=0)

    every = [(n, g) for n in range(HEADS_STEP) for g in range(blocks)]
    scores = []
    for n, g in every:
        part = [query[g * n_q : (g + 1) * n_q, h * HD : (h + 1) * HD] for h in range(n * heads, (n + 1) * heads)]
        scores.append(dot_t(jnp.concatenate(part, axis=0), block(n, g, cache_k, keys[n])))
    biases = []
    for g in range(blocks):
        filled = jnp.full(col.shape, lengths[g * GROUP], jnp.int32)
        for i in range(1, GROUP):
            filled = jnp.where(col // slots == i, lengths[g * GROUP + i], filled)
        bias = jnp.where((col >= n_c) | (col % slots < filled), 0.0, -1e30) + bias_here
        biases.append(jnp.concatenate([bias] * heads, axis=0))
    weights = []
    for (n, g), s in zip(every, scores):
        s = s * factor + biases[g]
        top = jnp.max(s, axis=-1, keepdims=True)
        weights.append(jnp.exp2(s - top).astype(BF))
    results = []
    for (n, g), w in zip(every, weights):
        here_v = block(n, g, cache_v, v[:, n * HD : (n + 1) * HD])
        r = dot(w, jnp.concatenate([here_v, ones], axis=1))
        total = r[:, HD:]
        inverse = pl.reciprocal(total, approx=True)
        inverse = inverse * (2.0 - total * inverse)
        results.append((r[:, :HD] * inverse).astype(BF))
    for n in range(HEADS_STEP):
        for h in range(heads):
            part = [r[h * n_q : (h + 1) * n_q] for r in results[n * blocks : (n + 1) * blocks]]
            at = (n * heads + h) * HD
            out[:, :, at : at + HD] = jnp.concatenate(part, axis=0).reshape(rows, STEPS, HD)


def attend_chunk(
    ids, lengths, start, count, queries, cache_keys, cache_values, terms, ub, tables, before
):
    rows, slots, _ = cache_keys.shape
    tokens = rows * STEPS
    heads = QH // KVH
    args = [queries, cache_keys, cache_values, *terms, *ub, *tables]
    assert start % HEADS_STEP == 0 and count % HEADS_STEP == 0
    first = jnp.full((1,), start // HEADS_STEP, jnp.int32)
    size = HEADS_STEP * HD
    part = pl.BlockSpec((tokens, size), lambda i, *_: (0, i))
    low = pl.BlockSpec((tokens, size), lambda i, *_: (1, i))
    cache = pl.BlockSpec((rows, slots, size), lambda i, _, first, *__: (0, 0, first[0] + i))
    wide = pl.BlockSpec((rows, STEPS, heads * size), lambda i, _, first, *__: (0, 0, first[0] + i))
    specs = [wide, cache, cache, part, low, part, part, part, part]
    specs += [whole(x.shape) for x in (*ub, *tables)]
    args.append(before)
    specs.append(pl.BlockSpec(memory_space=pl.ANY))
    return pl.pallas_call(
        attend_kernel,
        out_shape=jax.ShapeDtypeStruct(queries.shape, BF),
        grid_spec=pltpu.PrefetchScalarGridSpec(
            num_scalar_prefetch=3, grid=(count // HEADS_STEP,), in_specs=specs, out_specs=wide,
            scratch_shapes=[pltpu.VMEM((tokens, TOP), BF), pltpu.VMEM((TOP, size), BF)],
        ),
        input_output_aliases={len(args) + 2: 0},
        compiler_params=params(14),
        cost_estimate=cost(count * 4 * 10**9, *args),
        name="attend_chunk",
    )(ids, first, lengths, *args)


def rotary_tables(key_gain, positions):
    half = HD // 2
    place = positions[:, None] + jnp.arange(STEPS, dtype=jnp.int32)[None, :]
    freq = jnp.exp(-math.log(1000000.0) * (jnp.arange(half, dtype=F32) * 2.0 / HD))
    angle = place.reshape(-1).astype(F32)[:, None] * jnp.concatenate([freq, freq])
    turned = jnp.concatenate([-key_gain[half:], key_gain[:half]])
    return jnp.cos(angle) * key_gain, jnp.sin(angle) * turned


def across(x, r):
    return lax.ppermute(x, "tensor", [(i, i ^ r) for i in range(4)])


def square(
    hidden_in,
    kv_weight,
    factor_a,
    factor_b,
    grad_a,
    grad_b,
    key_gain,
    queries,
    cache_keys,
    cache_values,
    cache_lengths,
    positions,
):
    tokens = cache_keys.shape[0] * STEPS
    count_dp = lax.axis_size("dp")
    dp = lax.axis_index("dp")
    ids = jnp.stack([lax.axis_index("tensor"), dp // 2, dp % 2]).astype(jnp.int32)
    tables = rotary_tables(key_gain, positions)

    x, *first, packed = first_terms(ids, hidden_in, kv_weight, grad_a, grad_b, tokens)
    half = chip_grads(ids, grad_a, grad_b, core_flip(packed, count_dp))

    def first_exchange(term, *after):
        ksend, vsend, kkeep, vkeep0, vkeep1 = term
        kcame, vcame = across(ksend, 1), across(vsend, 2)
        mids = mid_sums(kkeep, kcame, vkeep1, vcame, *after)
        return mids, (kkeep, kcame, vkeep0, vcame)

    def second_exchange(mids, parts):
        kkeep, kcame, vkeep0, vcame = parts
        return kkeep, kcame, across(mids[0], 2), vkeep0, vcame, across(mids[1], 1)

    second = later_terms(x, kv_weight, half)
    step, after = 1, second[:1]
    while 2 * step < count_dp:
        came = along_line(half, step, count_dp)
        if step == 1:
            half, *sends = plus_handing(half, came, handed=second[:2])
            second = [*sends, *second[2:]]
        else:
            half = plus(half, came, *after)
        step *= 2
        if step == 2:
            *keeps, attended = keep_terms(x, kv_weight, queries, half)
            first += keeps
            mids, parts = first_exchange(first, half)
            after = (mids[0], tables[0])
    if step == 1:
        *keeps, attended = keep_terms(x, kv_weight, queries, half)
        first += keeps
        mids, parts = first_exchange(first, half)
    first = second_exchange(mids, parts)
    other = core_flip(half, count_dp)
    new_a, new_b, *sends = updated(
        ids, half, other, factor_a, factor_b, x, count_dp
    )
    ub = [sends[0]] + [across(sends[r], r) for r in (1, 2, 3)]
    second = second_exchange(*first_exchange(second, ub[1]))
    for start, count, came in ((0, CHUNKS[0], first), (CHUNKS[0], CHUNKS[1], second)):
        attended = attend_chunk(
            ids,
            cache_lengths,
            start,
            count,
            queries,
            cache_keys,
            cache_values,
            came,
            ub,
            tables,
            attended,
        )
    return attended, new_a, new_b


def solution(mesh):
    fits = mesh.shape["tensor"] == 4 and mesh.shape["dp"] in (2, 4, 8)
    return jax.shard_map(
        square if fits else general,
        mesh=mesh,
        in_specs=(
            P("dp", None, "tensor"),
            P(None, "tensor", None),
            P(None, None, "tensor"),
            P(None, None, "tensor"),
            P("dp", None, None, "tensor"),
            P("dp", None, None, "tensor"),
            P(),
            P(("dp", "tensor"), None, None),
            P(("dp", "tensor"), None, None),
            P(("dp", "tensor"), None, None),
            P(("dp", "tensor")),
            P(("dp", "tensor")),
        ),
        out_specs=(
            P(("dp", "tensor"), None, None),
            P(None, None, "tensor"),
            P(None, None, "tensor"),
        ),
        check_vma=False,
    )
```

```python
import functools
import math

import jax
import jax.numpy as jnp
from jax import lax
from jax.experimental import pallas as pl
from jax.experimental.pallas import tpu as pltpu
from jax.sharding import PartitionSpec as P

D = 5120
KVH = 8
HD = 128
QH = 32
R = 64
STEPS = 4
BF = jnp.bfloat16
F32 = jnp.float32
MIB = 1024 * 1024


def normed_rotated(keys, gain, position):
    scale = lax.rsqrt(jnp.mean(keys * keys, axis=-1, keepdims=True) + 1e-06)
    keys = keys * scale * gain
    half = keys.shape[-1] // 2
    freq = jnp.exp(
        -math.log(1000000.0) * (jnp.arange(half, dtype=jnp.float32) * 2.0 / keys.shape[-1])
    )
    angle = position.astype(jnp.float32)[..., None] * freq
    cosine = jnp.concatenate([jnp.cos(angle), jnp.cos(angle)], axis=-1)[..., None, :]
    sine = jnp.concatenate([jnp.sin(angle), jnp.sin(angle)], axis=-1)[..., None, :]
    turned = jnp.concatenate([-keys[..., half:], keys[..., :half]], axis=-1)
    return keys * cosine + turned * sine


def attend(queries, cache_keys, cache_values, new_keys, new_values, lengths):
    rows, steps, width = queries.shape
    slots = cache_keys.shape[1]
    slot = jnp.arange(slots, dtype=jnp.int32)
    for step in range(steps):
        hit = (slot[None, :] == lengths[:, None] + step)[:, :, None]
        cache_keys = jnp.where(hit, new_keys[:, step][:, None, :], cache_keys)
        cache_values = jnp.where(hit, new_values[:, step][:, None, :], cache_values)
    groups = QH // KVH
    query_five = queries.reshape(rows, steps, KVH, groups, HD)
    key_four = cache_keys.reshape(rows, slots, KVH, HD)
    value_four = cache_values.reshape(rows, slots, KVH, HD)
    scores = jnp.einsum(
        "rtkgd,rckd->rtkgc", query_five, key_four, preferred_element_type=jnp.float32
    ) * HD ** (-0.5)
    limit = lengths[:, None] + jnp.arange(steps, dtype=jnp.int32)[None, :]
    valid = (slot[None, None, :] <= limit[:, :, None])[:, :, None, None, :]
    scores = jnp.where(valid, scores, jnp.float32(-1e30))
    top = jnp.max(scores, axis=-1, keepdims=True)
    expo = jnp.exp(scores - top)
    weights = (expo / jnp.sum(expo, axis=-1, keepdims=True)).astype(jnp.bfloat16)
    result = jnp.einsum(
        "rtkgc,rckd->rtkgd", weights, value_four, preferred_element_type=jnp.float32
    )
    return result.reshape(rows, steps, width).astype(jnp.bfloat16)


def general(
    hidden_in,
    kv_weight,
    factor_a,
    factor_b,
    grad_a,
    grad_b,
    key_gain,
    queries,
    cache_keys,
    cache_values,
    cache_lengths,
    positions,
):
    groups_dp = lax.axis_size("dp")
    rate_a = 2.0 / math.sqrt(groups_dp * D)
    rate_b = 2.0 / math.sqrt(groups_dp * R)
    sum_a, sum_b = (
        lax.psum(grad_a[0].astype(jnp.bfloat16), "dp").astype(jnp.float32),
        lax.psum(grad_b[0].astype(jnp.bfloat16), "dp").astype(jnp.float32),
    )
    new_a = factor_a - rate_a * sum_a
    new_b = factor_b - rate_b * sum_b
    full_b = lax.all_gather(new_b.astype(jnp.bfloat16), "tensor", axis=2, tiled=True).astype(
        new_b.dtype
    )
    delta = jnp.einsum("prd,prk->pdk", new_a, full_b, precision=lax.Precision.HIGHEST)
    merged = (kv_weight.astype(jnp.float32) + 0.25 * delta).astype(jnp.bfloat16)
    joined = jnp.concatenate([merged[0], merged[1]], axis=1)
    rows_here = hidden_in.shape[0] // lax.axis_size("tensor")
    pieces = []
    for step in range(STEPS):
        term = jnp.dot(hidden_in[:, step, :], joined, preferred_element_type=jnp.float32)
        pieces.append(
            lax.psum_scatter(
                term.astype(jnp.bfloat16), "tensor", scatter_dimension=0, tiled=True
            ).astype(jnp.float32)
        )
    projected = jnp.stack(pieces, axis=1)
    kv_width = KVH * HD
    place = positions[:, None] + jnp.arange(STEPS, dtype=jnp.int32)[None, :]
    keys = normed_rotated(
        projected[..., :kv_width].reshape(rows_here, STEPS, KVH, HD), key_gain, place
    )
    new_keys = keys.reshape(rows_here, STEPS, kv_width).astype(jnp.bfloat16)
    new_values = projected[..., kv_width:].astype(jnp.bfloat16)
    attended = attend(queries, cache_keys, cache_values, new_keys, new_values, cache_lengths)
    return (attended, new_a, new_b)


CHUNKS = (4, 4)
GROUP = 4
HEADS_STEP = 2


def params(mib):
    return pltpu.CompilerParams(vmem_limit_bytes=mib * MIB)


def cost(flops, *arrays):
    size = sum(math.prod(x.shape) * x.dtype.itemsize for x in arrays)
    return pl.CostEstimate(flops=flops, bytes_accessed=size, transcendentals=0)


def dot(a, b):
    return jnp.dot(a, b, preferred_element_type=F32)


def dot_t(a, b):
    return lax.dot_general(a, b, (((1,), (1,)), ((), ())), preferred_element_type=F32)


def whole(shape):
    return pl.BlockSpec(shape, lambda i, *_: (0,) * len(shape))


def hbm(x):
    return pltpu.with_memory_space_constraint(x, pltpu.HBM)


TILE = 256


def multiply_terms(x, weight, base, w, sems, keys, values):
    tokens = x.shape[0] // 4
    steps = x.shape[1] // TILE
    units = (keys, values)

    def copy(p, i):
        at = pl.ds(base + i * TILE, TILE)
        return pltpu.make_async_copy(weight.at[p, :, at], w.at[p, i], sems.at[p, i])

    def start():
        for i in range(w.shape[1]):
            for p in range(2):
                copy(p, i).start()

    def multiply(*accs):
        accs = (accs[: len(keys)], accs[len(keys) :])

        @pl.loop(0, w.shape[1])
        def _(i):
            for p in range(2):
                copy(p, i).wait()

            def push(k):
                for p in range(2):
                    pltpu.matmul_push_rhs(w[p, i, k * TILE : (k + 1) * TILE, :], k % 2, p)

            push(0)
            for k in range(steps):
                if k + 1 < steps:
                    push(k + 1)
                for n in range(len(keys)):
                    for p in range(2):
                        r = units[p][n][0]
                        rows = x[r * tokens : (r + 1) * tokens, k * TILE : (k + 1) * TILE]
                        staged = k % 2 if n == 0 else None
                        pltpu.matmul_acc_lhs(accs[p][n], rows, load_staged_rhs=staged)
            at = pl.ds(pl.multiple_of(i * TILE, TILE), TILE)
            for n in range(len(keys)):
                for p in range(2):
                    _, out, row = units[p][n]
                    out[row : row + tokens, at] = pltpu.matmul_pop(accs[p][n]).astype(BF)

    def run():
        pl.run_scoped(
            multiply,
            *[pltpu.ACC(p)((tokens, TILE), F32) for p in range(2) for _ in units[p]],
        )

    return start, run


def send_parts(tokens, ksend, vsend):
    return [(3, ksend, 0), (1, ksend, tokens)], [(2, vsend, 0), (3, vsend, tokens)]


def keep_parts(tokens, kkeep, vkeep0, vkeep1):
    return [(0, kkeep, 0), (2, kkeep, tokens)], [(0, vkeep0, 0), (1, vkeep1, 0)]


def first_kernel(ids, hidden, weight, grad_a, grad_b, x, ksend, vsend, packed, *scratch):
    held, w, held_a, held_b, hidden_sems, sems, grad_sems = scratch
    tokens = x.shape[0] // 4
    rows = tokens // STEPS
    start, run = multiply_terms(x, weight, 0, w, sems, *send_parts(tokens, ksend, vsend))

    def hidden_copy(r):
        at = pl.ds((ids[0] ^ r) * rows, rows)
        return pltpu.make_async_copy(hidden.at[at], held.at[r], hidden_sems.at[r])

    grads = [
        pltpu.make_async_copy(grad_a.at[0, ids[2] ^ 1], held_a, grad_sems.at[0]),
        pltpu.make_async_copy(grad_b.at[0, ids[2] ^ 1], held_b, grad_sems.at[1]),
    ]
    for copy in grads:
        copy.start()
    for r in (3, 1, 2, 0):
        hidden_copy(r).start()
    start()
    for copy in grads:
        copy.wait()
    wide = grad_a.shape[-1]
    packed[:, :wide] = held_a[...].astype(BF)
    packed[:, wide:] = held_b[...].astype(BF)
    for r in (3, 1, 2, 0):
        hidden_copy(r).wait()
        x[r * tokens : (r + 1) * tokens] = held[r].reshape(tokens, x.shape[1])
    run()


def keep_kernel(x, weight, after, kkeep, vkeep0, vkeep1, _, w, sems):
    del after
    tokens = x.shape[0] // 4
    start, run = multiply_terms(x, weight, 0, w, sems, *keep_parts(tokens, kkeep, vkeep0, vkeep1))
    start()
    run()


def later_kernel(x, weight, after, *rest):
    del after
    ksend, vsend, kkeep, vkeep0, vkeep1, w, sems = rest
    tokens = x.shape[0] // 4
    sends = send_parts(tokens, ksend, vsend)
    keeps = keep_parts(tokens, kkeep, vkeep0, vkeep1)
    base = weight.shape[2] - w.shape[1] * TILE
    parts = [a + b for a, b in zip(sends, keeps)]
    start, run = multiply_terms(x, weight, base, w, sems, *parts)
    start()
    run()


SEND, KEEP = (2, 2), (2, 1, 1)


def term_shapes(rows, tokens, count):
    return [jax.ShapeDtypeStruct((n * tokens, count * HD), BF) for n in rows]


def weight_scratch(width, count):
    tiles = count * HD // TILE
    return [pltpu.VMEM((2, tiles, width, TILE), BF), pltpu.SemaphoreType.DMA((2, tiles))]


def first_terms(ids, hidden, kv_weight, grad_a, grad_b, tokens):
    width = hidden.shape[2]
    here = pl.BlockSpec(memory_space=pl.ANY)
    outs = [jax.ShapeDtypeStruct((4 * tokens, width), BF)]
    outs += [pltpu.VMEM(x.shape, BF) for x in term_shapes(SEND, tokens, CHUNKS[0])]
    outs.append(jax.ShapeDtypeStruct((grad_a.shape[2], grad_a.shape[3] + grad_b.shape[3]), BF))
    w, sems = weight_scratch(width, CHUNKS[0])
    return pl.pallas_call(
        first_kernel,
        out_shape=outs,
        grid_spec=pltpu.PrefetchScalarGridSpec(
            num_scalar_prefetch=1,
            grid=(1,),
            in_specs=[here] * 4,
            out_specs=[whole(x.shape) for x in outs],
            scratch_shapes=[
                pltpu.VMEM((4, tokens // STEPS, STEPS, width), BF),
                w,
                pltpu.VMEM(grad_a.shape[2:], F32),
                pltpu.VMEM(grad_b.shape[2:], F32),
                pltpu.SemaphoreType.DMA((4,)),
                sems,
                pltpu.SemaphoreType.DMA((2,)),
            ],
        ),
        compiler_params=params(16),
        cost_estimate=cost(8 * tokens * width * CHUNKS[0] * HD, hidden),
        name="first_terms",
    )(ids, *map(hbm, (hidden, kv_weight, grad_a, grad_b)))


def keep_terms(x, kv_weight, queries, after):
    tokens, width = x.shape[0] // 4, x.shape[1]
    here = pl.BlockSpec(memory_space=pl.ANY)
    outs = term_shapes(KEEP, tokens, CHUNKS[0])
    specs = [whole(out.shape) for out in outs] + [here]
    outs.append(jax.ShapeDtypeStruct(queries.shape, BF))
    return pl.pallas_call(
        keep_kernel,
        out_shape=outs,
        grid=(1,),
        in_specs=[whole(x.shape), here, here],
        out_specs=specs,
        scratch_shapes=weight_scratch(width, CHUNKS[0]),
        compiler_params=params(14),
        cost_estimate=cost(8 * tokens * width * CHUNKS[0] * HD, x),
        name="keep_terms",
    )(x, hbm(kv_weight), after)


def later_terms(x, kv_weight, after):
    outs = term_shapes(SEND + KEEP, x.shape[0] // 4, CHUNKS[1])
    here = pl.BlockSpec(memory_space=pl.ANY)
    return pl.pallas_call(
        later_kernel,
        out_shape=outs,
        grid=(1,),
        in_specs=[whole(x.shape), here, here],
        out_specs=[whole(out.shape) for out in outs],
        scratch_shapes=weight_scratch(x.shape[1], CHUNKS[1]),
        compiler_params=params(12),
        cost_estimate=cost(4 * math.prod(x.shape) * CHUNKS[1] * HD, x, *outs),
        name="later_terms",
    )(x, hbm(kv_weight), after)


def mid_kernel(kkeep, kcame, vkeep, vcame, *rest):
    kout, vout = rest[-2:]
    kout[...] = (kkeep[...].astype(F32) + kcame[...].astype(F32)).astype(BF)
    vout[...] = (vkeep[...].astype(F32) + vcame[...].astype(F32)).astype(BF)


def mid_sums(kkeep, kcame, vkeep, vcame, *after):
    shape = vkeep.shape
    low = pl.BlockSpec(shape, lambda i: (0, 0))
    high = pl.BlockSpec(shape, lambda i: (1, 0))
    return pl.pallas_call(
        mid_kernel,
        out_shape=[jax.ShapeDtypeStruct(shape, BF)] * 2,
        grid=(1,),
        in_specs=[high, low, low, high] + [pl.BlockSpec(memory_space=pl.ANY)] * len(after),
        out_specs=[low, low],
        compiler_params=params(4),
        cost_estimate=cost(0, *[vkeep] * 6),
        name="mid_sums",
    )(kkeep, kcame, vkeep, vcame, *after)


def chip_kernel(ids, grad_a, grad_b, other, out):
    del ids
    wide = grad_a.shape[-1]
    out[:, :wide] = (grad_a[0, 0] + other[:, :wide].astype(F32)).astype(BF)
    out[:, wide:] = (grad_b[0, 0] + other[:, wide:].astype(F32)).astype(BF)


def chip_grads(ids, grad_a, grad_b, other):
    def half(x):
        return pl.BlockSpec((1, 1) + x.shape[2:], lambda i, ids: (0, ids[2], 0, 0))

    return pl.pallas_call(
        chip_kernel,
        out_shape=jax.ShapeDtypeStruct(other.shape, BF),
        grid_spec=pltpu.PrefetchScalarGridSpec(
            num_scalar_prefetch=1,
            grid=(1,),
            in_specs=[half(grad_a), half(grad_b), whole(other.shape)],
            out_specs=whole(other.shape),
        ),
        compiler_params=params(4),
        cost_estimate=cost(0, *[other] * 4),
        name="chip_grads",
    )(ids, hbm(grad_a), hbm(grad_b), other)


def small_call(kernel, name, ids, args, outs, after=(), scratch=(), copied=0):
    count = len(args)

    def body(ids, *refs):
        kernel(ids, *refs[:count], *refs[count + len(after) :])

    return pl.pallas_call(
        body,
        out_shape=outs,
        grid_spec=pltpu.PrefetchScalarGridSpec(
            num_scalar_prefetch=1,
            grid=(1,),
            in_specs=[whole(x.shape) for x in args]
            + [pl.BlockSpec(memory_space=pl.ANY)] * len(after),
            out_specs=[pl.BlockSpec(memory_space=pltpu.HBM)] * copied
            + [whole(x.shape) for x in outs[copied:]],
            scratch_shapes=list(scratch),
        ),
        compiler_params=params(8),
        cost_estimate=cost(0, *args),
        name=name,
    )(ids, *args, *after)


def core_flip(x, count):
    return lax.ppermute(x, "dp", [(i, i ^ 1) for i in range(count)])


def plus_kernel(a, b, *rest):
    rest[-1][...] = (a[...].astype(F32) + b[...].astype(F32)).astype(BF)


def plus(a, b, *after):
    return plus_handing(a, b, *after)[0]


def plus_handing(a, b, *after, handed=()):
    out = jax.ShapeDtypeStruct(a.shape, BF)
    here = pl.BlockSpec(memory_space=pl.ANY)
    count = 2 + len(after)

    def kernel(a, b, *rest):
        plus_kernel(a, b, rest[len(after) + len(handed)])

    return pl.pallas_call(
        kernel,
        out_shape=[out] + [jax.ShapeDtypeStruct(x.shape, x.dtype) for x in handed],
        grid=(1,),
        in_specs=[whole(a.shape)] * 2 + [here] * (len(after) + len(handed)),
        out_specs=[whole(a.shape)] + [here] * len(handed),
        input_output_aliases={count + n: 1 + n for n in range(len(handed))},
        compiler_params=params(2),
        cost_estimate=cost(0, a, b, out),
        name="plus",
    )(a, b, *after, *handed)


def along_line(x, d, count):
    return lax.ppermute(x, "dp", [(i, i ^ (2 * d)) for i in range(count)])


TOP = 2 * R


def update_kernel(rates, ids, half, other, factor_a, factor_b, x, out_a, out_b, *rest):
    *sends, a, new_a, new_b, sems = rest
    copies = [
        pltpu.make_async_copy(new_a, out_a, sems.at[0]),
        pltpu.make_async_copy(new_b, out_b, sems.at[1]),
    ]
    wide = factor_a.shape[-1]
    for index, part in ((ids[2], half), (ids[2] ^ 1, other)):
        new_a[index] = factor_a[index] - rates[0] * part[:, :wide].astype(F32)
        new_b[index] = factor_b[index] - rates[1] * part[:, wide:].astype(F32)
    for copy in copies:
        copy.start()
    for p in range(2):
        a[p * R : (p + 1) * R] = new_a[p].astype(BF)
    a[TOP:] = jnp.zeros((TILE - TOP, wide), BF)
    tokens = x.shape[0] // 4

    def multiply(*accs):
        steps = wide // TILE

        def push(k):
            for unit in range(2):
                tile = a[:, k * TILE : (k + 1) * TILE]
                pltpu.matmul_push_rhs(tile, k % 2, unit, transpose=True)

        push(0)
        for k in range(steps):
            if k + 1 < steps:
                push(k + 1)
            for r in range(4):
                rows = x[r * tokens : (r + 1) * tokens, k * TILE : (k + 1) * TILE]
                staged = k % 2 if r < 2 else None
                pltpu.matmul_acc_lhs(accs[r], rows, load_staged_rhs=staged)
        for r, send in enumerate(sends):
            u = (0.25 * pltpu.matmul_pop(accs[r])[:, :TOP]).astype(BF)
            for p in range(2):
                send[p * R : (p + 1) * R, :] = new_b[p].astype(BF)
            send[TOP:, :TOP] = u[:TOP]
            send[TOP:tokens, TOP:] = u[TOP:]
            send[tokens:, TOP:] = jnp.zeros((2 * TOP - tokens, TOP), BF)

    pl.run_scoped(multiply, *[pltpu.ACC(r % 2)((tokens, TILE), F32) for r in range(4)])
    for copy in copies:
        copy.wait()


def updated(ids, half, other, factor_a, factor_b, x, dp, *after):
    rates = (2.0 / math.sqrt(dp * D), 2.0 / math.sqrt(dp * R))
    outs = [pltpu.HBM(f.shape, F32) for f in (factor_a, factor_b)]
    outs += [jax.ShapeDtypeStruct((2 * TOP, 2 * TOP), BF)] * 4
    return small_call(
        functools.partial(update_kernel, rates),
        "update_factors",
        ids,
        (half, other, factor_a, factor_b, x),
        outs,
        after,
        [
            pltpu.VMEM((TILE, factor_a.shape[-1]), BF),
            pltpu.VMEM(factor_a.shape, F32),
            pltpu.VMEM(factor_b.shape, F32),
            pltpu.SemaphoreType.DMA((2,)),
        ],
        2,
    )


def attend_kernel(ids, first, lengths, *refs):
    q, cache_k, cache_v, k0, k1, k2, v0, v1, v2, *ub, cosine, sine = refs[:15]
    out = refs[-3]
    rows, slots, _ = cache_k.shape
    tokens = rows * STEPS
    u_held, b_held = refs[-2:]

    @pl.when(pl.program_id(0) == 0)
    def _():
        u_held[:TOP] = sum(x[TOP:, :TOP].astype(F32) for x in ub).astype(BF)
        u_held[TOP:] = sum(x[TOP:tokens, TOP:].astype(F32) for x in ub).astype(BF)

    rel = ids[0] ^ (first[0] + pl.program_id(0))
    for r, x in enumerate(ub):

        @pl.when(rel == r)
        def _():
            b_held[...] = x[:TOP]

    u, b = u_held[...], b_held[...]
    k = k0[...].astype(F32) + k1[...].astype(F32) + k2[...].astype(F32) + dot(u[:, :R], b[:R])
    v = v0[...].astype(F32) + v1[...].astype(F32) + v2[...].astype(F32) + dot(u[:, R:], b[R:])
    v = v.astype(BF)
    keys = []
    for n in range(HEADS_STEP):
        key = k[:, n * HD : (n + 1) * HD]
        scale = lax.rsqrt(jnp.sum(key * key, axis=-1, keepdims=True) * (1.0 / HD) + 1e-06)
        key = scale * (key * cosine[...] + pltpu.roll(key, HD // 2, 1) * sine[...])
        keys.append(key.astype(BF))
    n_q, n_c = GROUP * STEPS, GROUP * slots
    shape = (n_q, n_c + n_q)
    here = lax.broadcasted_iota(jnp.int32, shape, 0)
    col = lax.broadcasted_iota(jnp.int32, shape, 1)
    fresh = col - n_c
    cached = (col < n_c) & (here // STEPS == col // slots)
    new = (col >= n_c) & (here // STEPS == fresh // STEPS) & (fresh % STEPS <= here % STEPS)
    bias_here = jnp.where(cached | new, 0.0, -1e30)
    col = lax.broadcasted_iota(jnp.int32, (1, n_c + n_q), 1)
    ones = jnp.ones((n_c + n_q, HD), BF)
    factor = math.log2(math.e) * HD**-0.5
    heads = QH // KVH
    blocks = rows // GROUP
    query = q[...].reshape(tokens, HEADS_STEP * heads * HD)

    def block(n, g, cache, fresh):
        old = cache[g * GROUP : (g + 1) * GROUP, :, n * HD : (n + 1) * HD].reshape(n_c, HD)
        return jnp.concatenate([old, fresh[g * n_q : (g + 1) * n_q]], axis=0)

    every = [(n, g) for n in range(HEADS_STEP) for g in range(blocks)]
    scores = []
    for n, g in every:
        part = [query[g * n_q : (g + 1) * n_q, h * HD : (h + 1) * HD] for h in range(n * heads, (n + 1) * heads)]
        scores.append(dot_t(jnp.concatenate(part, axis=0), block(n, g, cache_k, keys[n])))
    biases = []
    for g in range(blocks):
        filled = jnp.full(col.shape, lengths[g * GROUP], jnp.int32)
        for i in range(1, GROUP):
            filled = jnp.where(col // slots == i, lengths[g * GROUP + i], filled)
        bias = jnp.where((col >= n_c) | (col % slots < filled), 0.0, -1e30) + bias_here
        biases.append(jnp.concatenate([bias] * heads, axis=0))
    weights = []
    for (n, g), s in zip(every, scores):
        s = s * factor + biases[g]
        top = jnp.max(s, axis=-1, keepdims=True)
        weights.append(jnp.exp2(s - top).astype(BF))
    results = []
    for (n, g), w in zip(every, weights):
        here_v = block(n, g, cache_v, v[:, n * HD : (n + 1) * HD])
        r = dot(w, jnp.concatenate([here_v, ones], axis=1))
        total = r[:, HD:]
        inverse = pl.reciprocal(total, approx=True)
        inverse = inverse * (2.0 - total * inverse)
        results.append((r[:, :HD] * inverse).astype(BF))
    for n in range(HEADS_STEP):
        for h in range(heads):
            part = [r[h * n_q : (h + 1) * n_q] for r in results[n * blocks : (n + 1) * blocks]]
            at = (n * heads + h) * HD
            out[:, :, at : at + HD] = jnp.concatenate(part, axis=0).reshape(rows, STEPS, HD)


def attend_chunk(
    ids, lengths, start, count, queries, cache_keys, cache_values, terms, ub, tables, before
):
    rows, slots, _ = cache_keys.shape
    tokens = rows * STEPS
    heads = QH // KVH
    args = [queries, cache_keys, cache_values, *terms, *ub, *tables]
    assert start % HEADS_STEP == 0 and count % HEADS_STEP == 0
    first = jnp.full((1,), start // HEADS_STEP, jnp.int32)
    size = HEADS_STEP * HD
    part = pl.BlockSpec((tokens, size), lambda i, *_: (0, i))
    low = pl.BlockSpec((tokens, size), lambda i, *_: (1, i))
    cache = pl.BlockSpec((rows, slots, size), lambda i, _, first, *__: (0, 0, first[0] + i))
    wide = pl.BlockSpec((rows, STEPS, heads * size), lambda i, _, first, *__: (0, 0, first[0] + i))
    specs = [wide, cache, cache, part, low, part, part, part, part]
    specs += [whole(x.shape) for x in (*ub, *tables)]
    args.append(before)
    specs.append(pl.BlockSpec(memory_space=pl.ANY))
    return pl.pallas_call(
        attend_kernel,
        out_shape=jax.ShapeDtypeStruct(queries.shape, BF),
        grid_spec=pltpu.PrefetchScalarGridSpec(
            num_scalar_prefetch=3, grid=(count // HEADS_STEP,), in_specs=specs, out_specs=wide,
            scratch_shapes=[pltpu.VMEM((tokens, TOP), BF), pltpu.VMEM((TOP, size), BF)],
        ),
        input_output_aliases={len(args) + 2: 0},
        compiler_params=params(14),
        cost_estimate=cost(count * 4 * 10**9, *args),
        name="attend_chunk",
    )(ids, first, lengths, *args)


def rotary_tables(key_gain, positions):
    half = HD // 2
    place = positions[:, None] + jnp.arange(STEPS, dtype=jnp.int32)[None, :]
    freq = jnp.exp(-math.log(1000000.0) * (jnp.arange(half, dtype=F32) * 2.0 / HD))
    angle = place.reshape(-1).astype(F32)[:, None] * jnp.concatenate([freq, freq])
    turned = jnp.concatenate([-key_gain[half:], key_gain[:half]])
    return jnp.cos(angle) * key_gain, jnp.sin(angle) * turned


def across(x, r):
    return lax.ppermute(x, "tensor", [(i, i ^ r) for i in range(4)])


def square(
    hidden_in,
    kv_weight,
    factor_a,
    factor_b,
    grad_a,
    grad_b,
    key_gain,
    queries,
    cache_keys,
    cache_values,
    cache_lengths,
    positions,
):
    tokens = cache_keys.shape[0] * STEPS
    count_dp = lax.axis_size("dp")
    dp = lax.axis_index("dp")
    ids = jnp.stack([lax.axis_index("tensor"), dp // 2, dp % 2]).astype(jnp.int32)
    tables = rotary_tables(key_gain, positions)

    x, *first, packed = first_terms(ids, hidden_in, kv_weight, grad_a, grad_b, tokens)
    half = chip_grads(ids, grad_a, grad_b, core_flip(packed, count_dp))

    def first_exchange(term, *after):
        ksend, vsend, kkeep, vkeep0, vkeep1 = term
        kcame, vcame = across(ksend, 1), across(vsend, 2)
        mids = mid_sums(kkeep, kcame, vkeep1, vcame, *after)
        return mids, (kkeep, kcame, vkeep0, vcame)

    def second_exchange(mids, parts):
        kkeep, kcame, vkeep0, vcame = parts
        return kkeep, kcame, across(mids[0], 2), vkeep0, vcame, across(mids[1], 1)

    second = later_terms(x, kv_weight, half)
    step, after = 1, second[:1]
    while 2 * step < count_dp:
        came = along_line(half, step, count_dp)
        if step == 1:
            half, *sends = plus_handing(half, came, handed=second[:2])
            second = [*sends, *second[2:]]
        else:
            half = plus(half, came, *after)
        step *= 2
        if step == 2:
            *keeps, attended = keep_terms(x, kv_weight, queries, half)
            first += keeps
            mids, parts = first_exchange(first, half)
            after = (mids[0], tables[0])
    if step == 1:
        *keeps, attended = keep_terms(x, kv_weight, queries, half)
        first += keeps
        mids, parts = first_exchange(first, half)
    first = second_exchange(mids, parts)
    other = core_flip(half, count_dp)
    new_a, new_b, *sends = updated(
        ids, half, other, factor_a, factor_b, x, count_dp
    )
    ub = [sends[0]] + [across(sends[r], r) for r in (1, 2, 3)]
    second = second_exchange(*first_exchange(second, ub[1]))
    for start, count, came in ((0, CHUNKS[0], first), (CHUNKS[0], CHUNKS[1], second)):
        attended = attend_chunk(
            ids,
            cache_lengths,
            start,
            count,
            queries,
            cache_keys,
            cache_values,
            came,
            ub,
            tables,
            attended,
        )
    return attended, new_a, new_b


def solution(mesh):
    fits = mesh.shape["tensor"] == 4 and mesh.shape["dp"] in (2, 4, 8)
    return jax.shard_map(
        square if fits else general,
        mesh=mesh,
        in_specs=(
            P("dp", None, "tensor"),
            P(None, "tensor", None),
            P(None, None, "tensor"),
            P(None, None, "tensor"),
            P("dp", None, None, "tensor"),
            P("dp", None, None, "tensor"),
            P(),
            P(("dp", "tensor"), None, None),
            P(("dp", "tensor"), None, None),
            P(("dp", "tensor"), None, None),
            P(("dp", "tensor")),
            P(("dp", "tensor")),
        ),
        out_specs=(
            P(("dp", "tensor"), None, None),
            P(None, None, "tensor"),
            P(None, None, "tensor"),
        ),
        check_vma=False,
    )
```
